32 devices in a mesh: gx: 4 (over y, x), gy: 4 (over z), mem: 2 (over core).
Axes of the slice: x: 2, y: 2, z: 4, core: 2. Of those that a mesh axis runs over, the one named last changes fastest.
Arguments:
- src_hist: bfloat16 [4, 128, 512, 128], P('mem', 'gx', 'gy'), may hold values from -6 to 6
- rec_p: float32 [128, 512, 128], P('gx', 'gy'), may hold values from -6 to 6
- rec_q: float32 [128, 512, 128], P('gx', 'gy'), may hold values from -6 to 6
- prev_p: float32 [128, 512, 128], P('gx', 'gy'), may hold values from -6 to 6
- prev_q: float32 [128, 512, 128], P('gx', 'gy'), may hold values from -6 to 6
- horiz: float32 [128, 512, 128], P('gx', 'gy'), may hold values from 0.04 to 0.12
- vert: float32 [128, 512, 128], P('gx', 'gy'), may hold values from 0.04 to 0.12
- ratio: float32 [128, 512, 128], P('gx', 'gy'), may hold values from 0.6 to 1
- tilt: float32 [128, 512, 128], P('gx', 'gy'), may hold values from -0.4 to 0.4
- rec_pos: int32 [1024], replicated, may hold values from 0 to 8388607
- rec_data: float32 [4, 1024], replicated, may hold values from -6 to 6
- lag_offs: int32 [2, 2], P('mem'), may hold values from -8 to 8, as said below
Outputs:
- image: float32 [2, 128, 512, 128], P('mem', 'gx', 'gy')
- out_p: float32 [128, 512, 128], P('gx', 'gy')
- out_q: float32 [128, 512, 128], P('gx', 'gy')
The draws below stay inside these ranges and needn't reach their ends.
Inputs may be any that keep to these rules, and one draw needn't show every extreme that they name: `lag_offs`: each offset lies within -8 .. 8; the offset pair (8, -8) occurs in every draw.
All inputs are finite; a program needn't handle non-finite values.
Results may differ from the reference program's by a relative error of at most 0.0003.
Values may be sent and summed in bfloat16 or wider, within the bound.
No kernel may reach another device: no remote copies, remote signals or barrier semaphores. Data moves between devices by JAX's collectives and lax.ppermute only.
A program may use at most 128 MiB of HBM per device.

```python
import jax
import jax.numpy as jnp
from jax import lax

NZ = 128
NT = 4
HMAX = 8
NLAG = 2
NX = 128
NY = 512
NREC = 1024


def draw_lag_offs(key, part):
    values = jax.random.randint(key, (NLAG, 2), -HMAX, HMAX + 1, dtype=jnp.int32)
    values = values.at[0, 0].set(HMAX)
    values = values.at[0, 1].set(-HMAX)
    return values.astype(jnp.int32)


def set_ends(result, key, low, top_value):
    dims = result.shape
    place = [jax.random.randint(jax.random.fold_in(key, axis), (), 0, dims[axis]) for axis in range(len(dims))]
    result = result.at[tuple(place)].set(low)
    longest = dims.index(max(dims))
    place[longest] = (place[longest] + 1) % dims[longest]
    return result.at[tuple(place)].set(top_value)


def shard_levels(stream_key, shape, cuts, least, top_value):
    loudness = 1.0
    for axis_at, shards_of in cuts:
        heights = jax.random.uniform(jax.random.fold_in(jax.random.fold_in(stream_key, 6), axis_at), (shards_of,), jnp.float32, least / len(cuts), top_value / len(cuts))
        loudness = loudness * jnp.repeat(jnp.exp(heights), shape[axis_at] // shards_of).reshape((-1,) + (1,) * (len(shape) - 1 - axis_at))
    return loudness


def bell_draw(own_key, shape, width, limit, pieces=(), kind=jnp.bfloat16):
    factor_of = shard_levels(own_key, shape, pieces, -0.22, 0.18) if pieces else 1.0
    values = jax.random.normal(own_key, shape, jnp.float32) * width * factor_of
    return jnp.minimum(jnp.maximum(values, -limit), limit).astype(kind)


def setup_inputs(seed: int = 0) -> dict:
    arg_keys = jax.random.split(jax.random.key(seed), 13)
    return {
        "src_hist": bell_draw(arg_keys[0], (NT, NX, NY, NZ), 1.0, 6.0, ((0, 2), (1, 4), (2, 4))),
        "rec_p": bell_draw(arg_keys[1], (NX, NY, NZ), 1.0, 6.0, ((0, 4), (1, 4)), jnp.float32),
        "rec_q": bell_draw(arg_keys[2], (NX, NY, NZ), 1.0, 6.0, ((0, 4), (1, 4)), jnp.float32),
        "prev_p": bell_draw(arg_keys[3], (NX, NY, NZ), 1.0, 6.0, ((0, 4), (1, 4)), jnp.float32),
        "prev_q": bell_draw(arg_keys[4], (NX, NY, NZ), 1.0, 6.0, ((0, 4), (1, 4)), jnp.float32),
        "horiz": jnp.clip(0.04 + 0.08 * jax.random.uniform(arg_keys[5], (NX, NY, NZ), jnp.float32) ** shard_levels(arg_keys[5], (NX, NY, NZ), ((0, 4), (1, 4)), -0.2, 0.2), 0.04, 0.12),
        "vert": jnp.clip(0.04 + 0.08 * jax.random.uniform(arg_keys[6], (NX, NY, NZ), jnp.float32) ** shard_levels(arg_keys[6], (NX, NY, NZ), ((0, 4), (1, 4)), -0.2, 0.2), 0.04, 0.12),
        "ratio": jnp.clip(0.6 + 0.39999998 * jax.random.uniform(arg_keys[7], (NX, NY, NZ), jnp.float32) ** shard_levels(arg_keys[7], (NX, NY, NZ), ((0, 4), (1, 4)), -0.2, 0.2), 0.6, 1.0),
        "tilt": jnp.clip(jax.random.uniform(arg_keys[8], (NX, NY, NZ), jnp.float32, -0.4, 0.4) * shard_levels(arg_keys[8], (NX, NY, NZ), ((0, 4), (1, 4)), -0.4, 0.0), -0.4, 0.4),
        "rec_pos": set_ends(jax.random.randint(arg_keys[9], (NREC,), 0, NX * NY * NZ), jax.random.fold_in(arg_keys[9], 1), 0, (NX * NY * NZ) - 1).astype(jnp.int32),
        "rec_data": bell_draw(arg_keys[10], (NT, NREC), 1.0, 6.0, (), jnp.float32),
        "lag_offs": draw_lag_offs(jax.random.fold_in(arg_keys[12], 71), 0),
    }


def advance(p, q, old_p, old_q, wide_p, wide_q, horiz, vert, ratio, tilt):
    lateral = wide_p[2:, 1:-1] + wide_p[:-2, 1:-1] + wide_p[1:-1, 2:] + wide_p[1:-1, :-2] - 4.0 * p
    deep = jnp.pad(wide_q[:, 1:-1], ((0, 0), (0, 0), (1, 1)))
    center = deep[1:-1]
    second = center[:, :, 2:] + center[:, :, :-2] - 2.0 * q
    mixed = 0.25 * (deep[2:, :, 2:] - deep[2:, :, :-2] - deep[:-2, :, 2:] + deep[:-2, :, :-2])
    horizontal = horiz * lateral
    upright = vert * (second + tilt * mixed)
    new_p = 2.0 * p - old_p + horizontal + upright
    new_q = 2.0 * q - old_q + ratio * horizontal + upright
    return new_p, new_q


def reference(src_hist, rec_p, rec_q, prev_p, prev_q, horiz, vert, ratio, tilt, rec_pos, rec_data, lag_offs):
    shape = rec_p.shape
    fields = jnp.stack([rec_p, rec_q])
    older = jnp.stack([prev_p, prev_q])
    image = jnp.zeros((lag_offs.shape[0],) + shape, jnp.float32)

    def advance_step(carry, k):
        fields, older, image = carry
        t = NT - 1 - k
        snap = lax.dynamic_index_in_dim(src_hist, t, 0, keepdims=False)
        wide_s = jnp.pad(snap, ((HMAX, HMAX), (HMAX, HMAX), (0, 0)))
        current = fields[0]

        def one_lag(offset):
            piece = lax.dynamic_slice(wide_s, (HMAX - offset[0], HMAX - offset[1], jnp.int32(0)), shape)
            return piece.astype(jnp.float32) * current

        image = image + lax.map(one_lag, lag_offs)
        wide = jnp.pad(fields, ((0, 0), (1, 1), (1, 1), (0, 0)))
        new_p, new_q = advance(fields[0], fields[1], older[0], older[1], wide[0], wide[1], horiz, vert, ratio, tilt)
        amount = lax.dynamic_index_in_dim(rec_data, t, 0, keepdims=False)
        new_p = new_p.reshape(-1).at[rec_pos].add(amount).reshape(shape)
        new_q = new_q.reshape(-1).at[rec_pos].add(amount).reshape(shape)
        return (jnp.stack([new_p, new_q]), fields, image), None

    (fields, older, image), unused = lax.scan(advance_step, (fields, older, image), jnp.arange(NT, dtype=jnp.int32))
    return image, fields[0], fields[1]
```

```python
import functools

import jax
import jax.numpy as jnp
from jax import lax
from jax.experimental import pallas as pl
from jax.experimental.pallas import tpu as pltpu
from jax.sharding import PartitionSpec as P

NT = 4
HMAX = 8
DEEP = NT
ROW0 = 16
F32 = jnp.float32
BF16 = jnp.bfloat16
ANY = pl.BlockSpec(memory_space=pl.ANY)
SMEM = pl.BlockSpec(memory_space=pltpu.SMEM)
VMEM = pl.BlockSpec(memory_space=pltpu.VMEM)
DEPTHS = (DEEP, DEEP) + (DEEP - 1,) * 6
STARTS = tuple(sum(DEPTHS[:i]) for i in range(8))
LAYERS = sum(DEPTHS)


def params(mib):
    return pltpu.CompilerParams(vmem_limit_bytes=mib * 2**20)


def copy_all(pairs, sems):
    copies = [pltpu.make_async_copy(a, b, sems.at[i]) for i, (a, b) in enumerate(pairs)]
    for c in copies:
        c.start()
    return copies


def wait_all(copies):
    for c in copies:
        c.wait()


def pack_x_kernel(scal, *refs):
    fields, out, stage, sems = refs[:8], refs[8], refs[9], refs[10]
    core = scal[0]
    width = fields[0].shape[0]
    pairs = []
    for f, s, d in zip(fields, STARTS, DEPTHS):
        begin = jnp.where(core == 0, width - d, 0)
        pairs.append((f.at[pl.ds(begin, d)], stage.at[pl.ds(s, d)]))
    copies = copy_all(pairs, sems)
    for c, s, d in zip(copies, STARTS, DEPTHS):
        c.wait()
        out[s : s + d] = stage[s : s + d].astype(BF16)


def pack_x(scal, fields):
    shape = (LAYERS,) + fields[0].shape[1:]
    return pl.pallas_call(
        pack_x_kernel,
        out_shape=jax.ShapeDtypeStruct(shape, BF16),
        in_specs=[SMEM] + [ANY] * 8,
        out_specs=VMEM,
        scratch_shapes=[pltpu.VMEM(shape, F32), pltpu.SemaphoreType.DMA((8,))],
        compiler_params=params(16),
        name="pack_x",
    )(scal, *fields)


def pack_y_kernel(scal, *refs):
    fields, own, other, out, stage, snaps, mixed, sems = refs[:8], *refs[8:]
    core = scal[0]
    rows = fields[0].shape[1]
    start = pl.multiple_of(jnp.where(core == 0, rows - 8, 0), 8)
    wide = pl.multiple_of(jnp.where(core == 0, rows - 16, 0), 16)
    pairs = [(f.at[:, pl.ds(start, 8)], stage.at[i]) for i, f in enumerate(fields)]
    pairs.append((own.at[:, :, pl.ds(wide, 16)], snaps.at[core]))
    pairs.append((other.at[:, :, pl.ds(wide, 16)], snaps.at[1 - core]))
    copies = copy_all(pairs, sems)
    skip = jnp.where(core == 0, 4, 0)
    for slab in range(2):
        for i in range(4):
            f = 4 * slab + i
            copies[f].wait()
            mixed[:, 4 * i : 4 * i + 4, :] = stage[f, :, pl.ds(skip, 4), :]
        out[slab] = mixed[...].astype(BF16)
    wait_all(copies[8:])
    for pair in range(2):
        for i in range(2):
            both = snaps[pair, i].astype(F32)
            mixed[:, 8 * i : 8 * i + 8, :] = jnp.where(core == 0, both[:, 8:], both[:, :8])
        out[2 + pair] = mixed[...].astype(BF16)


def pack_y(scal, fields, own, other):
    width, _, depth = fields[0].shape
    return pl.pallas_call(
        pack_y_kernel,
        out_shape=jax.ShapeDtypeStruct((4, width, 16, depth), BF16),
        in_specs=[SMEM] + [ANY] * 10,
        out_specs=VMEM,
        scratch_shapes=[
            pltpu.VMEM((8, width, 8, depth), F32),
            pltpu.VMEM((2, 2, width, 16, depth), BF16),
            pltpu.VMEM((width, 16, depth), F32),
            pltpu.SemaphoreType.DMA((10,)),
        ],
        compiler_params=params(16),
        name="pack_y",
    )(scal, *fields, own, other)


def pack_corner_kernel(scal, y_own, y_other, own, other, xc, xs, sems):
    core = scal[0]
    width = own.shape[1]
    near = jnp.where(core == 0, width - DEEP, 0)
    far = jnp.where(core == 0, width - HMAX, 0)
    pairs = []
    for ref, side in ((y_own, core), (y_other, 1 - core)):
        pairs.append((ref.at[pl.ds(0, 2), pl.ds(near, DEEP)], xc.at[side]))
        for pair in range(2):
            for layer in range(HMAX):
                pairs.append(
                    (
                        ref.at[2 + pair, far + layer],
                        xs.at[NT * HMAX + 2 * side + pair, pl.ds(16 * layer, 16)],
                    )
                )
    for ref, half in ((own, core), (other, 1 - core)):
        for i in range(2):
            pairs.append(
                (ref.at[i, pl.ds(far, HMAX)], xs.at[pl.ds((2 * half + i) * HMAX, HMAX)])
            )
    wait_all(copy_all(pairs, sems))


def pack_corner(scal, y_own, y_other, own, other):
    _, width, rows, depth = own.shape
    return pl.pallas_call(
        pack_corner_kernel,
        out_shape=(
            jax.ShapeDtypeStruct((2, 2, DEEP, 16, depth), BF16),
            jax.ShapeDtypeStruct((NT * HMAX + 4, rows, depth), BF16),
        ),
        in_specs=[SMEM] + [ANY] * 4,
        out_specs=(ANY, ANY),
        scratch_shapes=[pltpu.SemaphoreType.DMA((2 + 4 * HMAX + 4,))],
        compiler_params=params(16),
        name="pack_corner",
    )(scal, y_own, y_other, own, other)


def pick_kernel(target, count, chosen, places):
    def one(r, n):
        place = target[r]
        chosen[n] = r
        places[n] = place
        return n + jnp.where(place >= 0, 1, 0)

    total = target.shape[0]
    count[0] = lax.fori_loop(0, total, one, jnp.int32(0), unroll=8)


def pick(target):
    n = target.shape[0]
    return pl.pallas_call(
        pick_kernel,
        out_shape=(
            jax.ShapeDtypeStruct((1,), jnp.int32),
            jax.ShapeDtypeStruct((n + 1,), jnp.int32),
            jax.ShapeDtypeStruct((n + 1,), jnp.int32),
        ),
        in_specs=[SMEM],
        out_specs=(SMEM, SMEM, SMEM),
        name="pick_receivers",
    )(target)


def wave_kernel(scal, count, chosen, places, data, *refs):
    fields = refs[:8]
    xw_own, xw_other, y_own, y_other, xc_own, xc_other = refs[8:14]
    p_outs, q_out = refs[14:18], refs[18]
    bufs = refs[19:27]
    s_xw, s_y, s_xc, stage, sem_in, sem_halo, sem_out = refs[27:]
    core = scal[0]
    width, rows, depth = fields[0].shape
    mid = (pl.ds(DEEP, width), pl.ds(ROW0, rows))
    mains = copy_all([(f, b.at[mid]) for f, b in zip(fields, bufs)], sem_in)
    halos = copy_all(
        [
            (xw_own, s_xw.at[core]),
            (xw_other, s_xw.at[1 - core]),
            (y_own.at[pl.ds(0, 2)], s_y.at[core]),
            (y_other.at[pl.ds(0, 2)], s_y.at[1 - core]),
            (xc_own, s_xc.at[core]),
            (xc_other, s_xc.at[1 - core]),
        ],
        sem_halo,
    )
    wait_all(halos)
    for side in range(2):
        for f in range(8):
            d = DEPTHS[f]
            to = DEEP - d if side == 0 else DEEP + width
            part = s_xw[side, STARTS[f] : STARTS[f] + d]
            bufs[f][to : to + d, ROW0 : ROW0 + rows, :] = part.astype(F32)
    for yside in range(2):
        to = ROW0 - DEEP if yside == 0 else ROW0 + rows
        for slab in range(2):
            stage[DEEP : DEEP + width] = s_y[yside, slab].astype(F32)
            for xside in range(2):
                at = 0 if xside == 0 else DEEP + width
                stage[at : at + DEEP] = s_xc[xside, yside, slab].astype(F32)
            for i in range(4):
                bufs[4 * slab + i][:, to : to + DEEP, :] = stage[:, 4 * i : 4 * i + 4, :]
    wait_all(mains)

    horiz, vert, ratio, tilt = bufs[4:]
    lane = lax.broadcasted_iota(jnp.int32, (16, depth), 1)
    first, last = lane == 0, lane == depth - 1
    thin = lax.broadcasted_iota(jnp.int32, (1, depth), 1)

    def up_z(v):
        return jnp.where(last, 0.0, pltpu.roll(v, depth - 1, 1))

    def down_z(v):
        return jnp.where(first, 0.0, pltpu.roll(v, 1, 1))

    def step(k, p, q, old_p, old_q):
        low, high = 1 + k, width + 2 * DEEP - 1 - k
        if k < NT - 1:
            begins = range(ROW0 - 8, ROW0 + rows + 8, 16)
        else:
            begins = range(ROW0, ROW0 + rows, 16)
        for r in begins:
            at = pl.ds(r, 16)

            def cell(x, carry, r=r, at=at):
                p_m, p_c, q_m, q_c = carry
                p_n, q_n = p[x + 1, at, :], q[x + 1, at, :]
                lateral = (p_m + p_n) + (p[x, pl.ds(r - 1, 16), :] + p[x, pl.ds(r + 1, 16), :]) - 4.0 * p_c
                slope = q_n - q_m
                second = (up_z(q_c) + down_z(q_c)) - 2.0 * q_c
                mixed = up_z(slope) - down_z(slope)
                horizontal = horiz[x, at, :] * lateral
                upright = vert[x, at, :] * (second + (0.25 * tilt[x, at, :]) * mixed)
                old_p[x, at, :] = (2.0 * p_c - old_p[x, at, :]) + (horizontal + upright)
                old_q[x, at, :] = (2.0 * q_c - old_q[x, at, :]) + (ratio[x, at, :] * horizontal + upright)
                return p_c, p_n, q_c, q_n

            init = (p[low - 1, at, :], p[low, at, :], q[low - 1, at, :], q[low, at, :])
            lax.fori_loop(low, high, cell, init, unroll=2)

        def inject(j, _):
            place = places[j]
            amount = data[NT - 1 - k, chosen[j]]
            x, y, z = place >> 16, (place >> 8) & 255, place & 255
            add = jnp.where(thin == z, amount, 0.0)
            old_p[x, pl.ds(y, 1), :] = old_p[x, pl.ds(y, 1), :] + add
            old_q[x, pl.ds(y, 1), :] = old_q[x, pl.ds(y, 1), :] + add
            return 0

        lax.fori_loop(0, count[0], inject, 0)

    p_now, q_now, p_old, q_old = bufs[:4]
    outs = []
    for k in range(NT):
        if k >= 2:
            outs[k - 2].wait()
        step(k, p_now, q_now, p_old, q_old)
        p_now, p_old, q_now, q_old = p_old, p_now, q_old, q_now
        outs.append(pltpu.make_async_copy(p_now.at[mid], p_outs[k], sem_out.at[k]))
        outs[-1].start()
    tail = pltpu.make_async_copy(q_now.at[mid], q_out, sem_out.at[NT])
    tail.start()
    wait_all(outs[NT - 2 :] + [tail])


def wave(scal, receivers, data, fields, halos):
    shape = fields[0].shape
    width, rows, depth = shape
    big = (width + 2 * DEEP, rows + 2 * ROW0, depth)
    return pl.pallas_call(
        wave_kernel,
        out_shape=(jax.ShapeDtypeStruct(shape, F32),) * 5,
        in_specs=[SMEM] * 5 + [ANY] * 14,
        out_specs=(ANY,) * 5,
        scratch_shapes=[pltpu.VMEM(big, F32)] * 8
        + [
            pltpu.VMEM((2, LAYERS, rows, depth), BF16),
            pltpu.VMEM((2, 2, width, 16, depth), BF16),
            pltpu.VMEM((2, 2, 2, DEEP, 16, depth), BF16),
            pltpu.VMEM((width + 2 * DEEP, 16, depth), F32),
            pltpu.SemaphoreType.DMA((8,)),
            pltpu.SemaphoreType.DMA((6,)),
            pltpu.SemaphoreType.DMA((5,)),
        ],
        compiler_params=params(48),
        name="wave",
    )(scal, *receivers, data, *fields, *halos)


def image_kernel(scal, own, other, y_own, y_other, xs_own, xs_other, *refs):
    ps, out = refs[:NT], refs[NT]
    snaps, strips, wide, sems = refs[NT + 1 :]
    core, off_x, off_y = scal[0], scal[1], scal[2]
    width, rows, depth = own.shape[1:]
    chunk = out.shape[0]
    step = pl.program_id(0)

    @pl.when(step == 0)
    def _():
        mains = [
            (own, snaps.at[pl.ds(2 * core, 2), pl.ds(HMAX, width)]),
            (other, snaps.at[pl.ds(2 - 2 * core, 2), pl.ds(HMAX, width)]),
        ]
        copies = copy_all(mains, sems)
        x_side = jnp.where(off_x > 0, 0, 1)
        y_side = jnp.where(off_y > 0, 0, 1)
        to = jnp.where(off_x > 0, 0, HMAX + width)

        def halo(xs):
            pairs = [
                (xs.at[pl.ds(t * HMAX, HMAX)], snaps.at[t, pl.ds(to, HMAX)]) for t in range(NT)
            ]
            for pair in range(2):
                for layer in range(HMAX):
                    pairs.append(
                        (
                            xs.at[NT * HMAX + 2 * y_side + pair, pl.ds(16 * layer, 16)],
                            strips.at[pair, to + layer],
                        )
                    )
            wait_all(copy_all(pairs, sems.at[pl.ds(3, 4 + 2 * HMAX)]))

        def edge(ref):
            pairs = [(ref.at[pl.ds(2, 2)], strips.at[:, pl.ds(HMAX, width)])]
            wait_all(copy_all(pairs, sems.at[pl.ds(2, 1)]))

        pl.when(x_side == core)(lambda: halo(xs_own))
        pl.when(x_side != core)(lambda: halo(xs_other))
        pl.when(y_side == core)(lambda: edge(y_own))
        pl.when(y_side != core)(lambda: edge(y_other))
        wait_all(copies)

    low = off_y > 0
    for i in range(chunk):
        x = step * chunk + i + HMAX - off_x
        total = None
        for pair in range(2):
            strip = strips[pair, x].astype(F32)
            for j in range(2):
                t = 2 * pair + j
                slot = t + NT * (i % 2)
                rim = strip[8 * j : 8 * j + 8]
                wide[slot, pl.ds(HMAX, rows), :] = snaps[t, x].astype(F32)
                wide[slot, pl.ds(0, HMAX), :] = rim
                wide[slot, pl.ds(HMAX + rows, HMAX), :] = rim
                term = wide[slot, pl.ds(HMAX - off_y, rows), :] * ps[NT - 1 - t][i]
                total = term if total is None else total + term
        out[i] = total


def image(scal, own, other, y_own, y_other, xs_own, xs_other, ps):
    shape = ps[0].shape
    width, rows, depth = shape
    chunk = 4
    block = pl.BlockSpec((chunk, rows, depth), lambda i: (i, 0, 0))
    return pl.pallas_call(
        image_kernel,
        grid=(width // chunk,),
        out_shape=jax.ShapeDtypeStruct(shape, F32),
        in_specs=[SMEM] + [ANY] * 6 + [block] * NT,
        out_specs=block,
        scratch_shapes=[
            pltpu.VMEM((NT, width + 2 * HMAX, rows, depth), BF16),
            pltpu.VMEM((2, width + 2 * HMAX, 16, depth), BF16),
            pltpu.VMEM((2 * NT, rows + 2 * HMAX, depth), F32),
            pltpu.SemaphoreType.DMA((3 + 4 + 2 * HMAX,)),
        ],
        compiler_params=params(32),
        name="image",
    )(scal, own, other, y_own, y_other, xs_own, xs_other, *ps)


def body(
    src_hist, rec_p, rec_q, prev_p, prev_q, horiz, vert, ratio, tilt, rec_pos, rec_data, lag_offs
):
    width, rows, depth = rec_p.shape
    core = lax.axis_index("mem")
    scal = jnp.concatenate([core[None].astype(jnp.int32), lag_offs[0]])
    fields = (rec_p, rec_q, prev_p, prev_q, horiz, vert, ratio, tilt)

    def swap(v):
        return lax.ppermute(v, "mem", [(0, 1), (1, 0)])

    def outward(v, axis):
        count = lax.axis_size(axis)
        up = [(2 * i, 2 * i + 2) for i in range(count - 1)]
        down = [(2 * i + 3, 2 * i + 1) for i in range(count - 1)]
        return lax.ppermute(v, (axis, "mem"), up + down)

    plane = rows * lax.axis_size("gy") * depth
    x = rec_pos // plane - lax.axis_index("gx") * width + DEEP
    rest = rec_pos % plane
    y = rest // depth - lax.axis_index("gy") * rows + ROW0
    z = rest % depth
    inside = (x >= 0) & (x < width + 2 * DEEP)
    inside &= (y >= ROW0 - DEEP) & (y < ROW0 + rows + DEEP)
    receivers = pick(jnp.where(inside, (x << 16) + (y << 8) + z, -1))

    other = swap(src_hist)
    xw = outward(pack_x(scal, fields), "gx")
    ys = outward(pack_y(scal, fields, src_hist, other), "gy")
    ys_other = swap(ys)
    xc, xs = pack_corner(scal, ys, ys_other, src_hist, other)
    xc = outward(xc, "gx")
    xs = outward(xs, "gx")
    halos = (xw, swap(xw), ys, ys_other, xc, swap(xc))
    p1, p2, p3, p4, q4 = wave(scal, receivers, rec_data, fields, halos)
    picture = image(scal, src_hist, other, ys, ys_other, xs, swap(xs), (rec_p, p1, p2, p3))
    return picture[None], p4, q4


def solution(mesh):
    block = P("gx", "gy", None)
    return jax.shard_map(
        body,
        mesh=mesh,
        in_specs=(P("mem", "gx", "gy", None),) + (block,) * 8 + (P(), P(), P("mem", None)),
        out_specs=(P("mem", "gx", "gy", None), block, block),
        check_vma=False,
    )
```

```python
import functools

import jax
import jax.numpy as jnp
from jax import lax
from jax.experimental import pallas as pl
from jax.experimental.pallas import tpu as pltpu
from jax.sharding import PartitionSpec as P

NT = 4
HMAX = 8
DEEP = NT
ROW0 = 16
F32 = jnp.float32
BF16 = jnp.bfloat16
HBM = pl.BlockSpec(memory_space=pltpu.HBM)
SMEM = pl.BlockSpec(memory_space=pltpu.SMEM)
VMEM = pl.BlockSpec(memory_space=pltpu.VMEM)
DEPTHS = (DEEP, DEEP) + (DEEP - 1,) * 6
STARTS = tuple(sum(DEPTHS[:i]) for i in range(8))
LAYERS = sum(DEPTHS)


def pin(arrays, space=pltpu.HBM):
    return [pltpu.with_memory_space_constraint(a, space) for a in arrays]


def params(mib=63):
    return pltpu.CompilerParams(vmem_limit_bytes=mib * 2**20)


def copy_all(pairs, sems):
    copies = [pltpu.make_async_copy(a, b, sems.at[i]) for i, (a, b) in enumerate(pairs)]
    for c in copies:
        c.start()
    return copies


def wait_all(copies):
    for c in copies:
        c.wait()


def pack_x_kernel(*refs):
    fields, out, stage, small, sems, out_sems = refs[:8], *refs[8:]
    core = lax.axis_index("mem")
    width = fields[0].shape[0]
    pairs = []
    for f, s, d in zip(fields, STARTS, DEPTHS):
        begin = jnp.where(core == 0, width - d, 0)
        pairs.append((f.at[pl.ds(begin, d)], stage.at[pl.ds(s, d)]))
    copies = copy_all(pairs, sems)
    sent = []
    for i, (s, d) in enumerate(zip(STARTS, DEPTHS)):
        copies[i].wait()
        small[s : s + d] = stage[s : s + d].astype(BF16)
        part = pl.ds(s, d)
        sent.append(pltpu.make_async_copy(small.at[part], out.at[part], out_sems.at[i]))
        sent[-1].start()
    wait_all(sent)


def pack_x(fields):
    shape = (LAYERS,) + fields[0].shape[1:]
    return pl.pallas_call(
        pack_x_kernel,
        out_shape=jax.ShapeDtypeStruct(shape, BF16),
        in_specs=[HBM] * 8,
        out_specs=HBM,
        scratch_shapes=[
            pltpu.VMEM(shape, F32),
            pltpu.VMEM(shape, BF16),
            pltpu.SemaphoreType.DMA((8,)),
            pltpu.SemaphoreType.DMA((8,)),
        ],
        compiler_params=params(),
        name="pack_x",
    )(*pin(fields))


def pack_rest_kernel(*refs):
    fields, own, other, _ = refs[:8], *refs[8:11]
    ys, same, cross, xs = refs[11:15]
    stage, snaps, edges, stage_c, snaps_c, mixed, s_ys, s_same, s_cross, sems, out_sems = refs[15:]
    core = lax.axis_index("mem")
    width, rows, _ = fields[0].shape
    near, far = width - DEEP, width - HMAX
    to_low = core == 1
    x_near, x_far = jnp.where(to_low, 0, near), jnp.where(to_low, 0, far)

    def y_at(low, size):
        return pl.multiple_of(jnp.where(low, 0, rows - size), size)

    pairs = []
    for i, f in enumerate(fields):
        pairs.append((f.at[:, pl.ds(y_at(to_low, 8), 8)], stage.at[i]))
        pairs.append((f.at[pl.ds(x_near, DEEP), pl.ds(y_at(~to_low, 8), 8)], stage_c.at[i]))
    for ref, half in ((own, core), (other, 1 - core)):
        pairs.append((ref.at[:, :, pl.ds(y_at(to_low, 16), 16)], snaps.at[half]))
        rim = ref.at[:, pl.ds(x_far, HMAX), pl.ds(y_at(~to_low, 16), 16)]
        pairs.append((rim, snaps_c.at[half]))
        pairs.append((ref.at[:, pl.ds(x_far, HMAX)], edges.at[pl.ds(2 * half, 2)]))
    copies = copy_all(pairs, sems)
    sent = []

    def send(a, b):
        sent.append(pltpu.make_async_copy(a, b, out_sems.at[len(sent)]))
        sent[-1].start()

    wait_all(copies[:16])
    skip, skip_c = jnp.where(to_low, 0, 4), jnp.where(to_low, 4, 0)
    for slab in range(2):
        for i in range(4):
            at = pl.ds(4 * i, 4)
            mixed[:width, at, :] = stage[4 * slab + i, :, pl.ds(skip, 4), :]
            mixed[width : width + DEEP, at, :] = stage_c[4 * slab + i, :, pl.ds(skip_c, 4), :]
        s_ys[slab] = mixed[:width].astype(BF16)
        s_cross[slab * DEEP : (slab + 1) * DEEP] = mixed[width : width + DEEP].astype(BF16)
    wait_all(copies[16:])
    for pair in range(2):
        for i in range(2):
            at = slice(8 * i, 8 * i + 8)
            both = snaps[pair, i].astype(F32)
            mixed[:width, at, :] = jnp.where(to_low, both[:, :8], both[:, 8:])
            both = snaps_c[pair, i].astype(F32)
            mixed[width : width + HMAX, at, :] = jnp.where(to_low, both[:, 8:], both[:, :8])
        s_ys[2 + pair] = mixed[:width].astype(BF16)
        begin = 2 * DEEP + pair * HMAX
        s_cross[begin : begin + HMAX] = mixed[width : width + HMAX].astype(BF16)
    send(s_ys, ys)
    send(s_cross, cross)
    send(edges, xs)
    for slab in range(2):
        begin = slab * DEEP
        s_same[begin : begin + DEEP] = s_ys[slab, pl.ds(x_near, DEEP)]
        begin = 2 * DEEP + slab * HMAX
        s_same[begin : begin + HMAX] = s_ys[2 + slab, pl.ds(x_far, HMAX)]
    send(s_same, same)
    wait_all(sent)


def pack_rest(fields, own, other, earlier):
    width, rows, depth = fields[0].shape
    corner = (2 * DEEP + 2 * HMAX, 16, depth)
    return pl.pallas_call(
        pack_rest_kernel,
        out_shape=(
            jax.ShapeDtypeStruct((4, width, 16, depth), BF16),
            jax.ShapeDtypeStruct(corner, BF16),
            jax.ShapeDtypeStruct(corner, BF16),
            jax.ShapeDtypeStruct((NT, HMAX, rows, depth), BF16),
        ),
        in_specs=[HBM] * 11,
        out_specs=(HBM,) * 4,
        scratch_shapes=[
            pltpu.VMEM((8, width, 8, depth), F32),
            pltpu.VMEM((2, 2, width, 16, depth), BF16),
            pltpu.VMEM((NT, HMAX, rows, depth), BF16),
            pltpu.VMEM((8, DEEP, 8, depth), F32),
            pltpu.VMEM((2, 2, HMAX, 16, depth), BF16),
            pltpu.VMEM((width + HMAX, 16, depth), F32),
            pltpu.VMEM((4, width, 16, depth), BF16),
            pltpu.VMEM(corner, BF16),
            pltpu.VMEM(corner, BF16),
            pltpu.SemaphoreType.DMA((22,)),
            pltpu.SemaphoreType.DMA((4,)),
        ],
        compiler_params=params(),
        name="pack_rest",
    )(*pin((*fields, own, other, earlier)))


def load_kernel(target, *refs):
    fields, bufs, (count, chosen, places, sems) = refs[:8], refs[8:16], refs[16:]
    width, rows, _ = fields[0].shape
    mid = (pl.ds(DEEP, width), pl.ds(ROW0, rows))
    copies = copy_all([(f, b.at[mid]) for f, b in zip(fields, bufs)], sems)

    def one(r, n):
        place = target[r]
        chosen[n] = r
        places[n] = place
        return n + jnp.where(place >= 0, 1, 0)

    count[0] = lax.fori_loop(0, target.shape[0], one, jnp.int32(0), unroll=8)
    wait_all(copies)


def load(target, fields, earlier):
    width, rows, depth = fields[0].shape
    n = target.shape[0]
    ints = jax.ShapeDtypeStruct((n + 1,), jnp.int32)
    out = pl.pallas_call(
        lambda target, *refs: load_kernel(target, *refs[:8], *refs[9:]),
        out_shape=(pltpu.VMEM((width + 2 * DEEP, rows + 2 * ROW0, depth), F32),) * 8
        + (jax.ShapeDtypeStruct((1,), jnp.int32), ints, ints),
        in_specs=[SMEM] + [HBM] * 9,
        out_specs=(VMEM,) * 8 + (SMEM,) * 3,
        scratch_shapes=[pltpu.SemaphoreType.DMA((8,))],
        compiler_params=params(8),
        name="load",
    )(target, *pin((*fields, earlier)))
    return out[:8], out[8:]


def wave_kernel(count, chosen, places, data, offs, *refs):
    halo_refs, own, other = refs[:8], refs[8], refs[9]
    p_out, q_out, image, p_rims = refs[18:22]
    bufs = refs[22:30]
    s_xw, s_y, s_xc, stage, snaps, wide, total, sem_halo, sem_in, sem_out = refs[30:]
    core, off_x, off_y = lax.axis_index("mem"), offs[0, 0], offs[0, 1]
    width, rows, depth = p_out.shape
    mid = (pl.ds(DEEP, width), pl.ds(ROW0, rows))
    pairs = []
    for i, side in ((0, core), (1, 1 - core)):
        xw, ys, same, cross = halo_refs[i::2]
        wave_part = pl.ds(0, 2 * DEEP)
        pairs.append((xw, s_xw.at[side]))
        pairs.append((ys, s_y.at[side]))
        pairs.append((same.at[wave_part], s_xc.at[side, side]))
        pairs.append((cross.at[wave_part], s_xc.at[side, 1 - side]))
    halos = copy_all(pairs, sem_halo)
    mains = copy_all(
        [(own, snaps.at[pl.ds(2 * core, 2)]), (other, snaps.at[pl.ds(2 - 2 * core, 2)])], sem_in
    )
    wait_all(halos)
    for side in range(2):
        for f in range(8):
            d = DEPTHS[f]
            to = DEEP - d if side == 0 else DEEP + width
            part = s_xw[side, STARTS[f] : STARTS[f] + d]
            bufs[f][to : to + d, ROW0 : ROW0 + rows, :] = part.astype(F32)
    for yside in range(2):
        to = ROW0 - DEEP if yside == 0 else ROW0 + rows
        for slab in range(2):
            stage[DEEP : DEEP + width] = s_y[yside, slab].astype(F32)
            for xside in range(2):
                at = 0 if xside == 0 else DEEP + width
                part = s_xc[xside, yside, slab * DEEP : slab * DEEP + DEEP]
                stage[at : at + DEEP] = part.astype(F32)
            for i in range(4):
                bufs[4 * slab + i][:, to : to + DEEP, :] = stage[:, 4 * i : 4 * i + 4, :]
    wait_all(mains)

    horiz, vert, ratio, tilt = bufs[4:]
    thin = lax.broadcasted_iota(jnp.int32, (1, depth), 1)

    def slopes(v):
        lane = lax.broadcasted_iota(jnp.int32, v.shape, 1)
        up = jnp.where(lane == depth - 1, 0.0, pltpu.roll(v, depth - 1, 1))
        down = jnp.where(lane == 0, 0.0, pltpu.roll(v, 1, 1))
        return up + down, up - down

    def step(k, p, q, old_p, old_q):
        low, high = 1 + k, width + 2 * DEEP - 1 - k
        begin, end = (ROW0 - 8, ROW0 + rows + 8) if k < NT - 1 else (ROW0, ROW0 + rows)
        size = 24 if (end - begin) % 24 == 0 else 32 if (end - begin) % 32 == 0 else 8

        def strip(i, _):
            r = pl.multiple_of(begin + i * size, 8)
            at = pl.ds(r, size)
            p_m, p_c, q_c = p[low - 1, at, :], p[low, at, :], q[low, at, :]
            _, d_m = slopes(q[low - 1, at, :])
            s_c, d_c = slopes(q_c)
            for x in range(low, high):
                p_n, q_n = p[x + 1, at, :], q[x + 1, at, :]
                s_n, d_n = slopes(q_n)
                beside = p[x, pl.ds(r - 1, size), :] + p[x, pl.ds(r + 1, size), :]
                lateral = ((p_m + p_n) + beside) - 4.0 * p_c
                q_2 = 2.0 * q_c
                horizontal = horiz[x, at, :] * lateral
                mixed = (0.25 * tilt[x, at, :]) * (d_n - d_m)
                upright = vert[x, at, :] * ((s_c - q_2) + mixed)
                old_p[x, at, :] = (2.0 * p_c - old_p[x, at, :]) + (horizontal + upright)
                old_q[x, at, :] = (q_2 - old_q[x, at, :]) + (ratio[x, at, :] * horizontal + upright)
                p_m, p_c, q_c, s_c, d_m, d_c = p_c, p_n, q_n, s_n, d_c, d_n
            return 0

        lax.fori_loop(0, (end - begin) // size, strip, 0)

        def inject(j, _):
            place = places[j]
            amount = data[NT - 1 - k, chosen[j]]
            x, y, z = place >> 16, (place >> 8) & 255, place & 255
            add = jnp.where(thin == z, amount, 0.0)
            old_p[x, pl.ds(y, 1), :] = old_p[x, pl.ds(y, 1), :] + add
            old_q[x, pl.ds(y, 1), :] = old_q[x, pl.ds(y, 1), :] + add
            return 0

        lax.fori_loop(0, count[0], inject, 0)

    y_side = jnp.where(off_y > 0, 0, 1)

    def add_image(k, p):
        t = NT - 1 - k
        pair, half = t // 2, t % 2

        def layer(x, _):
            at = jnp.clip(x - off_x, 0, width - 1)
            slot = x % 4
            rim = s_y[y_side, 2 + pair, at].astype(F32)[8 * half : 8 * half + 8]
            wide[slot, HMAX : HMAX + rows, :] = snaps[t, at].astype(F32)
            wide[slot, 0:HMAX, :] = rim
            wide[slot, HMAX + rows :, :] = rim
            term = wide[slot, pl.ds(HMAX - off_y, rows), :] * p[x + DEEP, ROW0 : ROW0 + rows, :]
            total[x] = term if k == 0 else total[x] + term
            return 0

        lax.fori_loop(0, width, layer, 0, unroll=4)

    p_now, q_now, p_old, q_old = bufs[:4]
    rim_at = pl.ds(jnp.where(off_x > 0, DEEP, DEEP + width - HMAX), HMAX)
    for k in range(NT):
        keep = pltpu.make_async_copy(p_now.at[rim_at, mid[1]], p_rims.at[k], sem_out.at[k])
        keep.start()
        add_image(k, p_now)
        step(k, p_now, q_now, p_old, q_old)
        p_now, p_old, q_now, q_old = p_old, p_now, q_old, q_now
        keep.wait()
    results = [(total, image), (p_now.at[mid], p_out), (q_now.at[mid], q_out)]
    wait_all(copy_all(results, sem_out))


def wave(receivers, data, offs, halos, own, other, bufs):
    width, rows, depth = own.shape[1:]
    block = jax.ShapeDtypeStruct((width, rows, depth), F32)
    return pl.pallas_call(
        wave_kernel,
        out_shape=(block, block, block, jax.ShapeDtypeStruct((NT, HMAX, rows, depth), F32))
        + tuple(pltpu.VMEM(b.shape, F32) for b in bufs),
        in_specs=[SMEM] * 5 + [HBM] * 10 + [VMEM] * 8,
        out_specs=(HBM,) * 4 + (VMEM,) * 8,
        input_output_aliases={15 + i: 4 + i for i in range(8)},
        scratch_shapes=[
            pltpu.VMEM((2, LAYERS, rows, depth), BF16),
            pltpu.VMEM((2, 4, width, 16, depth), BF16),
            pltpu.VMEM((2, 2, 2 * DEEP, 16, depth), BF16),
            pltpu.VMEM((width + 2 * DEEP, 16, depth), F32),
            pltpu.VMEM((NT, width, rows, depth), BF16),
            pltpu.VMEM((4, rows + 2 * HMAX, depth), F32),
            pltpu.VMEM((width, rows, depth), F32),
            pltpu.SemaphoreType.DMA((8,)),
            pltpu.SemaphoreType.DMA((2,)),
            pltpu.SemaphoreType.DMA((NT,)),
        ],
        compiler_params=params(24),
        name="wave",
    )(*receivers, data, offs, *halos, *pin((own, other)), *pin(bufs, pltpu.VMEM))[:4]


def rim_kernel(offs, *refs):
    halos, p_rims, image = refs[:6], refs[6], refs[8]
    snaps, strips, ps, wide, total, sems, sem_out = refs[9:]
    core, off_x, off_y = lax.axis_index("mem"), offs[0, 0], offs[0, 1]
    width, rows, _ = image.shape
    low = off_x > 0
    layers = jnp.abs(off_x)
    x_side = jnp.where(low, 0, 1)
    y_side = jnp.where(off_y > 0, 0, 1)
    rims = pltpu.make_async_copy(p_rims, ps, sems.at[2])
    rims.start()

    def fetch(xs, corner):
        source = corner.at[pl.ds(2 * DEEP, 2 * HMAX)]
        wait_all(copy_all([(xs, snaps), (source, strips)], sems))

    for i in range(2):
        xs, same, cross = halos[i::2]
        mine = x_side == (core if i == 0 else 1 - core)
        pl.when(mine & (x_side == y_side))(lambda xs=xs, c=same: fetch(xs, c))
        pl.when(mine & (x_side != y_side))(lambda xs=xs, c=cross: fetch(xs, c))
    rims.wait()

    def out_copy(i):
        x = jnp.where(low, i, width - layers + i)
        return pltpu.make_async_copy(total.at[i], image.at[x], sem_out.at[i])

    for i in range(HMAX):

        @pl.when(i < layers)
        def _(i=i):
            at = jnp.where(low, HMAX - layers + i, i)
            mine = jnp.where(low, i, HMAX - layers + i)
            result = None
            for pair in range(2):
                strip = strips[pair * HMAX + at].astype(F32)
                for half in range(2):
                    t = 2 * pair + half
                    rim = strip[8 * half : 8 * half + 8]
                    wide[t, HMAX : HMAX + rows, :] = snaps[t, at].astype(F32)
                    wide[t, 0:HMAX, :] = rim
                    wide[t, HMAX + rows :, :] = rim
                    term = wide[t, pl.ds(HMAX - off_y, rows), :] * ps[NT - 1 - t, mine]
                    result = term if result is None else result + term
            total[i] = result
            out_copy(i).start()

    for i in range(HMAX):
        pl.when(i < layers)(lambda i=i: out_copy(i).wait())


def rim_image(offs, halos, p_rims, image):
    width, rows, depth = image.shape
    return pl.pallas_call(
        rim_kernel,
        out_shape=jax.ShapeDtypeStruct(image.shape, F32),
        in_specs=[SMEM] + [HBM] * 8,
        out_specs=HBM,
        input_output_aliases={8: 0},
        scratch_shapes=[
            pltpu.VMEM((NT, HMAX, rows, depth), BF16),
            pltpu.VMEM((2 * HMAX, 16, depth), BF16),
            pltpu.VMEM((NT, HMAX, rows, depth), F32),
            pltpu.VMEM((NT, rows + 2 * HMAX, depth), F32),
            pltpu.VMEM((HMAX, rows, depth), F32),
            pltpu.SemaphoreType.DMA((3,)),
            pltpu.SemaphoreType.DMA((HMAX,)),
        ],
        compiler_params=params(),
        name="rim_image",
    )(offs, *halos, *pin((p_rims, image)))


def body(
    src_hist, rec_p, rec_q, prev_p, prev_q, horiz, vert, ratio, tilt, rec_pos, rec_data, lag_offs
):
    width, rows, depth = rec_p.shape
    fields = (rec_p, rec_q, prev_p, prev_q, horiz, vert, ratio, tilt)

    def swap(v):
        return lax.ppermute(v, "mem", [(0, 1), (1, 0)])

    def after(v, earlier):
        return lax.optimization_barrier((v, earlier))[0]

    def outward(v, step_x, step_y):
        count_x, count_y = lax.axis_size("gx"), lax.axis_size("gy")
        pairs = []
        for x in range(count_x):
            for y in range(count_y):
                for core, sign in ((0, 1), (1, -1)):
                    to_x, to_y = x + sign * step_x, y + sign * step_y
                    if 0 <= to_x < count_x and 0 <= to_y < count_y:
                        pairs.append(((x * count_y + y) * 2 + core, (to_x * count_y + to_y) * 2 + core))
        return lax.ppermute(v, ("gx", "gy", "mem"), pairs)

    plane = rows * lax.axis_size("gy") * depth
    x = rec_pos // plane - lax.axis_index("gx") * width + DEEP
    rest = rec_pos % plane
    y = rest // depth - lax.axis_index("gy") * rows + ROW0
    z = rest % depth
    inside = (x >= 0) & (x < width + 2 * DEEP)
    inside &= (y >= ROW0 - DEEP) & (y < ROW0 + rows + DEEP)
    target = jnp.where(inside, (x << 16) + (y << 8) + z, -1)

    other = swap(src_hist)
    packed = pack_x(fields)
    xw = outward(packed, 1, 0)
    ys, same, cross, xs = pack_rest(fields, src_hist, other, packed)
    ys, same, cross = outward(ys, 0, 1), outward(same, 1, 1), outward(cross, 1, -1)
    xs = outward(after(xs, (same, cross)), 1, 0)
    bufs, receivers = load(target, fields, packed)
    same, cross = (same, swap(same)), (cross, swap(cross))
    halos = (xw, swap(xw), ys, swap(ys)) + same + cross
    p, q, image, p_rims = wave(receivers, rec_data, lag_offs, halos, src_hist, other, bufs)
    image = rim_image(lag_offs, (xs, swap(after(xs, p))) + same + cross, p_rims, image)
    return image[None], p, q


def solution(mesh):
    block = P("gx", "gy", None)
    return jax.shard_map(
        body,
        mesh=mesh,
        in_specs=(P("mem", "gx", "gy", None),) + (block,) * 8 + (P(), P(), P("mem", None)),
        out_specs=(P("mem", "gx", "gy", None), block, block),
        check_vma=False,
    )
```

```python
import functools

import jax
import jax.numpy as jnp
from jax import lax
from jax.experimental import pallas as pl
from jax.experimental.pallas import tpu as pltpu
from jax.sharding import PartitionSpec as P

NT = 4
HMAX = 8
DEEP = NT
ROW0 = 16
GROUP = 4
F32 = jnp.float32
BF16 = jnp.bfloat16
HBM = pl.BlockSpec(memory_space=pltpu.HBM)
SMEM = pl.BlockSpec(memory_space=pltpu.SMEM)
VMEM = pl.BlockSpec(memory_space=pltpu.VMEM)
DEPTHS = (DEEP, DEEP) + (DEEP - 1,) * 6
STARTS = tuple(sum(DEPTHS[:i]) for i in range(8))
LAYERS = sum(DEPTHS)


def pin(arrays, space=pltpu.HBM):
    return [pltpu.with_memory_space_constraint(a, space) for a in arrays]


def params(mib=63):
    return pltpu.CompilerParams(vmem_limit_bytes=mib * 2**20)


def copy_all(pairs, sems):
    copies = [pltpu.make_async_copy(a, b, sems.at[i]) for i, (a, b) in enumerate(pairs)]
    for c in copies:
        c.start()
    return copies


def wait_all(copies):
    for c in copies:
        c.wait()


def pack_x_kernel(*refs):
    fields, out, stage, small, sems, out_sems = refs[:8], *refs[8:]
    core = lax.axis_index("mem")
    width = fields[0].shape[0]
    pairs = []
    for f, s, d in zip(fields, STARTS, DEPTHS):
        begin = jnp.where(core == 0, width - d, 0)
        pairs.append((f.at[pl.ds(begin, d)], stage.at[pl.ds(s, d)]))
    copies = copy_all(pairs, sems)
    sent = []
    for i, (s, d) in enumerate(zip(STARTS, DEPTHS)):
        copies[i].wait()
        small[s : s + d] = stage[s : s + d].astype(BF16)
        part = pl.ds(s, d)
        sent.append(pltpu.make_async_copy(small.at[part], out.at[part], out_sems.at[i]))
        sent[-1].start()
    wait_all(sent)


def pack_x(fields):
    shape = (LAYERS,) + fields[0].shape[1:]
    return pl.pallas_call(
        pack_x_kernel,
        out_shape=jax.ShapeDtypeStruct(shape, BF16),
        in_specs=[HBM] * 8,
        out_specs=HBM,
        scratch_shapes=[
            pltpu.VMEM(shape, F32),
            pltpu.VMEM(shape, BF16),
            pltpu.SemaphoreType.DMA((8,)),
            pltpu.SemaphoreType.DMA((8,)),
        ],
        compiler_params=params(),
        name="pack_x",
    )(*pin(fields))


def pack_rest_kernel(*refs):
    fields, own, other, _ = refs[:8], *refs[8:11]
    ys, same, cross, xs = refs[11:15]
    stage, snaps, edges, stage_c, snaps_c, mixed, s_ys, s_same, s_cross, sems, out_sems = refs[15:]
    core = lax.axis_index("mem")
    width, rows, _ = fields[0].shape
    near, far = width - DEEP, width - HMAX
    to_low = core == 1
    x_near, x_far = jnp.where(to_low, 0, near), jnp.where(to_low, 0, far)

    def y_at(low, size):
        return pl.multiple_of(jnp.where(low, 0, rows - size), size)

    pairs = []
    for i, f in enumerate(fields):
        pairs.append((f.at[:, pl.ds(y_at(to_low, 8), 8)], stage.at[i]))
        pairs.append((f.at[pl.ds(x_near, DEEP), pl.ds(y_at(~to_low, 8), 8)], stage_c.at[i]))
    for ref, half in ((own, core), (other, 1 - core)):
        pairs.append((ref.at[:, :, pl.ds(y_at(to_low, 16), 16)], snaps.at[half]))
        rim = ref.at[:, pl.ds(x_far, HMAX), pl.ds(y_at(~to_low, 16), 16)]
        pairs.append((rim, snaps_c.at[half]))
        pairs.append((ref.at[:, pl.ds(x_far, HMAX)], edges.at[pl.ds(2 * half, 2)]))
    copies = copy_all(pairs, sems)
    sent = []

    def send(a, b):
        sent.append(pltpu.make_async_copy(a, b, out_sems.at[len(sent)]))
        sent[-1].start()

    wait_all(copies[:16])
    skip, skip_c = jnp.where(to_low, 0, 4), jnp.where(to_low, 4, 0)
    for slab in range(2):
        for i in range(4):
            at = pl.ds(4 * i, 4)
            mixed[:width, at, :] = stage[4 * slab + i, :, pl.ds(skip, 4), :]
            mixed[width : width + DEEP, at, :] = stage_c[4 * slab + i, :, pl.ds(skip_c, 4), :]
        s_ys[slab] = mixed[:width].astype(BF16)
        s_cross[slab * DEEP : (slab + 1) * DEEP] = mixed[width : width + DEEP].astype(BF16)
    wait_all(copies[16:])
    for pair in range(2):
        for i in range(2):
            at = slice(8 * i, 8 * i + 8)
            both = snaps[pair, i].astype(F32)
            mixed[:width, at, :] = jnp.where(to_low, both[:, :8], both[:, 8:])
            both = snaps_c[pair, i].astype(F32)
            mixed[width : width + HMAX, at, :] = jnp.where(to_low, both[:, 8:], both[:, :8])
        s_ys[2 + pair] = mixed[:width].astype(BF16)
        begin = 2 * DEEP + pair * HMAX
        s_cross[begin : begin + HMAX] = mixed[width : width + HMAX].astype(BF16)
    send(s_ys, ys)
    send(s_cross, cross)
    send(edges, xs)
    for slab in range(2):
        begin = slab * DEEP
        s_same[begin : begin + DEEP] = s_ys[slab, pl.ds(x_near, DEEP)]
        begin = 2 * DEEP + slab * HMAX
        s_same[begin : begin + HMAX] = s_ys[2 + slab, pl.ds(x_far, HMAX)]
    send(s_same, same)
    wait_all(sent)


def pack_rest(fields, own, other, earlier):
    width, rows, depth = fields[0].shape
    corner = (2 * DEEP + 2 * HMAX, 16, depth)
    return pl.pallas_call(
        pack_rest_kernel,
        out_shape=(
            jax.ShapeDtypeStruct((4, width, 16, depth), BF16),
            jax.ShapeDtypeStruct(corner, BF16),
            jax.ShapeDtypeStruct(corner, BF16),
            jax.ShapeDtypeStruct((NT, HMAX, rows, depth), BF16),
        ),
        in_specs=[HBM] * 11,
        out_specs=(HBM,) * 4,
        scratch_shapes=[
            pltpu.VMEM((8, width, 8, depth), F32),
            pltpu.VMEM((2, 2, width, 16, depth), BF16),
            pltpu.VMEM((NT, HMAX, rows, depth), BF16),
            pltpu.VMEM((8, DEEP, 8, depth), F32),
            pltpu.VMEM((2, 2, HMAX, 16, depth), BF16),
            pltpu.VMEM((width + HMAX, 16, depth), F32),
            pltpu.VMEM((4, width, 16, depth), BF16),
            pltpu.VMEM(corner, BF16),
            pltpu.VMEM(corner, BF16),
            pltpu.SemaphoreType.DMA((22,)),
            pltpu.SemaphoreType.DMA((4,)),
        ],
        compiler_params=params(),
        name="pack_rest",
    )(*pin((*fields, own, other, earlier)))


def load_kernel(target, *refs):
    n = (len(refs) - 5) // 2
    fields, bufs, (count, chosen, places, sems) = refs[:n], refs[n + 1 : 2 * n + 1], refs[2 * n + 1 :]
    width, rows, _ = fields[0].shape
    mid = (pl.ds(DEEP, width), pl.ds(ROW0, rows))
    copies = copy_all([(f, b.at[mid]) for f, b in zip(fields, bufs)], sems)

    def one(r, n):
        place = target[r]
        chosen[n] = r
        places[n] = place
        return n + jnp.where(place >= 0, 1, 0)

    found = lax.fori_loop(0, target.shape[0], one, jnp.int32(0), unroll=8)
    for i in range(GROUP):
        chosen[found + i] = 0
        places[found + i] = 0
    count[0] = (found + GROUP - 1) // GROUP
    wait_all(copies)


def load(target, fields, earlier, name):
    width, rows, depth = fields[0].shape
    n, m = target.shape[0], len(fields)
    ints = jax.ShapeDtypeStruct((n + GROUP,), jnp.int32)
    out = pl.pallas_call(
        load_kernel,
        out_shape=(pltpu.VMEM((width + 2 * DEEP, rows + 2 * ROW0, depth), F32),) * m
        + (jax.ShapeDtypeStruct((1,), jnp.int32), ints, ints),
        in_specs=[SMEM] + [HBM] * (m + 1),
        out_specs=(VMEM,) * m + (SMEM,) * 3,
        scratch_shapes=[pltpu.SemaphoreType.DMA((m,))],
        compiler_params=params(8),
        name=name,
    )(target, *pin((*fields, earlier)))
    return out[:m], out[m:]


def wave_kernel(count, chosen, places, data, offs, *refs):
    halo_refs, own, other = refs[:8], refs[8], refs[9]
    p_out, q_out, image, p_rims = refs[18:22]
    bufs = refs[22:30]
    s_xw, s_y, s_xc, stage, snaps, wide, total, sem_halo, sem_in, sem_out = refs[30:]
    core, off_x, off_y = lax.axis_index("mem"), offs[0, 0], offs[0, 1]
    width, rows, depth = p_out.shape
    mid = (pl.ds(DEEP, width), pl.ds(ROW0, rows))
    pairs = []
    for i, side in ((0, core), (1, 1 - core)):
        xw, ys, same, cross = halo_refs[i::2]
        wave_part = pl.ds(0, 2 * DEEP)
        pairs.append((xw, s_xw.at[side]))
        pairs.append((ys, s_y.at[side]))
        pairs.append((same.at[wave_part], s_xc.at[side, side]))
        pairs.append((cross.at[wave_part], s_xc.at[side, 1 - side]))
    halos = copy_all(pairs, sem_halo)
    mains = copy_all(
        [(own, snaps.at[pl.ds(2 * core, 2)]), (other, snaps.at[pl.ds(2 - 2 * core, 2)])], sem_in
    )
    wait_all(halos)
    for side in range(2):
        for f in range(8):
            d = DEPTHS[f]
            to = DEEP - d if side == 0 else DEEP + width
            part = s_xw[side, STARTS[f] : STARTS[f] + d]
            bufs[f][to : to + d, ROW0 : ROW0 + rows, :] = part.astype(F32)
    for yside in range(2):
        to = ROW0 - DEEP if yside == 0 else ROW0 + rows
        for slab in range(2):
            stage[DEEP : DEEP + width] = s_y[yside, slab].astype(F32)
            for xside in range(2):
                at = 0 if xside == 0 else DEEP + width
                part = s_xc[xside, yside, slab * DEEP : slab * DEEP + DEEP]
                stage[at : at + DEEP] = part.astype(F32)
            for i in range(4):
                bufs[4 * slab + i][:, to : to + DEEP, :] = stage[:, 4 * i : 4 * i + 4, :]

    horiz, vert, ratio, tilt = bufs[4:]
    thin = lax.broadcasted_iota(jnp.int32, (1, depth), 1)

    def slopes(v):
        lane = lax.broadcasted_iota(jnp.int32, v.shape, 1)
        up = jnp.where(lane == depth - 1, 0.0, pltpu.roll(v, depth - 1, 1))
        down = jnp.where(lane == 0, 0.0, pltpu.roll(v, 1, 1))
        return up + down, up - down

    def step(k, p, q, old_p, old_q):
        low, high = 1 + k, width + 2 * DEEP - 1 - k
        begin, end = (ROW0 - 8, ROW0 + rows + 8) if k < NT - 1 else (ROW0, ROW0 + rows)
        size = 24 if (end - begin) % 24 == 0 else 32 if (end - begin) % 32 == 0 else 8

        def strip(i, _):
            r = pl.multiple_of(begin + i * size, 8)
            at = pl.ds(r, size)
            p_m, p_c, q_c = p[low - 1, at, :], p[low, at, :], q[low, at, :]
            _, d_m = slopes(q[low - 1, at, :])
            s_c, d_c = slopes(q_c)
            for x in range(low, high):
                p_n, q_n = p[x + 1, at, :], q[x + 1, at, :]
                s_n, d_n = slopes(q_n)
                beside = p[x, pl.ds(r - 1, size), :] + p[x, pl.ds(r + 1, size), :]
                lateral = ((p_m + p_n) + beside) - 4.0 * p_c
                q_2 = 2.0 * q_c
                horizontal = horiz[x, at, :] * lateral
                mixed = (0.25 * tilt[x, at, :]) * (d_n - d_m)
                upright = vert[x, at, :] * ((s_c - q_2) + mixed)
                old_p[x, at, :] = (2.0 * p_c - old_p[x, at, :]) + (horizontal + upright)
                old_q[x, at, :] = (q_2 - old_q[x, at, :]) + (ratio[x, at, :] * horizontal + upright)
                p_m, p_c, q_c, s_c, d_m, d_c = p_c, p_n, q_n, s_n, d_c, d_n
            if k == NT - 1:
                wait_or_start(old_p, old_q, r - ROW0, size, i, True)
            return 0

        parts = (end - begin) // size
        lax.fori_loop(0, parts, strip, 0)
        if k == NT - 1:
            for i in range(parts):
                wait_or_start(old_p, old_q, i * size, size, i, False)

    def wait_or_start(p, q, at, size, i, start):
        for j, (buf, out) in enumerate(((p, p_out), (q, q_out))):
            here = buf.at[mid[0], pl.ds(ROW0 + at, size)]
            c = pltpu.make_async_copy(here, out.at[:, pl.ds(at, size)], sem_out.at[j, i])
            c.start() if start else c.wait()

    def inject(k, old_p, old_q):
        def group(g, _):
            for i in range(GROUP):
                j = g * GROUP + i
                place = places[j]
                amount = data[NT - 1 - k, chosen[j]]
                x, y, z = place >> 16, (place >> 8) & 255, place & 255
                add = jnp.where(thin == z, amount, 0.0)
                old_p[x, pl.ds(y, 1), :] = old_p[x, pl.ds(y, 1), :] - add
                old_q[x, pl.ds(y, 1), :] = old_q[x, pl.ds(y, 1), :] - add
            return 0

        lax.fori_loop(0, count[0], group, 0)

    y_side = jnp.where(off_y > 0, 0, 1)

    def add_image(k, p):
        t = NT - 1 - k
        pair, half = t // 2, t % 2

        def layer(x, _):
            at = jnp.clip(x - off_x, 0, width - 1)
            slot = x % 4
            rim = s_y[y_side, 2 + pair, at].astype(F32)[8 * half : 8 * half + 8]
            wide[slot, HMAX : HMAX + rows, :] = snaps[t, at].astype(F32)
            wide[slot, 0:HMAX, :] = rim
            wide[slot, HMAX + rows :, :] = rim
            term = wide[slot, pl.ds(HMAX - off_y, rows), :] * p[x + DEEP, ROW0 : ROW0 + rows, :]
            total[x] = term if k == 0 else total[x] + term
            return 0

        lax.fori_loop(0, width, layer, 0, unroll=4)

    p_now, q_now, p_old, q_old = bufs[:4]
    rim_x = jnp.where(off_x > 0, DEEP, DEEP + width - HMAX)
    finished = pltpu.make_async_copy(total, image, sem_in.at[0])
    for k in range(NT):
        p_rims[k] = p_now[pl.ds(rim_x, HMAX), ROW0 : ROW0 + rows, :]
        if k == 1:
            wait_all(mains)
        if k >= 1:
            add_image(k - 1, p_old)
        if k == NT - 1:
            add_image(k, p_now)
            finished.start()
        inject(k, p_old, q_old)
        step(k, p_now, q_now, p_old, q_old)
        p_now, p_old, q_now, q_old = p_old, p_now, q_old, q_now
    finished.wait()


def wave(receivers, data, offs, halos, own, other, bufs):
    width, rows, depth = own.shape[1:]
    block = jax.ShapeDtypeStruct((width, rows, depth), F32)
    return pl.pallas_call(
        wave_kernel,
        out_shape=(block, block, block, pltpu.VMEM((NT, HMAX, rows, depth), F32))
        + tuple(pltpu.VMEM(b.shape, F32) for b in bufs),
        in_specs=[SMEM] * 5 + [HBM] * 10 + [VMEM] * 8,
        out_specs=(HBM,) * 3 + (VMEM,) * 9,
        input_output_aliases={15 + i: 4 + i for i in range(8)},
        scratch_shapes=[
            pltpu.VMEM((2, LAYERS, rows, depth), BF16),
            pltpu.VMEM((2, 4, width, 16, depth), BF16),
            pltpu.VMEM((2, 2, 2 * DEEP, 16, depth), BF16),
            pltpu.VMEM((width + 2 * DEEP, 16, depth), F32),
            pltpu.VMEM((NT, width, rows, depth), BF16),
            pltpu.VMEM((4, rows + 2 * HMAX, depth), F32),
            pltpu.VMEM((width, rows, depth), F32),
            pltpu.SemaphoreType.DMA((8,)),
            pltpu.SemaphoreType.DMA((2,)),
            pltpu.SemaphoreType.DMA((2, rows // 8)),
        ],
        compiler_params=params(24),
        name="wave",
    )(*receivers, data, offs, *halos, *pin((own, other)), *pin(bufs, pltpu.VMEM))[:4]


def rim_kernel(offs, *refs):
    halos, p_rims, image = refs[:6], refs[6], refs[8]
    snaps, strips, wide, total, sems, sem_out = refs[9:]
    core, off_x, off_y = lax.axis_index("mem"), offs[0, 0], offs[0, 1]
    width, rows, _ = image.shape
    low = off_x > 0
    layers = jnp.abs(off_x)
    x_side = jnp.where(low, 0, 1)
    y_side = jnp.where(off_y > 0, 0, 1)

    def fetch(xs, corner):
        source = corner.at[pl.ds(2 * DEEP, 2 * HMAX)]
        wait_all(copy_all([(xs, snaps), (source, strips)], sems))

    for i in range(2):
        xs, same, cross = halos[i::2]
        mine = x_side == (core if i == 0 else 1 - core)
        pl.when(mine & (x_side == y_side))(lambda xs=xs, c=same: fetch(xs, c))
        pl.when(mine & (x_side != y_side))(lambda xs=xs, c=cross: fetch(xs, c))

    def out_copy(i):
        x = jnp.where(low, i, width - layers + i)
        return pltpu.make_async_copy(total.at[i], image.at[x], sem_out.at[i])

    for i in range(HMAX):

        @pl.when(i < layers)
        def _(i=i):
            at = jnp.where(low, HMAX - layers + i, i)
            mine = jnp.where(low, i, HMAX - layers + i)
            result = None
            for pair in range(2):
                strip = strips[pair * HMAX + at].astype(F32)
                for half in range(2):
                    t = 2 * pair + half
                    rim = strip[8 * half : 8 * half + 8]
                    wide[t, HMAX : HMAX + rows, :] = snaps[t, at].astype(F32)
                    wide[t, 0:HMAX, :] = rim
                    wide[t, HMAX + rows :, :] = rim
                    term = wide[t, pl.ds(HMAX - off_y, rows), :] * p_rims[NT - 1 - t, mine]
                    result = term if result is None else result + term
            total[i] = result
            out_copy(i).start()

    for i in range(HMAX):
        pl.when(i < layers)(lambda i=i: out_copy(i).wait())


def rim_image(offs, halos, p_rims, image):
    width, rows, depth = image.shape
    return pl.pallas_call(
        rim_kernel,
        out_shape=jax.ShapeDtypeStruct(image.shape, F32),
        in_specs=[SMEM] + [HBM] * 6 + [VMEM, HBM],
        out_specs=HBM,
        input_output_aliases={8: 0},
        scratch_shapes=[
            pltpu.VMEM((NT, HMAX, rows, depth), BF16),
            pltpu.VMEM((2 * HMAX, 16, depth), BF16),
            pltpu.VMEM((NT, rows + 2 * HMAX, depth), F32),
            pltpu.VMEM((HMAX, rows, depth), F32),
            pltpu.SemaphoreType.DMA((2,)),
            pltpu.SemaphoreType.DMA((HMAX,)),
        ],
        compiler_params=params(16),
        name="rim_image",
    )(offs, *halos, *pin((p_rims,), pltpu.VMEM), *pin((image,)))


def body(
    src_hist, rec_p, rec_q, prev_p, prev_q, horiz, vert, ratio, tilt, rec_pos, rec_data, lag_offs
):
    width, rows, depth = rec_p.shape
    fields = (rec_p, rec_q, prev_p, prev_q, horiz, vert, ratio, tilt)

    def swap(v):
        return lax.ppermute(v, "mem", [(0, 1), (1, 0)])

    def after(v, earlier):
        return lax.optimization_barrier((v, earlier))[0]

    def outward(v, step_x, step_y):
        count_x, count_y = lax.axis_size("gx"), lax.axis_size("gy")
        pairs = []
        for x in range(count_x):
            for y in range(count_y):
                for core, sign in ((0, 1), (1, -1)):
                    to_x, to_y = x + sign * step_x, y + sign * step_y
                    if 0 <= to_x < count_x and 0 <= to_y < count_y:
                        pairs.append(((x * count_y + y) * 2 + core, (to_x * count_y + to_y) * 2 + core))
        return lax.ppermute(v, ("gx", "gy", "mem"), pairs)

    plane = rows * lax.axis_size("gy") * depth
    x = rec_pos // plane - lax.axis_index("gx") * width + DEEP
    rest = rec_pos % plane
    y = rest // depth - lax.axis_index("gy") * rows + ROW0
    z = rest % depth
    inside = (x >= 0) & (x < width + 2 * DEEP)
    inside &= (y >= ROW0 - DEEP) & (y < ROW0 + rows + DEEP)
    target = jnp.where(inside, (x << 16) + (y << 8) + z, -1)

    other = swap(src_hist)
    packed = pack_x(fields)
    xw = outward(packed, 1, 0)
    ys, same, cross, xs = pack_rest(fields, src_hist, other, packed)
    ys, same, cross = outward(ys, 0, 1), outward(same, 1, 1), outward(cross, 1, -1)
    factors, receivers = load(target, fields[4:], packed, "load_factors")
    xs = outward(after(xs, (same, cross, receivers)), 1, 0)
    states, _ = load(target[:8], fields[:4], receivers[2], "load_states")
    bufs = (*states, *factors)
    same, cross = (same, swap(same)), (cross, swap(cross))
    halos = (xw, swap(xw), ys, swap(ys)) + same + cross
    p, q, image, p_rims = wave(receivers, rec_data, lag_offs, halos, src_hist, other, bufs)
    image = rim_image(lag_offs, (xs, swap(after(xs, p))) + same + cross, p_rims, image)
    return image[None], p, q


def solution(mesh):
    block = P("gx", "gy", None)
    return jax.shard_map(
        body,
        mesh=mesh,
        in_specs=(P("mem", "gx", "gy", None),) + (block,) * 8 + (P(), P(), P("mem", None)),
        out_specs=(P("mem", "gx", "gy", None), block, block),
        check_vma=False,
    )
```

```python
import functools

import jax
import jax.numpy as jnp
from jax import lax
from jax.experimental import pallas as pl
from jax.experimental.pallas import tpu as pltpu
from jax.sharding import PartitionSpec as P

NT = 4
HMAX = 8
DEEP = NT
ROW0 = 16
GROUP = 4
HEAD = 8
F32 = jnp.float32
BF16 = jnp.bfloat16
HBM = pl.BlockSpec(memory_space=pltpu.HBM)
SMEM = pl.BlockSpec(memory_space=pltpu.SMEM)
VMEM = pl.BlockSpec(memory_space=pltpu.VMEM)
DEPTHS = (DEEP, DEEP) + (DEEP - 1,) * 6
STARTS = tuple(sum(DEPTHS[:i]) for i in range(8))
SENT = tuple(d - 1 for d in DEPTHS)
SENT_AT = tuple(sum(SENT[:i]) for i in range(8))
AHEAD = sum(SENT)
LAYERS = AHEAD + 3


def pin(arrays, space=pltpu.HBM):
    return [pltpu.with_memory_space_constraint(a, space) for a in arrays]


def params(mib=63):
    return pltpu.CompilerParams(vmem_limit_bytes=mib * 2**20)


def copy_all(pairs, sems):
    copies = [pltpu.make_async_copy(a, b, sems.at[i]) for i, (a, b) in enumerate(pairs)]
    for c in copies:
        c.start()
    return copies


def wait_all(copies):
    for c in copies:
        c.wait()


def slopes(v):
    depth = v.shape[-1]
    lane = lax.broadcasted_iota(jnp.int32, v.shape, 1)
    up = jnp.where(lane == depth - 1, 0.0, pltpu.roll(v, depth - 1, 1))
    down = jnp.where(lane == 0, 0.0, pltpu.roll(v, 1, 1))
    return up + down, up - down


def pack_x_kernel(*refs):
    fields, out, stage, small, sems, out_sems = refs[:8], *refs[8:]
    core = lax.axis_index("mem")
    width, rows, _ = fields[0].shape
    pairs = []
    for f, s, d in zip(fields, STARTS, DEPTHS):
        begin = jnp.where(core == 0, width - d, 0)
        pairs.append((f.at[pl.ds(begin, d)], stage.at[pl.ds(s, d)]))
    copies = copy_all(pairs, sems)
    sent = []

    def send(i, begin, size):
        part = pl.ds(begin, size)
        sent.append(pltpu.make_async_copy(small.at[part], out.at[part], out_sems.at[i]))
        sent[-1].start()

    for i in range(8):
        copies[i].wait()
        small[SENT_AT[i] : SENT_AT[i] + SENT[i]] = stage[pl.ds(STARTS[i] + 1 - core, SENT[i])].astype(BF16)
        send(i, SENT_AT[i], SENT[i])
    at = [s + (1 + core if i < 2 else 2 * core) for i, s in enumerate(STARTS)]
    p, q, old_p, old_q, horiz, vert, ratio, tilt = [stage[j] for j in at]
    row = lax.broadcasted_iota(jnp.int32, p.shape, 0)
    beside = jnp.where(row == 0, 0.0, pltpu.roll(p, 1, 0))
    beside += jnp.where(row == rows - 1, 0.0, pltpu.roll(p, rows - 1, 0))
    lateral = stage[at[0] - 1] + stage[at[0] + 1] + beside - 4.0 * p
    mixed = slopes(stage[at[1] + 1])[1] - slopes(stage[at[1] - 1])[1]
    horizontal = horiz * lateral
    upright = vert * ((slopes(q)[0] - 2.0 * q) + (0.25 * tilt) * mixed)
    small[AHEAD] = ((2.0 * p - old_p) + (horizontal + upright)).astype(BF16)
    small[AHEAD + 1] = ((2.0 * q - old_q) + (ratio * horizontal + upright)).astype(BF16)
    both = ratio * horiz
    ends = jnp.where(row == 0, horiz[:1], jnp.where(row == 1, horiz[rows - 1 :], 0.0))
    ends = jnp.where(row == 2, both[:1], jnp.where(row == 3, both[rows - 1 :], ends))
    small[AHEAD + 2] = ends.astype(BF16)
    send(8, AHEAD, 3)
    wait_all(sent)


def pack_x(fields):
    shape = fields[0].shape[1:]
    return pl.pallas_call(
        pack_x_kernel,
        out_shape=jax.ShapeDtypeStruct((LAYERS,) + shape, BF16),
        in_specs=[HBM] * 8,
        out_specs=HBM,
        scratch_shapes=[
            pltpu.VMEM((sum(DEPTHS),) + shape, F32),
            pltpu.VMEM((LAYERS,) + shape, BF16),
            pltpu.SemaphoreType.DMA((8,)),
            pltpu.SemaphoreType.DMA((9,)),
        ],
        compiler_params=params(),
        name="pack_x",
    )(*pin(fields))


def pack_rest_kernel(*refs):
    fields, own, other, _ = refs[:8], *refs[8:11]
    ys, same, cross, xs = refs[11:15]
    stage, snaps, edges, stage_c, snaps_c, mixed, s_ys, s_same, s_cross, sems, out_sems = refs[15:]
    core = lax.axis_index("mem")
    width, rows, _ = fields[0].shape
    near, far = width - DEEP, width - HMAX
    to_low = core == 1
    x_near, x_far = jnp.where(to_low, 0, near), jnp.where(to_low, 0, far)

    def y_at(low, size):
        return pl.multiple_of(jnp.where(low, 0, rows - size), size)

    pairs = []
    for i, f in enumerate(fields):
        pairs.append((f.at[:, pl.ds(y_at(to_low, 8), 8)], stage.at[i]))
        pairs.append((f.at[pl.ds(x_near, DEEP), pl.ds(y_at(~to_low, 8), 8)], stage_c.at[i]))
    for ref, half in ((own, core), (other, 1 - core)):
        pairs.append((ref.at[:, :, pl.ds(y_at(to_low, 16), 16)], snaps.at[half]))
        rim = ref.at[:, pl.ds(x_far, HMAX), pl.ds(y_at(~to_low, 16), 16)]
        pairs.append((rim, snaps_c.at[half]))
        pairs.append((ref.at[:, pl.ds(x_far, HMAX)], edges.at[pl.ds(2 * half, 2)]))
    copies = copy_all(pairs, sems)
    sent = []

    def send(a, b):
        sent.append(pltpu.make_async_copy(a, b, out_sems.at[len(sent)]))
        sent[-1].start()

    wait_all(copies[:16])
    skip, skip_c = jnp.where(to_low, 0, 4), jnp.where(to_low, 4, 0)
    for slab in range(2):
        for i in range(4):
            at = pl.ds(4 * i, 4)
            mixed[:width, at, :] = stage[4 * slab + i, :, pl.ds(skip, 4), :]
            mixed[width : width + DEEP, at, :] = stage_c[4 * slab + i, :, pl.ds(skip_c, 4), :]
        s_ys[slab] = mixed[:width].astype(BF16)
        s_cross[slab * DEEP : (slab + 1) * DEEP] = mixed[width : width + DEEP].astype(BF16)
    wait_all(copies[16:])
    for pair in range(2):
        for i in range(2):
            at = slice(8 * i, 8 * i + 8)
            both = snaps[pair, i].astype(F32)
            mixed[:width, at, :] = jnp.where(to_low, both[:, :8], both[:, 8:])
            both = snaps_c[pair, i].astype(F32)
            mixed[width : width + HMAX, at, :] = jnp.where(to_low, both[:, 8:], both[:, :8])
        s_ys[2 + pair] = mixed[:width].astype(BF16)
        begin = 2 * DEEP + pair * HMAX
        s_cross[begin : begin + HMAX] = mixed[width : width + HMAX].astype(BF16)
    send(s_ys, ys)
    send(s_cross, cross)
    send(edges, xs)
    for slab in range(2):
        begin = slab * DEEP
        s_same[begin : begin + DEEP] = s_ys[slab, pl.ds(x_near, DEEP)]
        begin = 2 * DEEP + slab * HMAX
        s_same[begin : begin + HMAX] = s_ys[2 + slab, pl.ds(x_far, HMAX)]
    send(s_same, same)
    wait_all(sent)


def pack_rest(fields, own, other, earlier):
    width, rows, depth = fields[0].shape
    corner = (2 * DEEP + 2 * HMAX, 16, depth)
    return pl.pallas_call(
        pack_rest_kernel,
        out_shape=(
            jax.ShapeDtypeStruct((4, width, 16, depth), BF16),
            jax.ShapeDtypeStruct(corner, BF16),
            jax.ShapeDtypeStruct(corner, BF16),
            jax.ShapeDtypeStruct((NT, HMAX, rows, depth), BF16),
        ),
        in_specs=[HBM] * 11,
        out_specs=(HBM,) * 4,
        scratch_shapes=[
            pltpu.VMEM((8, width, 8, depth), F32),
            pltpu.VMEM((2, 2, width, 16, depth), BF16),
            pltpu.VMEM((NT, HMAX, rows, depth), BF16),
            pltpu.VMEM((8, DEEP, 8, depth), F32),
            pltpu.VMEM((2, 2, HMAX, 16, depth), BF16),
            pltpu.VMEM((width + HMAX, 16, depth), F32),
            pltpu.VMEM((4, width, 16, depth), BF16),
            pltpu.VMEM(corner, BF16),
            pltpu.VMEM(corner, BF16),
            pltpu.SemaphoreType.DMA((22,)),
            pltpu.SemaphoreType.DMA((4,)),
        ],
        compiler_params=params(),
        name="pack_rest",
    )(*pin((*fields, own, other, earlier)))


def load_kernel(target, *refs):
    fields, bufs, (ints, listed, s_target, sems, sem_target, sem_ints) = refs[:8], refs[-14:-6], refs[-6:]
    core = lax.axis_index("mem")
    n = target.shape[0] - 4
    fetch = pltpu.make_async_copy(target, s_target, sem_target)
    fetch.start()
    width, rows, _ = fields[0].shape
    inner = width // 2 + DEEP
    pairs = []
    for f, b in zip(fields, bufs):
        to = b.at[pl.ds(DEEP * (1 - core), inner), pl.ds(ROW0, rows)]
        pairs.append((f.at[pl.ds((width - inner) * core, inner)], to))
    copies = copy_all(pairs, sems)
    fetch.wait()

    def one(r, at):
        place = s_target[r]
        listed[at] = r
        listed[at + n + GROUP] = place
        return at + jnp.where(place >= 0, 1, 0)

    end = lax.fori_loop(0, n, one, jnp.int32(HEAD), unroll=16)
    for i in range(GROUP):
        listed[end + i] = 0
        listed[end + i + n + GROUP] = 0
    listed[0] = (end - HEAD + GROUP - 1) // GROUP
    for i in range(4):
        listed[1 + i] = s_target[n + i]
    save = pltpu.make_async_copy(listed, ints, sem_ints)
    save.start()
    wait_all(copies + [save])


def load(fields, earlier, target):
    width, rows, depth = fields[0].shape
    any_space = pl.BlockSpec(memory_space=pl.ANY)
    n = target.shape[0] - 4
    listed = (HEAD + 2 * (n + GROUP),)
    shape = (width // 2 + 2 * DEEP, rows + 2 * ROW0, depth)
    return pl.pallas_call(
        load_kernel,
        out_shape=(pltpu.VMEM(shape, F32),) * 8 + (jax.ShapeDtypeStruct(listed, jnp.int32),),
        in_specs=[any_space] + [HBM] * 8 + [any_space],
        out_specs=(VMEM,) * 8 + (any_space,),
        scratch_shapes=[
            pltpu.SMEM(listed, jnp.int32),
            pltpu.SMEM((n + 4,), jnp.int32),
            pltpu.SemaphoreType.DMA((8,)),
            pltpu.SemaphoreType.DMA,
            pltpu.SemaphoreType.DMA,
        ],
        compiler_params=params(8),
        name="load",
    )(target, *pin(fields), earlier)


def wave_kernel(ints, amounts, *refs):
    xw, y_own, y_other, same, cross, own, other = refs[:7]
    p_out, q_out, *totals, p_rims = refs[16:21]
    bufs = refs[21:29]
    listed, data, stage, snaps, wide, outer, sem_in = refs[29:]
    core = lax.axis_index("mem")
    half, rows, depth = p_out.shape
    lists = copy_all([(ints, listed), (amounts, data)], sem_in)
    near = pl.ds(core * HMAX, half + HMAX)
    mains = copy_all(
        [
            (own.at[:, near], snaps.at[pl.ds(2 * core, 2)]),
            (other.at[:, near], snaps.at[pl.ds(2 - 2 * core, 2)]),
        ],
        sem_in.at[pl.ds(2, 2)],
    )
    face = core * (half + DEEP)
    inner = half + DEEP
    for f in range(8):
        d = SENT[f]
        to = jnp.where(core == 0, DEEP - d, half + DEEP)
        part = xw[SENT_AT[f] : SENT_AT[f] + d]
        bufs[f][pl.ds(to, d), ROW0 : ROW0 + rows, :] = part.astype(F32)
    for ys, corner, side in ((y_own, same, core), (y_other, cross, 1 - core)):
        to = jnp.where(side == 0, ROW0 - DEEP, ROW0 + rows)
        for slab in range(2):
            part = ys[slab, pl.ds(core * (half - DEEP), inner)]
            stage[pl.ds(DEEP * (1 - core), inner)] = part.astype(F32)
            part = corner[slab * DEEP : slab * DEEP + DEEP]
            stage[pl.ds(face, DEEP)] = part.astype(F32)
            for i in range(4):
                bufs[4 * slab + i][:, pl.ds(to, DEEP), :] = stage[:, 4 * i : 4 * i + 4, :]

    wait_all(lists)
    horiz, vert, ratio, tilt = bufs[4:]
    thin = lax.broadcasted_iota(jnp.int32, (1, depth), 1)

    def step(k, p, q, old_p, old_q):
        low, high = 1 + k, half + 2 * DEEP - 1 - k
        begin, end = (ROW0 - 8, ROW0 + rows + 8) if k < NT - 1 else (ROW0, ROW0 + rows)
        size = 24 if (end - begin) % 24 == 0 else 32 if (end - begin) % 32 == 0 else 8

        def strip(i, _):
            r = pl.multiple_of(begin + i * size, 8)
            at = pl.ds(r, size)
            p_m, p_c, q_c = p[low - 1, at, :], p[low, at, :], q[low, at, :]
            _, d_m = slopes(q[low - 1, at, :])
            s_c, d_c = slopes(q_c)
            for x in range(low, high):
                p_n, q_n = p[x + 1, at, :], q[x + 1, at, :]
                s_n, d_n = slopes(q_n)
                beside = p[x, pl.ds(r - 1, size), :] + p[x, pl.ds(r + 1, size), :]
                lateral = ((p_m + p_n) + beside) - 4.0 * p_c
                q_2 = 2.0 * q_c
                horizontal = horiz[x, at, :] * lateral
                mixed = (0.25 * tilt[x, at, :]) * (d_n - d_m)
                upright = vert[x, at, :] * ((s_c - q_2) + mixed)
                p_new = (2.0 * p_c - old_p[x, at, :]) + (horizontal + upright)
                q_new = (q_2 - old_q[x, at, :]) + (ratio[x, at, :] * horizontal + upright)
                if k < NT - 1:
                    old_p[x, at, :] = p_new
                    old_q[x, at, :] = q_new
                else:
                    out_at = pl.ds(pl.multiple_of(r - ROW0, 8), size)
                    p_out[x - DEEP, out_at, :] = p_new
                    q_out[x - DEEP, out_at, :] = q_new
                p_m, p_c, q_c, s_c, d_m, d_c = p_c, p_n, q_n, s_n, d_c, d_n
            return 0

        lax.fori_loop(0, (end - begin) // size, strip, 0)

    def inject(k, old_p, old_q):
        def group(g, _):
            for i in range(GROUP):
                j = HEAD + g * GROUP + i
                place = listed[j + (listed.shape[0] - HEAD) // 2]
                amount = data[NT - 1 - k, listed[j]]
                x, y, z = place >> 16, (place >> 8) & 255, place & 255
                add = jnp.where(thin == z, amount, 0.0)
                old_p[x, pl.ds(y, 1), :] = old_p[x, pl.ds(y, 1), :] - add
                old_q[x, pl.ds(y, 1), :] = old_q[x, pl.ds(y, 1), :] - add
            return 0

        lax.fori_loop(0, listed[0], group, 0)

    def add_image(k, p, lag):
        off_x, off_y = listed[1 + 2 * lag], listed[2 + 2 * lag]
        t = NT - 1 - k
        pair, part = t // 2, t % 2
        from_own = core == jnp.where(off_y > 0, 0, 1)

        def layer(i, _):
            at = jnp.clip(core * HMAX + i - off_x, 0, half + HMAX - 1)
            slot = i % 4
            mine, others = y_own[2 + pair, core * HMAX + at], y_other[2 + pair, core * HMAX + at]
            rim = jnp.where(from_own, mine.astype(F32), others.astype(F32))
            rim = rim[8 * part : 8 * part + 8]
            wide[slot, HMAX : HMAX + rows, :] = snaps[t, at].astype(F32)
            wide[slot, 0:HMAX, :] = rim
            wide[slot, HMAX + rows :, :] = rim
            term = wide[slot, pl.ds(HMAX - off_y, rows), :] * p[i + DEEP, ROW0 : ROW0 + rows, :]
            totals[lag][i] = term if k == 0 else totals[lag][i] + term
            return 0

        lax.fori_loop(0, half, layer, 0, unroll=4)

    p_now, q_now, p_old, q_old = bufs[:4]
    main = slice(ROW0, ROW0 + rows)
    far = jnp.where(core == 0, DEEP - 3, half + DEEP + 2)
    for buf in (p_old, q_old):
        buf[far, main, :] = jnp.zeros((rows, depth), F32)
    for k in range(NT):
        inject(k, p_old, q_old)
        if k == 0:
            row = lax.broadcasted_iota(jnp.int32, (rows, depth), 0)
            ends = xw[AHEAD + 2].astype(F32)
            before, behind = p_now[far, pl.ds(ROW0 - 1, 1), :], p_now[far, pl.ds(ROW0 + rows, 1), :]
            for i, buf in enumerate((p_old, q_old)):
                value = xw[AHEAD + i].astype(F32) - buf[far, main, :]
                value += jnp.where(row == 0, ends[2 * i : 2 * i + 1] * before, 0.0)
                value += jnp.where(row == rows - 1, ends[2 * i + 1 : 2 * i + 2] * behind, 0.0)
                outer[i] = value
        p_rims[k] = p_now[pl.ds(DEEP + core * HMAX, HMAX), ROW0 : ROW0 + rows, :]
        step(k, p_now, q_now, p_old, q_old)
        if k == 0:
            for i, buf in enumerate((p_old, q_old)):
                buf[far, main, :] = outer[i]
            wait_all(mains)
        for lag in range(2):
            add_image(k, p_now, lag)
        p_now, p_old, q_now, q_old = p_old, p_now, q_old, q_now


def wave(ints, data, halos, own, other, earlier, bufs):
    width, rows, depth = own.shape[1:]
    half = width // 2
    any_space = pl.BlockSpec(memory_space=pl.ANY)
    return pl.pallas_call(
        wave_kernel,
        out_shape=(
            *(pltpu.VMEM((half, rows, depth), F32),) * 4,
            pltpu.VMEM((NT, HMAX, rows, depth), F32),
        )
        + tuple(pltpu.VMEM(b.shape, F32) for b in bufs),
        in_specs=[any_space] * 2 + [VMEM] * 5 + [HBM] * 2 + [any_space] + [VMEM] * 8,
        out_specs=(VMEM,) * 13,
        input_output_aliases={10 + i: 5 + i for i in range(8)},
        scratch_shapes=[
            pltpu.SMEM(ints.shape, jnp.int32),
            pltpu.SMEM(data.shape, F32),
            pltpu.VMEM((half + 2 * DEEP, 16, depth), F32),
            pltpu.VMEM((NT, half + HMAX, rows, depth), BF16),
            pltpu.VMEM((4, rows + 2 * HMAX, depth), F32),
            pltpu.VMEM((2, rows, depth), F32),
            pltpu.SemaphoreType.DMA((4,)),
        ],
        compiler_params=params(8),
        name="wave",
    )(ints, data, *pin(halos, pltpu.VMEM), *pin((own, other)), earlier, *pin(bufs, pltpu.VMEM))[:5]


def merge_kernel(*refs):
    halves, outs, sems = refs[:6], refs[6:9], refs[9]
    core = lax.axis_index("mem")
    half = outs[0].shape[0] // 2
    pairs = []
    for i, out in enumerate(outs):
        pairs.append((halves[2 * i], out.at[pl.ds(half * core, half)]))
        pairs.append((halves[2 * i + 1], out.at[pl.ds(half - half * core, half)]))
    wait_all(copy_all(pairs, sems))


def merge(p, p_other, q, q_other, total, image_other):
    block = jax.ShapeDtypeStruct((2 * p.shape[0],) + p.shape[1:], F32)
    return pl.pallas_call(
        merge_kernel,
        out_shape=(block,) * 3,
        in_specs=[VMEM] * 6,
        out_specs=(HBM,) * 3,
        scratch_shapes=[pltpu.SemaphoreType.DMA((6,))],
        compiler_params=params(8),
        name="merge",
    )(*pin((p, p_other, q, q_other, total, image_other), pltpu.VMEM))


def rim_kernel(offs, offs_other, xs, same, cross, p_rims, _, total, given, wide):
    core = lax.axis_index("mem")
    half, rows, _ = total.shape
    for lag, off in enumerate((offs, offs_other)):
        off_x, off_y = off[0, 0], off[0, 1]
        layers = jnp.maximum(jnp.where(core == 0, off_x, -off_x), 0)
        from_same = core == jnp.where(off_y > 0, 0, 1)

        def layer(i, lag=lag, off_y=off_y, layers=layers, from_same=from_same):
            at = jnp.where(core == 0, HMAX - layers + i, i)
            mine = jnp.where(core == 0, i, HMAX - layers + i)
            result = None
            for pair in range(2):
                place = 2 * DEEP + pair * HMAX + at
                strip = jnp.where(from_same, same[place].astype(F32), cross[place].astype(F32))
                for part in range(2):
                    t = 2 * pair + part
                    rim = strip[8 * part : 8 * part + 8]
                    wide[t, HMAX : HMAX + rows, :] = xs[t, at].astype(F32)
                    wide[t, 0:HMAX, :] = rim
                    wide[t, HMAX + rows :, :] = rim
                    term = wide[t, pl.ds(HMAX - off_y, rows), :] * p_rims[NT - 1 - t, mine]
                    result = term if result is None else result + term
            if lag == 1:
                given[i] = result
            else:
                total[jnp.where(core == 0, i, half - layers + i)] = result

        for i in range(HMAX):
            pl.when(i < layers)(lambda i=i, layer=layer: layer(i))


def rim_image(offs, offs_other, halos, p_rims, total):
    half, rows, depth = total.shape
    return pl.pallas_call(
        rim_kernel,
        out_shape=(
            pltpu.VMEM(total.shape, F32),
            pltpu.VMEM((HMAX, rows, depth), F32),
        ),
        in_specs=[SMEM] * 2 + [VMEM] * 5,
        out_specs=(VMEM, VMEM),
        input_output_aliases={6: 0},
        scratch_shapes=[pltpu.VMEM((NT, rows + 2 * HMAX, depth), F32)],
        compiler_params=params(8),
        name="rim_image",
    )(offs, offs_other, *pin((*halos, p_rims, total), pltpu.VMEM))


def place_kernel(offs, given, _, image, sem_out):
    core = lax.axis_index("mem")
    width = image.shape[0]
    layers = jnp.maximum(jnp.where(core == 0, -offs[0, 0], offs[0, 0]), 0)

    def out_copy(i):
        x = jnp.where(core == 0, width - layers + i, i)
        return pltpu.make_async_copy(given.at[i], image.at[x], sem_out.at[i])

    for i in range(HMAX):
        pl.when(i < layers)(lambda i=i: out_copy(i).start())
    for i in range(HMAX):
        pl.when(i < layers)(lambda i=i: out_copy(i).wait())


def place_rim(offs, given, image):
    return pl.pallas_call(
        place_kernel,
        out_shape=jax.ShapeDtypeStruct(image.shape, F32),
        in_specs=[SMEM, VMEM, HBM],
        out_specs=HBM,
        input_output_aliases={2: 0},
        scratch_shapes=[pltpu.SemaphoreType.DMA((HMAX,))],
        compiler_params=params(8),
        name="place_rim",
    )(offs, *pin((given,), pltpu.VMEM), *pin((image,)))


def body(
    src_hist, rec_p, rec_q, prev_p, prev_q, horiz, vert, ratio, tilt, rec_pos, rec_data, lag_offs
):
    width, rows, depth = rec_p.shape
    fields = (rec_p, rec_q, prev_p, prev_q, horiz, vert, ratio, tilt)

    def swap(v):
        return lax.ppermute(v, "mem", [(0, 1), (1, 0)])

    def after(v, earlier):
        return lax.optimization_barrier((v, earlier))[0]

    def outward(v, step_x, step_y):
        count_x, count_y = lax.axis_size("gx"), lax.axis_size("gy")
        pairs = []
        for x in range(count_x):
            for y in range(count_y):
                for core, sign in ((0, 1), (1, -1)):
                    to_x, to_y = x + sign * step_x, y + sign * step_y
                    if 0 <= to_x < count_x and 0 <= to_y < count_y:
                        pairs.append(((x * count_y + y) * 2 + core, (to_x * count_y + to_y) * 2 + core))
        return lax.ppermute(v, ("gx", "gy", "mem"), pairs)

    plane = rows * lax.axis_size("gy") * depth
    half = width // 2
    x = rec_pos // plane - lax.axis_index("gx") * width - lax.axis_index("mem") * half + DEEP
    rest = rec_pos % plane
    y = rest // depth - lax.axis_index("gy") * rows + ROW0
    z = rest % depth
    inside = (x >= 0) & (x < half + 2 * DEEP)
    inside &= (y >= ROW0 - DEEP) & (y < ROW0 + rows + DEEP)
    target = jnp.where(inside, (x << 16) + (y << 8) + z, -1)
    offs_other = swap(lag_offs)
    target = jnp.concatenate([target, lag_offs[0], offs_other[0]])

    other = swap(src_hist)
    packed = pack_x(fields)
    xw = outward(packed, 1, 0)
    ys, same, cross, xs = pack_rest(fields, src_hist, other, packed)
    ys, same, cross = outward(ys, 0, 1), outward(same, 1, 1), outward(cross, 1, -1)
    *bufs, ints = load(fields, packed, target)
    xs = outward(after(xs, (same, cross)), 1, 0)
    halos = (xw, ys, swap(ys), same, cross)
    token = swap(xw[0, :16])
    p, q, total, total_other, p_rims = wave(ints, rec_data, halos, src_hist, other, token, bufs)
    parts = (swap(p), swap(q), swap(total_other))
    total, given = rim_image(lag_offs, offs_other, (after(xs, p), same, cross), p_rims, total)
    p, q, image = merge(p, parts[0], q, parts[1], total, parts[2])
    image = place_rim(lag_offs, swap(given), image)
    return image[None], p, q


def solution(mesh):
    block = P("gx", "gy", None)
    return jax.shard_map(
        body,
        mesh=mesh,
        in_specs=(P("mem", "gx", "gy", None),) + (block,) * 8 + (P(), P(), P("mem", None)),
        out_specs=(P("mem", "gx", "gy", None), block, block),
        check_vma=False,
    )
```

```python
import functools

import jax
import jax.numpy as jnp
from jax import lax
from jax.experimental import pallas as pl
from jax.experimental.pallas import tpu as pltpu
from jax.sharding import PartitionSpec as P

NT = 4
HMAX = 8
DEEP = NT
ROW0 = 16
GROUP = 4
HEAD = 8
F32 = jnp.float32
BF16 = jnp.bfloat16
HBM = pl.BlockSpec(memory_space=pltpu.HBM)
SMEM = pl.BlockSpec(memory_space=pltpu.SMEM)
VMEM = pl.BlockSpec(memory_space=pltpu.VMEM)
DEPTHS = (DEEP, DEEP) + (DEEP - 1,) * 6
STARTS = tuple(sum(DEPTHS[:i]) for i in range(8))
SENT = tuple(d - 1 for d in DEPTHS)
SENT_AT = tuple(sum(SENT[:i]) for i in range(8))
AHEAD = sum(SENT)
LAYERS = AHEAD + 3


def pin(arrays, space=pltpu.HBM):
    return [pltpu.with_memory_space_constraint(a, space) for a in arrays]


def params(mib=63):
    return pltpu.CompilerParams(vmem_limit_bytes=mib * 2**20)


def copy_all(pairs, sems):
    copies = [pltpu.make_async_copy(a, b, sems.at[i]) for i, (a, b) in enumerate(pairs)]
    for c in copies:
        c.start()
    return copies


def wait_all(copies):
    for c in copies:
        c.wait()


def slopes(v):
    depth = v.shape[-1]
    lane = lax.broadcasted_iota(jnp.int32, v.shape, 1)
    up = jnp.where(lane == depth - 1, 0.0, pltpu.roll(v, depth - 1, 1))
    down = jnp.where(lane == 0, 0.0, pltpu.roll(v, 1, 1))
    return up + down, up - down


def pack_x_kernel(*refs):
    fields, small, stage, sems = refs[:8], *refs[8:]
    core = lax.axis_index("mem")
    width, rows, _ = fields[0].shape
    pairs = []
    for f, s, d in zip(fields, STARTS, DEPTHS):
        begin = jnp.where(core == 0, width - d, 0)
        pairs.append((f.at[pl.ds(begin, d)], stage.at[pl.ds(s, d)]))
    copies = copy_all(pairs, sems)
    for i in range(8):
        copies[i].wait()
        small[SENT_AT[i] : SENT_AT[i] + SENT[i]] = stage[pl.ds(STARTS[i] + 1 - core, SENT[i])].astype(BF16)
    at = [s + (1 + core if i < 2 else 2 * core) for i, s in enumerate(STARTS)]
    p, q, old_p, old_q, horiz, vert, ratio, tilt = [stage[j] for j in at]
    row = lax.broadcasted_iota(jnp.int32, p.shape, 0)
    beside = jnp.where(row == 0, 0.0, pltpu.roll(p, 1, 0))
    beside += jnp.where(row == rows - 1, 0.0, pltpu.roll(p, rows - 1, 0))
    lateral = stage[at[0] - 1] + stage[at[0] + 1] + beside - 4.0 * p
    mixed = slopes(stage[at[1] + 1])[1] - slopes(stage[at[1] - 1])[1]
    horizontal = horiz * lateral
    upright = vert * ((slopes(q)[0] - 2.0 * q) + (0.25 * tilt) * mixed)
    small[AHEAD] = ((2.0 * p - old_p) + (horizontal + upright)).astype(BF16)
    small[AHEAD + 1] = ((2.0 * q - old_q) + (ratio * horizontal + upright)).astype(BF16)
    both = ratio * horiz
    ends = jnp.where(row == 0, horiz[:1], jnp.where(row == 1, horiz[rows - 1 :], 0.0))
    ends = jnp.where(row == 2, both[:1], jnp.where(row == 3, both[rows - 1 :], ends))
    small[AHEAD + 2] = ends.astype(BF16)


def pack_x(fields):
    shape = fields[0].shape[1:]
    return pl.pallas_call(
        pack_x_kernel,
        out_shape=pltpu.VMEM((LAYERS,) + shape, BF16),
        in_specs=[HBM] * 8,
        out_specs=VMEM,
        scratch_shapes=[
            pltpu.VMEM((sum(DEPTHS),) + shape, F32),
            pltpu.SemaphoreType.DMA((8,)),
        ],
        compiler_params=params(16),
        name="pack_x",
    )(*pin(fields))


def pack_rest_kernel(*refs):
    fields, own, other = refs[:8], *refs[8:10]
    s_ys, s_same, s_cross, edges = refs[10:14]
    stage, snaps, stage_c, snaps_c, mixed, sems = refs[14:]
    core = lax.axis_index("mem")
    width, rows, _ = fields[0].shape
    near, far = width - DEEP, width - HMAX
    to_low = core == 1
    x_near, x_far = jnp.where(to_low, 0, near), jnp.where(to_low, 0, far)

    def y_at(low, size):
        return pl.multiple_of(jnp.where(low, 0, rows - size), size)

    pairs = []
    for i, f in enumerate(fields):
        pairs.append((f.at[:, pl.ds(y_at(to_low, 8), 8)], stage.at[i]))
        pairs.append((f.at[pl.ds(x_near, DEEP), pl.ds(y_at(~to_low, 8), 8)], stage_c.at[i]))
    for ref, half in ((own, core), (other, 1 - core)):
        pairs.append((ref.at[:, :, pl.ds(y_at(to_low, 16), 16)], snaps.at[half]))
        rim = ref.at[:, pl.ds(x_far, HMAX), pl.ds(y_at(~to_low, 16), 16)]
        pairs.append((rim, snaps_c.at[half]))
        pairs.append((ref.at[:, pl.ds(x_far, HMAX)], edges.at[pl.ds(2 * half, 2)]))
    copies = copy_all(pairs, sems)
    wait_all(copies[:16])
    skip, skip_c = jnp.where(to_low, 0, 4), jnp.where(to_low, 4, 0)
    for slab in range(2):
        for i in range(4):
            at = pl.ds(4 * i, 4)
            mixed[:width, at, :] = stage[4 * slab + i, :, pl.ds(skip, 4), :]
            mixed[width : width + DEEP, at, :] = stage_c[4 * slab + i, :, pl.ds(skip_c, 4), :]
        s_ys[slab] = mixed[:width].astype(BF16)
        s_cross[slab * DEEP : (slab + 1) * DEEP] = mixed[width : width + DEEP].astype(BF16)
    wait_all(copies[16:])
    for pair in range(2):
        for i in range(2):
            at = slice(8 * i, 8 * i + 8)
            both = snaps[pair, i].astype(F32)
            mixed[:width, at, :] = jnp.where(to_low, both[:, :8], both[:, 8:])
            both = snaps_c[pair, i].astype(F32)
            mixed[width : width + HMAX, at, :] = jnp.where(to_low, both[:, 8:], both[:, :8])
        s_ys[2 + pair] = mixed[:width].astype(BF16)
        begin = 2 * DEEP + pair * HMAX
        s_cross[begin : begin + HMAX] = mixed[width : width + HMAX].astype(BF16)
    for slab in range(2):
        begin = slab * DEEP
        s_same[begin : begin + DEEP] = s_ys[slab, pl.ds(x_near, DEEP)]
        begin = 2 * DEEP + slab * HMAX
        s_same[begin : begin + HMAX] = s_ys[2 + slab, pl.ds(x_far, HMAX)]


def pack_rest(fields, own, other):
    width, rows, depth = fields[0].shape
    corner = (2 * DEEP + 2 * HMAX, 16, depth)
    return pl.pallas_call(
        pack_rest_kernel,
        out_shape=(
            pltpu.VMEM((4, width, 16, depth), BF16),
            pltpu.VMEM(corner, BF16),
            pltpu.VMEM(corner, BF16),
            pltpu.VMEM((NT, HMAX, rows, depth), BF16),
        ),
        in_specs=[HBM] * 9 + [pl.BlockSpec(memory_space=pl.ANY)],
        out_specs=(VMEM,) * 4,
        scratch_shapes=[
            pltpu.VMEM((8, width, 8, depth), F32),
            pltpu.VMEM((2, 2, width, 16, depth), BF16),
            pltpu.VMEM((8, DEEP, 8, depth), F32),
            pltpu.VMEM((2, 2, HMAX, 16, depth), BF16),
            pltpu.VMEM((width + HMAX, 16, depth), F32),
            pltpu.SemaphoreType.DMA((22,)),
        ],
        compiler_params=params(16),
        name="pack_rest",
    )(*pin((*fields, own)), other)


def load_kernel(target, *refs):
    fields, bufs, (ints, listed, s_target, sems, sem_target, sem_ints) = refs[:8], refs[-14:-6], refs[-6:]
    core = lax.axis_index("mem")
    n = target.shape[0] - 4
    fetch = pltpu.make_async_copy(target, s_target, sem_target)
    fetch.start()
    width, rows, _ = fields[0].shape
    inner = width // 2 + DEEP
    pairs = []
    for f, b in zip(fields, bufs):
        to = b.at[pl.ds(DEEP * (1 - core), inner), pl.ds(ROW0, rows)]
        pairs.append((f.at[pl.ds((width - inner) * core, inner)], to))
    copies = copy_all(pairs, sems)
    fetch.wait()

    def one(r, at):
        place = s_target[r]
        listed[at] = r
        listed[at + n + GROUP] = place
        return at + jnp.where(place >= 0, 1, 0)

    end = lax.fori_loop(0, n, one, jnp.int32(HEAD), unroll=16)
    for i in range(GROUP):
        listed[end + i] = 0
        listed[end + i + n + GROUP] = 0
    listed[0] = (end - HEAD + GROUP - 1) // GROUP
    for i in range(4):
        listed[1 + i] = s_target[n + i]
    save = pltpu.make_async_copy(listed, ints, sem_ints)
    save.start()
    wait_all(copies + [save])


def load(fields, target):
    width, rows, depth = fields[0].shape
    any_space = pl.BlockSpec(memory_space=pl.ANY)
    n = target.shape[0] - 4
    listed = (HEAD + 2 * (n + GROUP),)
    shape = (width // 2 + 2 * DEEP, rows + 2 * ROW0, depth)
    return pl.pallas_call(
        load_kernel,
        out_shape=(pltpu.VMEM(shape, F32),) * 8 + (jax.ShapeDtypeStruct(listed, jnp.int32),),
        in_specs=[any_space] + [HBM] * 8,
        out_specs=(VMEM,) * 8 + (any_space,),
        scratch_shapes=[
            pltpu.SMEM(listed, jnp.int32),
            pltpu.SMEM((n + 4,), jnp.int32),
            pltpu.SemaphoreType.DMA((8,)),
            pltpu.SemaphoreType.DMA,
            pltpu.SemaphoreType.DMA,
        ],
        compiler_params=params(8),
        name="load",
    )(target, *pin(fields))


def wave_kernel(ints, amounts, *refs):
    xw, y_own, y_other, same, cross, own, other = refs[:7]
    p_out, q_out, *totals, p_rims = refs[16:21]
    bufs = refs[21:29]
    listed, data, stage, snaps, wide, outer, sem_in = refs[29:]
    core = lax.axis_index("mem")
    half, rows, depth = p_out.shape
    lists = copy_all([(ints, listed), (amounts, data)], sem_in)
    near = pl.ds(core * HMAX, half + HMAX)
    mains = copy_all(
        [
            (own.at[:, near], snaps.at[pl.ds(2 * core, 2)]),
            (other.at[:, near], snaps.at[pl.ds(2 - 2 * core, 2)]),
        ],
        sem_in.at[pl.ds(2, 2)],
    )
    face = core * (half + DEEP)
    inner = half + DEEP
    for f in range(8):
        d = SENT[f]
        to = jnp.where(core == 0, DEEP - d, half + DEEP)
        part = xw[SENT_AT[f] : SENT_AT[f] + d]
        bufs[f][pl.ds(to, d), ROW0 : ROW0 + rows, :] = part.astype(F32)
    for ys, corner, side in ((y_own, same, core), (y_other, cross, 1 - core)):
        to = jnp.where(side == 0, ROW0 - DEEP, ROW0 + rows)
        for slab in range(2):
            part = ys[slab, pl.ds(core * (half - DEEP), inner)]
            stage[pl.ds(DEEP * (1 - core), inner)] = part.astype(F32)
            part = corner[slab * DEEP : slab * DEEP + DEEP]
            stage[pl.ds(face, DEEP)] = part.astype(F32)
            for i in range(4):
                bufs[4 * slab + i][:, pl.ds(to, DEEP), :] = stage[:, 4 * i : 4 * i + 4, :]

    wait_all(lists)
    horiz, vert, ratio, tilt = bufs[4:]
    thin = lax.broadcasted_iota(jnp.int32, (1, depth), 1)

    def step(k, p, q, old_p, old_q):
        low, high = 1 + k, half + 2 * DEEP - 1 - k
        begin, end = (ROW0 - 8, ROW0 + rows + 8) if k < NT - 1 else (ROW0, ROW0 + rows)
        size = 48 if (end - begin) % 48 == 0 else 64 if (end - begin) % 64 == 0 else 8

        def strip(i, _):
            r = pl.multiple_of(begin + i * size, 8)
            at = pl.ds(r, size)
            p_m, p_c, q_c = p[low - 1, at, :], p[low, at, :], q[low, at, :]
            _, d_m = slopes(q[low - 1, at, :])
            s_c, d_c = slopes(q_c)
            for x in range(low, high):
                p_n, q_n = p[x + 1, at, :], q[x + 1, at, :]
                s_n, d_n = slopes(q_n)
                beside = p[x, pl.ds(r - 1, size), :] + p[x, pl.ds(r + 1, size), :]
                lateral = ((p_m + p_n) + beside) - 4.0 * p_c
                q_2 = 2.0 * q_c
                horizontal = horiz[x, at, :] * lateral
                mixed = (0.25 * tilt[x, at, :]) * (d_n - d_m)
                upright = vert[x, at, :] * ((s_c - q_2) + mixed)
                p_new = (2.0 * p_c - old_p[x, at, :]) + (horizontal + upright)
                q_new = (q_2 - old_q[x, at, :]) + (ratio[x, at, :] * horizontal + upright)
                if k < NT - 1:
                    old_p[x, at, :] = p_new
                    old_q[x, at, :] = q_new
                else:
                    out_at = pl.ds(pl.multiple_of(r - ROW0, 8), size)
                    p_out[x - DEEP, out_at, :] = p_new
                    q_out[x - DEEP, out_at, :] = q_new
                p_m, p_c, q_c, s_c, d_m, d_c = p_c, p_n, q_n, s_n, d_c, d_n
            return 0

        lax.fori_loop(0, (end - begin) // size, strip, 0)

    def inject(k, old_p, old_q):
        def group(g, _):
            for i in range(GROUP):
                j = HEAD + g * GROUP + i
                place = listed[j + (listed.shape[0] - HEAD) // 2]
                amount = data[NT - 1 - k, listed[j]]
                x, y, z = place >> 16, (place >> 8) & 255, place & 255
                add = jnp.where(thin == z, amount, 0.0)
                old_p[x, pl.ds(y, 1), :] = old_p[x, pl.ds(y, 1), :] - add
                old_q[x, pl.ds(y, 1), :] = old_q[x, pl.ds(y, 1), :] - add
            return 0

        lax.fori_loop(0, listed[0], group, 0)

    def add_image(k, p, lag):
        off_x, off_y = listed[1 + 2 * lag], listed[2 + 2 * lag]
        t = NT - 1 - k
        pair, part = t // 2, t % 2
        from_own = core == jnp.where(off_y > 0, 0, 1)

        def layer(i, _):
            at = jnp.clip(core * HMAX + i - off_x, 0, half + HMAX - 1)
            slot = i % 8
            mine, others = y_own[2 + pair, core * HMAX + at], y_other[2 + pair, core * HMAX + at]
            rim = jnp.where(from_own, mine.astype(F32), others.astype(F32))
            rim = rim[8 * part : 8 * part + 8]
            wide[slot, HMAX : HMAX + rows, :] = snaps[t, at].astype(F32)
            wide[slot, 0:HMAX, :] = rim
            wide[slot, HMAX + rows :, :] = rim
            term = wide[slot, pl.ds(HMAX - off_y, rows), :] * p[i + DEEP, ROW0 : ROW0 + rows, :]
            totals[lag][i] = term if k == 0 else totals[lag][i] + term
            return 0

        lax.fori_loop(0, half, layer, 0, unroll=8)

    p_now, q_now, p_old, q_old = bufs[:4]
    main = slice(ROW0, ROW0 + rows)
    far = jnp.where(core == 0, DEEP - 3, half + DEEP + 2)
    for buf in (p_old, q_old):
        buf[far, main, :] = jnp.zeros((rows, depth), F32)
    for k in range(NT):
        inject(k, p_old, q_old)
        if k == 0:
            row = lax.broadcasted_iota(jnp.int32, (rows, depth), 0)
            ends = xw[AHEAD + 2].astype(F32)
            before, behind = p_now[far, pl.ds(ROW0 - 1, 1), :], p_now[far, pl.ds(ROW0 + rows, 1), :]
            for i, buf in enumerate((p_old, q_old)):
                value = xw[AHEAD + i].astype(F32) - buf[far, main, :]
                value += jnp.where(row == 0, ends[2 * i : 2 * i + 1] * before, 0.0)
                value += jnp.where(row == rows - 1, ends[2 * i + 1 : 2 * i + 2] * behind, 0.0)
                outer[i] = value
        p_rims[k] = p_now[pl.ds(DEEP + core * HMAX, HMAX), ROW0 : ROW0 + rows, :]
        step(k, p_now, q_now, p_old, q_old)
        if k == 0:
            for i, buf in enumerate((p_old, q_old)):
                buf[far, main, :] = outer[i]
            wait_all(mains)
        for lag in range(2):
            add_image(k, p_now, lag)
        p_now, p_old, q_now, q_old = p_old, p_now, q_old, q_now


def wave(ints, data, halos, own, other, earlier, bufs):
    width, rows, depth = own.shape[1:]
    half = width // 2
    any_space = pl.BlockSpec(memory_space=pl.ANY)
    return pl.pallas_call(
        wave_kernel,
        out_shape=(
            *(pltpu.VMEM((half, rows, depth), F32),) * 4,
            pltpu.VMEM((NT, HMAX, rows, depth), F32),
        )
        + tuple(pltpu.VMEM(b.shape, F32) for b in bufs),
        in_specs=[any_space] * 2 + [VMEM] * 5 + [HBM] + [any_space] * 2 + [VMEM] * 8,
        out_specs=(VMEM,) * 13,
        input_output_aliases={10 + i: 5 + i for i in range(8)},
        scratch_shapes=[
            pltpu.SMEM(ints.shape, jnp.int32),
            pltpu.SMEM(data.shape, F32),
            pltpu.VMEM((half + 2 * DEEP, 16, depth), F32),
            pltpu.VMEM((NT, half + HMAX, rows, depth), BF16),
            pltpu.VMEM((8, rows + 2 * HMAX, depth), F32),
            pltpu.VMEM((2, rows, depth), F32),
            pltpu.SemaphoreType.DMA((4,)),
        ],
        compiler_params=params(8),
        name="wave",
    )(ints, data, *pin(halos, pltpu.VMEM), *pin((own,)), other, earlier, *pin(bufs, pltpu.VMEM))[:5]


def merge_kernel(*refs):
    halves, outs, sems = refs[:6], refs[6:9], refs[9]
    core = lax.axis_index("mem")
    half = outs[0].shape[0] // 2
    pairs = []
    for i, out in enumerate(outs):
        pairs.append((halves[2 * i], out.at[pl.ds(half * core, half)]))
        pairs.append((halves[2 * i + 1], out.at[pl.ds(half - half * core, half)]))
    wait_all(copy_all(pairs, sems))


def merge(p, p_other, q, q_other, total, image_other):
    block = jax.ShapeDtypeStruct((2 * p.shape[0],) + p.shape[1:], F32)
    return pl.pallas_call(
        merge_kernel,
        out_shape=(block,) * 3,
        in_specs=[VMEM] * 6,
        out_specs=(HBM,) * 3,
        scratch_shapes=[pltpu.SemaphoreType.DMA((6,))],
        compiler_params=params(8),
        name="merge",
    )(*pin((p, p_other, q, q_other, total, image_other), pltpu.VMEM))


def rim_kernel(offs, offs_other, xs, same, cross, p_rims, _, total, given, wide):
    core = lax.axis_index("mem")
    half, rows, _ = total.shape
    for lag, off in enumerate((offs, offs_other)):
        off_x, off_y = off[0, 0], off[0, 1]
        layers = jnp.maximum(jnp.where(core == 0, off_x, -off_x), 0)
        from_same = core == jnp.where(off_y > 0, 0, 1)

        def layer(i, lag=lag, off_y=off_y, layers=layers, from_same=from_same):
            at = jnp.where(core == 0, HMAX - layers + i, i)
            mine = jnp.where(core == 0, i, HMAX - layers + i)
            result = None
            for pair in range(2):
                place = 2 * DEEP + pair * HMAX + at
                strip = jnp.where(from_same, same[place].astype(F32), cross[place].astype(F32))
                for part in range(2):
                    t = 2 * pair + part
                    rim = strip[8 * part : 8 * part + 8]
                    wide[t, HMAX : HMAX + rows, :] = xs[t, at].astype(F32)
                    wide[t, 0:HMAX, :] = rim
                    wide[t, HMAX + rows :, :] = rim
                    term = wide[t, pl.ds(HMAX - off_y, rows), :] * p_rims[NT - 1 - t, mine]
                    result = term if result is None else result + term
            if lag == 1:
                given[i] = result
            else:
                total[jnp.where(core == 0, i, half - layers + i)] = result

        for i in range(HMAX):
            pl.when(i < layers)(lambda i=i, layer=layer: layer(i))


def rim_image(offs, offs_other, halos, p_rims, total):
    half, rows, depth = total.shape
    return pl.pallas_call(
        rim_kernel,
        out_shape=(
            pltpu.VMEM(total.shape, F32),
            pltpu.VMEM((HMAX, rows, depth), F32),
        ),
        in_specs=[SMEM] * 2 + [VMEM] * 5,
        out_specs=(VMEM, VMEM),
        input_output_aliases={6: 0},
        scratch_shapes=[pltpu.VMEM((NT, rows + 2 * HMAX, depth), F32)],
        compiler_params=params(8),
        name="rim_image",
    )(offs, offs_other, *pin((*halos, p_rims, total), pltpu.VMEM))


def place_kernel(offs, given, _, image, sem_out):
    core = lax.axis_index("mem")
    width = image.shape[0]
    layers = jnp.maximum(jnp.where(core == 0, -offs[0, 0], offs[0, 0]), 0)

    def out_copy(i):
        x = jnp.where(core == 0, width - layers + i, i)
        return pltpu.make_async_copy(given.at[i], image.at[x], sem_out.at[i])

    for i in range(HMAX):
        pl.when(i < layers)(lambda i=i: out_copy(i).start())
    for i in range(HMAX):
        pl.when(i < layers)(lambda i=i: out_copy(i).wait())


def place_rim(offs, given, image):
    return pl.pallas_call(
        place_kernel,
        out_shape=jax.ShapeDtypeStruct(image.shape, F32),
        in_specs=[SMEM, VMEM, HBM],
        out_specs=HBM,
        input_output_aliases={2: 0},
        scratch_shapes=[pltpu.SemaphoreType.DMA((HMAX,))],
        compiler_params=params(8),
        name="place_rim",
    )(offs, *pin((given,), pltpu.VMEM), *pin((image,)))


def body(
    src_hist, rec_p, rec_q, prev_p, prev_q, horiz, vert, ratio, tilt, rec_pos, rec_data, lag_offs
):
    width, rows, depth = rec_p.shape
    fields = (rec_p, rec_q, prev_p, prev_q, horiz, vert, ratio, tilt)

    def swap(v):
        return lax.ppermute(v, "mem", [(0, 1), (1, 0)])

    def after(v, earlier):
        return lax.optimization_barrier((v, earlier))[0]

    def outward(v, step_x, step_y):
        count_x, count_y = lax.axis_size("gx"), lax.axis_size("gy")
        pairs = []
        for x in range(count_x):
            for y in range(count_y):
                for core, sign in ((0, 1), (1, -1)):
                    to_x, to_y = x + sign * step_x, y + sign * step_y
                    if 0 <= to_x < count_x and 0 <= to_y < count_y:
                        pairs.append(((x * count_y + y) * 2 + core, (to_x * count_y + to_y) * 2 + core))
        return lax.ppermute(v, ("gx", "gy", "mem"), pairs)

    plane = rows * lax.axis_size("gy") * depth
    half = width // 2
    x = rec_pos // plane - lax.axis_index("gx") * width - lax.axis_index("mem") * half + DEEP
    rest = rec_pos % plane
    y = rest // depth - lax.axis_index("gy") * rows + ROW0
    z = rest % depth
    inside = (x >= 0) & (x < half + 2 * DEEP)
    inside &= (y >= ROW0 - DEEP) & (y < ROW0 + rows + DEEP)
    target = jnp.where(inside, (x << 16) + (y << 8) + z, -1)
    offs_other = swap(lag_offs)
    target = jnp.concatenate([target, lag_offs[0], offs_other[0]])

    other = swap(src_hist)
    packed = pack_x(fields)
    xw = outward(packed, 1, 0)
    ys, same, cross, xs = pack_rest(fields, src_hist, after(other, packed))
    ys, same, cross = outward(ys, 0, 1), outward(same, 1, 1), outward(cross, 1, -1)
    *bufs, ints = load(fields, after(target, packed))
    xs = outward(after(xs, (same, cross)), 1, 0)
    halos = (xw, ys, swap(ys), same, cross)
    token = swap(xw[0, :16])
    p, q, total, total_other, p_rims = wave(ints, rec_data, halos, src_hist, other, token, bufs)
    parts = (swap(p), swap(q), swap(total_other))
    total, given = rim_image(lag_offs, offs_other, (after(xs, p), same, cross), p_rims, total)
    p, q, image = merge(p, parts[0], q, parts[1], total, parts[2])
    image = place_rim(lag_offs, swap(given), image)
    return image[None], p, q


def solution(mesh):
    block = P("gx", "gy", None)
    return jax.shard_map(
        body,
        mesh=mesh,
        in_specs=(P("mem", "gx", "gy", None),) + (block,) * 8 + (P(), P(), P("mem", None)),
        out_specs=(P("mem", "gx", "gy", None), block, block),
        check_vma=False,
    )
```

```python
import functools

import jax
import jax.numpy as jnp
from jax import lax
from jax.experimental import pallas as pl
from jax.experimental.pallas import tpu as pltpu
from jax.sharding import PartitionSpec as P

NT = 4
HMAX = 8
DEEP = NT
ROW0 = 16
GROUP = 4
HEAD = 8
F32 = jnp.float32
BF16 = jnp.bfloat16
HBM = pl.BlockSpec(memory_space=pltpu.HBM)
SMEM = pl.BlockSpec(memory_space=pltpu.SMEM)
VMEM = pl.BlockSpec(memory_space=pltpu.VMEM)
DEPTHS = (DEEP, DEEP) + (DEEP - 1,) * 6
STARTS = tuple(sum(DEPTHS[:i]) for i in range(8))
SENT = tuple(d - 1 for d in DEPTHS)
SENT_AT = tuple(sum(SENT[:i]) for i in range(8))
AHEAD = sum(SENT)
LAYERS = AHEAD + 3


def pin(arrays, space=pltpu.HBM):
    return [pltpu.with_memory_space_constraint(a, space) for a in arrays]


def params(mib=63):
    return pltpu.CompilerParams(vmem_limit_bytes=mib * 2**20)


def copy_all(pairs, sems):
    copies = [pltpu.make_async_copy(a, b, sems.at[i]) for i, (a, b) in enumerate(pairs)]
    for c in copies:
        c.start()
    return copies


def wait_all(copies):
    for c in copies:
        c.wait()


def slopes(v):
    depth = v.shape[-1]
    lane = lax.broadcasted_iota(jnp.int32, v.shape, 1)
    up = jnp.where(lane == depth - 1, 0.0, pltpu.roll(v, depth - 1, 1))
    down = jnp.where(lane == 0, 0.0, pltpu.roll(v, 1, 1))
    return up + down, up - down


def pack_x_kernel(*refs):
    fields, small, stage, sems = refs[:8], *refs[8:]
    core = lax.axis_index("mem")
    width, rows, _ = fields[0].shape
    pairs = []
    for f, s, d in zip(fields, STARTS, DEPTHS):
        begin = jnp.where(core == 0, width - d, 0)
        pairs.append((f.at[pl.ds(begin, d)], stage.at[pl.ds(s, d)]))
    copies = copy_all(pairs, sems)
    for i in range(8):
        copies[i].wait()
        small[SENT_AT[i] : SENT_AT[i] + SENT[i]] = stage[pl.ds(STARTS[i] + 1 - core, SENT[i])].astype(BF16)
    at = [s + (1 + core if i < 2 else 2 * core) for i, s in enumerate(STARTS)]
    p, q, old_p, old_q, horiz, vert, ratio, tilt = [stage[j] for j in at]
    row = lax.broadcasted_iota(jnp.int32, p.shape, 0)
    beside = jnp.where(row == 0, 0.0, pltpu.roll(p, 1, 0))
    beside += jnp.where(row == rows - 1, 0.0, pltpu.roll(p, rows - 1, 0))
    lateral = stage[at[0] - 1] + stage[at[0] + 1] + beside - 4.0 * p
    mixed = slopes(stage[at[1] + 1])[1] - slopes(stage[at[1] - 1])[1]
    horizontal = horiz * lateral
    upright = vert * ((slopes(q)[0] - 2.0 * q) + (0.25 * tilt) * mixed)
    small[AHEAD] = ((2.0 * p - old_p) + (horizontal + upright)).astype(BF16)
    small[AHEAD + 1] = ((2.0 * q - old_q) + (ratio * horizontal + upright)).astype(BF16)
    both = ratio * horiz
    ends = jnp.where(row == 0, horiz[:1], jnp.where(row == 1, horiz[rows - 1 :], 0.0))
    ends = jnp.where(row == 2, both[:1], jnp.where(row == 3, both[rows - 1 :], ends))
    small[AHEAD + 2] = ends.astype(BF16)


def pack_x(fields):
    shape = fields[0].shape[1:]
    return pl.pallas_call(
        pack_x_kernel,
        out_shape=pltpu.VMEM((LAYERS,) + shape, BF16),
        in_specs=[HBM] * 8,
        out_specs=VMEM,
        scratch_shapes=[
            pltpu.VMEM((sum(DEPTHS),) + shape, F32),
            pltpu.SemaphoreType.DMA((8,)),
        ],
        compiler_params=params(16),
        name="pack_x",
    )(*pin(fields))


def pack_rest_kernel(*refs):
    fields, own, other = refs[:8], *refs[8:10]
    s_ys, s_same, s_cross, edges = refs[10:14]
    stage, snaps, stage_c, snaps_c, mixed, sems = refs[14:]
    core = lax.axis_index("mem")
    width, rows, _ = fields[0].shape
    near, far = width - DEEP, width - HMAX
    to_low = core == 1
    x_near, x_far = jnp.where(to_low, 0, near), jnp.where(to_low, 0, far)

    def y_at(low, size):
        return pl.multiple_of(jnp.where(low, 0, rows - size), size)

    pairs = []
    for i, f in enumerate(fields):
        pairs.append((f.at[:, pl.ds(y_at(to_low, 8), 8)], stage.at[i]))
        pairs.append((f.at[pl.ds(x_near, DEEP), pl.ds(y_at(~to_low, 8), 8)], stage_c.at[i]))
    for ref, half in ((own, core), (other, 1 - core)):
        pairs.append((ref.at[:, :, pl.ds(y_at(to_low, 16), 16)], snaps.at[half]))
        rim = ref.at[:, pl.ds(x_far, HMAX), pl.ds(y_at(~to_low, 16), 16)]
        pairs.append((rim, snaps_c.at[half]))
        pairs.append((ref.at[:, pl.ds(x_far, HMAX)], edges.at[pl.ds(2 * half, 2)]))
    copies = copy_all(pairs, sems)
    wait_all(copies[:16])
    skip, skip_c = jnp.where(to_low, 0, 4), jnp.where(to_low, 4, 0)
    for slab in range(2):
        for i in range(4):
            at = pl.ds(4 * i, 4)
            mixed[:width, at, :] = stage[4 * slab + i, :, pl.ds(skip, 4), :]
            mixed[width : width + DEEP, at, :] = stage_c[4 * slab + i, :, pl.ds(skip_c, 4), :]
        s_ys[slab] = mixed[:width].astype(BF16)
        s_cross[slab * DEEP : (slab + 1) * DEEP] = mixed[width : width + DEEP].astype(BF16)
    wait_all(copies[16:])
    for pair in range(2):
        for i in range(2):
            at = slice(8 * i, 8 * i + 8)
            both = snaps[pair, i].astype(F32)
            mixed[:width, at, :] = jnp.where(to_low, both[:, :8], both[:, 8:])
            both = snaps_c[pair, i].astype(F32)
            mixed[width : width + HMAX, at, :] = jnp.where(to_low, both[:, 8:], both[:, :8])
        s_ys[2 + pair] = mixed[:width].astype(BF16)
        begin = 2 * DEEP + pair * HMAX
        s_cross[begin : begin + HMAX] = mixed[width : width + HMAX].astype(BF16)
    for slab in range(2):
        begin = slab * DEEP
        s_same[begin : begin + DEEP] = s_ys[slab, pl.ds(x_near, DEEP)]
        begin = 2 * DEEP + slab * HMAX
        s_same[begin : begin + HMAX] = s_ys[2 + slab, pl.ds(x_far, HMAX)]


def pack_rest(fields, own, other):
    width, rows, depth = fields[0].shape
    corner = (2 * DEEP + 2 * HMAX, 16, depth)
    return pl.pallas_call(
        pack_rest_kernel,
        out_shape=(
            pltpu.VMEM((4, width, 16, depth), BF16),
            pltpu.VMEM(corner, BF16),
            pltpu.VMEM(corner, BF16),
            pltpu.VMEM((NT, HMAX, rows, depth), BF16),
        ),
        in_specs=[HBM] * 9 + [pl.BlockSpec(memory_space=pl.ANY)],
        out_specs=(VMEM,) * 4,
        scratch_shapes=[
            pltpu.VMEM((8, width, 8, depth), F32),
            pltpu.VMEM((2, 2, width, 16, depth), BF16),
            pltpu.VMEM((8, DEEP, 8, depth), F32),
            pltpu.VMEM((2, 2, HMAX, 16, depth), BF16),
            pltpu.VMEM((width + HMAX, 16, depth), F32),
            pltpu.SemaphoreType.DMA((22,)),
        ],
        compiler_params=params(16),
        name="pack_rest",
    )(*pin((*fields, own)), other)


def load_kernel(target, *refs):
    fields, bufs, (ints, listed, s_target, sems, sem_target, sem_ints) = refs[:8], refs[-14:-6], refs[-6:]
    core = lax.axis_index("mem")
    n = target.shape[0] - 4
    fetch = pltpu.make_async_copy(target, s_target, sem_target)
    fetch.start()
    width, rows, _ = fields[0].shape
    inner = width // 2 + DEEP
    pairs = []
    for f, b in zip(fields, bufs):
        to = b.at[pl.ds(DEEP * (1 - core), inner), pl.ds(ROW0, rows)]
        pairs.append((f.at[pl.ds((width - inner) * core, inner)], to))
    copies = copy_all(pairs, sems)
    fetch.wait()

    def one(r, at):
        place = s_target[r]
        listed[at] = r
        listed[at + n + GROUP] = place
        return at + jnp.where(place >= 0, 1, 0)

    end = lax.fori_loop(0, n, one, jnp.int32(HEAD), unroll=16)
    for i in range(GROUP):
        listed[end + i] = 0
        listed[end + i + n + GROUP] = 0
    listed[0] = (end - HEAD + GROUP - 1) // GROUP
    for i in range(4):
        listed[1 + i] = s_target[n + i]
    save = pltpu.make_async_copy(listed, ints, sem_ints)
    save.start()
    wait_all(copies + [save])


def load(fields, target):
    width, rows, depth = fields[0].shape
    any_space = pl.BlockSpec(memory_space=pl.ANY)
    n = target.shape[0] - 4
    listed = (HEAD + 2 * (n + GROUP),)
    shape = (width // 2 + 2 * DEEP, rows + 2 * ROW0, depth)
    return pl.pallas_call(
        load_kernel,
        out_shape=(pltpu.VMEM(shape, F32),) * 8 + (jax.ShapeDtypeStruct(listed, jnp.int32),),
        in_specs=[any_space] + [HBM] * 8,
        out_specs=(VMEM,) * 8 + (any_space,),
        scratch_shapes=[
            pltpu.SMEM(listed, jnp.int32),
            pltpu.SMEM((n + 4,), jnp.int32),
            pltpu.SemaphoreType.DMA((8,)),
            pltpu.SemaphoreType.DMA,
            pltpu.SemaphoreType.DMA,
        ],
        compiler_params=params(8),
        name="load",
    )(target, *pin(fields))


def wave_kernel(ints, amounts, *refs):
    xw, y_own, y_other, same, cross, own, other = refs[:7]
    p_out, q_out, *totals, p_rims = refs[16:21]
    bufs = refs[21:29]
    listed, data, stage, snaps, wide, outer, sem_in = refs[29:]
    core = lax.axis_index("mem")
    half, rows, depth = p_out.shape
    lists = copy_all([(ints, listed), (amounts, data)], sem_in)
    near = pl.ds(core * HMAX, half + HMAX)
    mains = copy_all(
        [
            (own.at[:, near], snaps.at[pl.ds(2 * core, 2)]),
            (other.at[:, near], snaps.at[pl.ds(2 - 2 * core, 2)]),
        ],
        sem_in.at[pl.ds(2, 2)],
    )
    face = core * (half + DEEP)
    inner = half + DEEP
    for f in range(8):
        d = SENT[f]
        to = jnp.where(core == 0, DEEP - d, half + DEEP)
        part = xw[SENT_AT[f] : SENT_AT[f] + d]
        bufs[f][pl.ds(to, d), ROW0 : ROW0 + rows, :] = part.astype(F32)
    for ys, corner, side in ((y_own, same, core), (y_other, cross, 1 - core)):
        to = jnp.where(side == 0, ROW0 - DEEP, ROW0 + rows)
        for slab in range(2):
            part = ys[slab, pl.ds(core * (half - DEEP), inner)]
            stage[pl.ds(DEEP * (1 - core), inner)] = part.astype(F32)
            part = corner[slab * DEEP : slab * DEEP + DEEP]
            stage[pl.ds(face, DEEP)] = part.astype(F32)
            for i in range(4):
                bufs[4 * slab + i][:, pl.ds(to, DEEP), :] = stage[:, 4 * i : 4 * i + 4, :]

    wait_all(lists)
    horiz, vert, ratio, tilt = bufs[4:]
    thin = lax.broadcasted_iota(jnp.int32, (1, depth), 1)

    def step(k, p, q, old_p, old_q):
        low, high = 1 + k, half + 2 * DEEP - 1 - k
        begin, end = (ROW0 - 8, ROW0 + rows + 8) if k < NT - 1 else (ROW0, ROW0 + rows)
        size = 48 if (end - begin) % 48 == 0 else 64 if (end - begin) % 64 == 0 else 8

        def strip(i, _):
            r = pl.multiple_of(begin + i * size, 8)
            at = pl.ds(r, size)
            p_m, p_c, q_c = p[low - 1, at, :], p[low, at, :], q[low, at, :]
            _, d_m = slopes(q[low - 1, at, :])
            s_c, d_c = slopes(q_c)
            for x in range(low, high):
                p_n, q_n = p[x + 1, at, :], q[x + 1, at, :]
                s_n, d_n = slopes(q_n)
                beside = p[x, pl.ds(r - 1, size), :] + p[x, pl.ds(r + 1, size), :]
                lateral = ((p_m + p_n) + beside) - 4.0 * p_c
                q_2 = 2.0 * q_c
                horizontal = horiz[x, at, :] * lateral
                mixed = (0.25 * tilt[x, at, :]) * (d_n - d_m)
                upright = vert[x, at, :] * ((s_c - q_2) + mixed)
                p_new = (2.0 * p_c - old_p[x, at, :]) + (horizontal + upright)
                q_new = (q_2 - old_q[x, at, :]) + (ratio[x, at, :] * horizontal + upright)
                if k < NT - 1:
                    old_p[x, at, :] = p_new
                    old_q[x, at, :] = q_new
                else:
                    out_at = pl.ds(pl.multiple_of(r - ROW0, 8), size)
                    p_out[x - DEEP, out_at, :] = p_new
                    q_out[x - DEEP, out_at, :] = q_new
                p_m, p_c, q_c, s_c, d_m, d_c = p_c, p_n, q_n, s_n, d_c, d_n
            return 0

        lax.fori_loop(0, (end - begin) // size, strip, 0)

    def inject(k, old_p, old_q):
        def group(g, _):
            for i in range(GROUP):
                j = HEAD + g * GROUP + i
                place = listed[j + (listed.shape[0] - HEAD) // 2]
                amount = data[NT - 1 - k, listed[j]]
                x, y, z = place >> 16, (place >> 8) & 255, place & 255
                add = jnp.where(thin == z, amount, 0.0)
                old_p[x, pl.ds(y, 1), :] = old_p[x, pl.ds(y, 1), :] - add
                old_q[x, pl.ds(y, 1), :] = old_q[x, pl.ds(y, 1), :] - add
            return 0

        lax.fori_loop(0, listed[0], group, 0)

    def add_image(k, p, lag):
        off_x, off_y = listed[1 + 2 * lag], listed[2 + 2 * lag]
        t = NT - 1 - k
        pair, part = t // 2, t % 2
        from_own = core == jnp.where(off_y > 0, 0, 1)

        def layer(i, _):
            at = jnp.clip(core * HMAX + i - off_x, 0, half + HMAX - 1)
            slot = i % 8
            mine, others = y_own[2 + pair, core * HMAX + at], y_other[2 + pair, core * HMAX + at]
            rim = jnp.where(from_own, mine.astype(F32), others.astype(F32))
            rim = rim[8 * part : 8 * part + 8]
            wide[slot, HMAX : HMAX + rows, :] = snaps[t, at].astype(F32)
            wide[slot, 0:HMAX, :] = rim
            wide[slot, HMAX + rows :, :] = rim
            term = wide[slot, pl.ds(HMAX - off_y, rows), :] * p[i + DEEP, ROW0 : ROW0 + rows, :]
            totals[lag][i] = term if k == 0 else totals[lag][i] + term
            return 0

        lax.fori_loop(0, half, layer, 0, unroll=8)

    p_now, q_now, p_old, q_old = bufs[:4]
    main = slice(ROW0, ROW0 + rows)
    far = jnp.where(core == 0, DEEP - 3, half + DEEP + 2)
    for buf in (p_old, q_old):
        buf[far, main, :] = jnp.zeros((rows, depth), F32)
    for k in range(NT):
        inject(k, p_old, q_old)
        if k == 0:
            row = lax.broadcasted_iota(jnp.int32, (rows, depth), 0)
            ends = xw[AHEAD + 2].astype(F32)
            before, behind = p_now[far, pl.ds(ROW0 - 1, 1), :], p_now[far, pl.ds(ROW0 + rows, 1), :]
            for i, buf in enumerate((p_old, q_old)):
                value = xw[AHEAD + i].astype(F32) - buf[far, main, :]
                value += jnp.where(row == 0, ends[2 * i : 2 * i + 1] * before, 0.0)
                value += jnp.where(row == rows - 1, ends[2 * i + 1 : 2 * i + 2] * behind, 0.0)
                outer[i] = value
        p_rims[k] = p_now[pl.ds(DEEP + core * HMAX, HMAX), ROW0 : ROW0 + rows, :]
        step(k, p_now, q_now, p_old, q_old)
        if k == 0:
            for i, buf in enumerate((p_old, q_old)):
                buf[far, main, :] = outer[i]
            wait_all(mains)
        for lag in range(2):
            add_image(k, p_now, lag)
        p_now, p_old, q_now, q_old = p_old, p_now, q_old, q_now


def wave(ints, data, halos, own, other, earlier, bufs):
    width, rows, depth = own.shape[1:]
    half = width // 2
    any_space = pl.BlockSpec(memory_space=pl.ANY)
    return pl.pallas_call(
        wave_kernel,
        out_shape=(
            *(pltpu.VMEM((half, rows, depth), F32),) * 4,
            pltpu.VMEM((NT, HMAX, rows, depth), F32),
        )
        + tuple(pltpu.VMEM(b.shape, F32) for b in bufs),
        in_specs=[any_space] * 2 + [VMEM] * 5 + [HBM] + [any_space] * 2 + [VMEM] * 8,
        out_specs=(VMEM,) * 13,
        input_output_aliases={10 + i: 5 + i for i in range(8)},
        scratch_shapes=[
            pltpu.SMEM(ints.shape, jnp.int32),
            pltpu.SMEM(data.shape, F32),
            pltpu.VMEM((half + 2 * DEEP, 16, depth), F32),
            pltpu.VMEM((NT, half + HMAX, rows, depth), BF16),
            pltpu.VMEM((8, rows + 2 * HMAX, depth), F32),
            pltpu.VMEM((2, rows, depth), F32),
            pltpu.SemaphoreType.DMA((4,)),
        ],
        compiler_params=params(8),
        name="wave",
    )(ints, data, *pin(halos, pltpu.VMEM), *pin((own,)), other, earlier, *pin(bufs, pltpu.VMEM))[:5]


def merge_kernel(n, *refs):
    halves, outs, sems = refs[: 2 * n], refs[-n - 1 : -1], refs[-1]
    core = lax.axis_index("mem")
    half = halves[0].shape[0]
    pairs = []
    for i, out in enumerate(outs):
        pairs.append((halves[2 * i], out.at[pl.ds(half * core, half)]))
        pairs.append((halves[2 * i + 1], out.at[pl.ds(half - half * core, half)]))
    wait_all(copy_all(pairs, sems))


def merge(halves, earlier, name):
    n = len(halves) // 2
    block = jax.ShapeDtypeStruct((2 * halves[0].shape[0],) + halves[0].shape[1:], F32)
    return pl.pallas_call(
        functools.partial(merge_kernel, n),
        out_shape=(block,) * n,
        in_specs=[VMEM] * 2 * n + [pl.BlockSpec(memory_space=pl.ANY)] * len(earlier),
        out_specs=(HBM,) * n,
        scratch_shapes=[pltpu.SemaphoreType.DMA((2 * n,))],
        compiler_params=params(8),
        name=name,
    )(*pin(halves, pltpu.VMEM), *earlier)


def rim_kernel(offs, offs_other, xs, same, cross, p_rims, _, total, given, wide):
    core = lax.axis_index("mem")
    half, rows, _ = total.shape
    for lag, off in enumerate((offs, offs_other)):
        off_x, off_y = off[0, 0], off[0, 1]
        layers = jnp.maximum(jnp.where(core == 0, off_x, -off_x), 0)
        from_same = core == jnp.where(off_y > 0, 0, 1)

        def layer(i, lag=lag, off_y=off_y, layers=layers, from_same=from_same):
            at = jnp.where(core == 0, HMAX - layers + i, i)
            mine = jnp.where(core == 0, i, HMAX - layers + i)
            result = None
            for pair in range(2):
                place = 2 * DEEP + pair * HMAX + at
                strip = jnp.where(from_same, same[place].astype(F32), cross[place].astype(F32))
                for part in range(2):
                    t = 2 * pair + part
                    rim = strip[8 * part : 8 * part + 8]
                    wide[t, HMAX : HMAX + rows, :] = xs[t, at].astype(F32)
                    wide[t, 0:HMAX, :] = rim
                    wide[t, HMAX + rows :, :] = rim
                    term = wide[t, pl.ds(HMAX - off_y, rows), :] * p_rims[NT - 1 - t, mine]
                    result = term if result is None else result + term
            if lag == 1:
                given[i] = result
            else:
                total[jnp.where(core == 0, i, half - layers + i)] = result

        for i in range(HMAX):
            pl.when(i < layers)(lambda i=i, layer=layer: layer(i))


def rim_image(offs, offs_other, halos, p_rims, total):
    half, rows, depth = total.shape
    return pl.pallas_call(
        rim_kernel,
        out_shape=(
            pltpu.VMEM(total.shape, F32),
            pltpu.VMEM((HMAX, rows, depth), F32),
        ),
        in_specs=[SMEM] * 2 + [VMEM] * 5,
        out_specs=(VMEM, VMEM),
        input_output_aliases={6: 0},
        scratch_shapes=[pltpu.VMEM((NT, rows + 2 * HMAX, depth), F32)],
        compiler_params=params(8),
        name="rim_image",
    )(offs, offs_other, *pin((*halos, p_rims, total), pltpu.VMEM))


def place_kernel(offs, given, _, image, sem_out):
    core = lax.axis_index("mem")
    width = image.shape[0]
    layers = jnp.maximum(jnp.where(core == 0, -offs[0, 0], offs[0, 0]), 0)

    def out_copy(i):
        x = jnp.where(core == 0, width - layers + i, i)
        return pltpu.make_async_copy(given.at[i], image.at[x], sem_out.at[i])

    for i in range(HMAX):
        pl.when(i < layers)(lambda i=i: out_copy(i).start())
    for i in range(HMAX):
        pl.when(i < layers)(lambda i=i: out_copy(i).wait())


def place_rim(offs, given, image):
    return pl.pallas_call(
        place_kernel,
        out_shape=jax.ShapeDtypeStruct(image.shape, F32),
        in_specs=[SMEM, VMEM, HBM],
        out_specs=HBM,
        input_output_aliases={2: 0},
        scratch_shapes=[pltpu.SemaphoreType.DMA((HMAX,))],
        compiler_params=params(8),
        name="place_rim",
    )(offs, *pin((given,), pltpu.VMEM), *pin((image,)))


def body(
    src_hist, rec_p, rec_q, prev_p, prev_q, horiz, vert, ratio, tilt, rec_pos, rec_data, lag_offs
):
    width, rows, depth = rec_p.shape
    fields = (rec_p, rec_q, prev_p, prev_q, horiz, vert, ratio, tilt)

    def swap(v):
        return lax.ppermute(v, "mem", [(0, 1), (1, 0)])

    def after(v, earlier):
        return lax.optimization_barrier((v, earlier))[0]

    def outward(v, step_x, step_y):
        count_x, count_y = lax.axis_size("gx"), lax.axis_size("gy")
        pairs = []
        for x in range(count_x):
            for y in range(count_y):
                for core, sign in ((0, 1), (1, -1)):
                    to_x, to_y = x + sign * step_x, y + sign * step_y
                    if 0 <= to_x < count_x and 0 <= to_y < count_y:
                        pairs.append(((x * count_y + y) * 2 + core, (to_x * count_y + to_y) * 2 + core))
        return lax.ppermute(v, ("gx", "gy", "mem"), pairs)

    plane = rows * lax.axis_size("gy") * depth
    half = width // 2
    x = rec_pos // plane - lax.axis_index("gx") * width - lax.axis_index("mem") * half + DEEP
    rest = rec_pos % plane
    y = rest // depth - lax.axis_index("gy") * rows + ROW0
    z = rest % depth
    inside = (x >= 0) & (x < half + 2 * DEEP)
    inside &= (y >= ROW0 - DEEP) & (y < ROW0 + rows + DEEP)
    target = jnp.where(inside, (x << 16) + (y << 8) + z, -1)
    offs_other = swap(lag_offs)
    target = jnp.concatenate([target, lag_offs[0], offs_other[0]])

    other = swap(src_hist)
    packed = pack_x(fields)
    xw = outward(packed, 1, 0)
    ys, same, cross, xs = pack_rest(fields, src_hist, after(other, packed))
    ys, same, cross = outward(ys, 0, 1), outward(same, 1, 1), outward(cross, 1, -1)
    *bufs, ints = load(fields, after(target, packed))
    xs = outward(after(xs, (same, cross)), 1, 0)
    halos = (xw, ys, swap(ys), same, cross)
    token = swap(xw[0, :16])
    p, q, total, total_other, p_rims = wave(ints, rec_data, halos, src_hist, other, token, bufs)
    parts = (swap(p), swap(q), swap(total_other))
    total, given = rim_image(lag_offs, offs_other, (after(xs, p), same, cross), p_rims, total)
    p, q = merge((p, parts[0], q, parts[1]), (given,), "merge_fields")
    (image,) = merge((total, parts[2]), pin((p,)), "merge_image")
    image = place_rim(lag_offs, swap(given), image)
    return image[None], p, q


def solution(mesh):
    block = P("gx", "gy", None)
    return jax.shard_map(
        body,
        mesh=mesh,
        in_specs=(P("mem", "gx", "gy", None),) + (block,) * 8 + (P(), P(), P("mem", None)),
        out_specs=(P("mem", "gx", "gy", None), block, block),
        check_vma=False,
    )
```

```python
import functools

import jax
import jax.numpy as jnp
from jax import lax
from jax.experimental import pallas as pl
from jax.experimental.pallas import tpu as pltpu
from jax.sharding import PartitionSpec as P

NT = 4
HMAX = 8
DEEP = NT
ROW0 = 16
GROUP = 4
CORNER = (DEEP - 1, DEEP - 2)
HEAD = 8
F32 = jnp.float32
BF16 = jnp.bfloat16
HBM = pl.BlockSpec(memory_space=pltpu.HBM)
SMEM = pl.BlockSpec(memory_space=pltpu.SMEM)
VMEM = pl.BlockSpec(memory_space=pltpu.VMEM)
DEPTHS = (DEEP, DEEP) + (DEEP - 1,) * 6
STARTS = tuple(sum(DEPTHS[:i]) for i in range(8))
SENT = tuple(d - 1 for d in DEPTHS)
SENT_AT = tuple(sum(SENT[:i]) for i in range(8))
AHEAD = sum(SENT)
LAYERS = AHEAD + 3


def pin(arrays, space=pltpu.HBM):
    return [pltpu.with_memory_space_constraint(a, space) for a in arrays]


def params(mib=63):
    return pltpu.CompilerParams(vmem_limit_bytes=mib * 2**20)


def copy_all(pairs, sems):
    copies = [pltpu.make_async_copy(a, b, sems.at[i]) for i, (a, b) in enumerate(pairs)]
    for c in copies:
        c.start()
    return copies


def wait_all(copies):
    for c in copies:
        c.wait()


def slopes(v):
    depth = v.shape[-1]
    lane = lax.broadcasted_iota(jnp.int32, v.shape, 1)
    up = jnp.where(lane == depth - 1, 0.0, pltpu.roll(v, depth - 1, 1))
    down = jnp.where(lane == 0, 0.0, pltpu.roll(v, 1, 1))
    return up + down, up - down


def pack_x_kernel(*refs):
    fields, small, stage, sems = refs[:8], *refs[8:]
    core = lax.axis_index("mem")
    width, rows, _ = fields[0].shape
    pairs = []
    for f, s, d in zip(fields, STARTS, DEPTHS):
        begin = jnp.where(core == 0, width - d, 0)
        pairs.append((f.at[pl.ds(begin, d)], stage.at[pl.ds(s, d)]))
    copies = copy_all(pairs, sems)
    for i in range(8):
        copies[i].wait()
        small[SENT_AT[i] : SENT_AT[i] + SENT[i]] = stage[pl.ds(STARTS[i] + 1 - core, SENT[i])].astype(BF16)
    at = [s + (1 + core if i < 2 else 2 * core) for i, s in enumerate(STARTS)]
    p, q, old_p, old_q, horiz, vert, ratio, tilt = [stage[j] for j in at]
    row = lax.broadcasted_iota(jnp.int32, p.shape, 0)
    beside = jnp.where(row == 0, 0.0, pltpu.roll(p, 1, 0))
    beside += jnp.where(row == rows - 1, 0.0, pltpu.roll(p, rows - 1, 0))
    lateral = stage[at[0] - 1] + stage[at[0] + 1] + beside - 4.0 * p
    mixed = slopes(stage[at[1] + 1])[1] - slopes(stage[at[1] - 1])[1]
    horizontal = horiz * lateral
    upright = vert * ((slopes(q)[0] - 2.0 * q) + (0.25 * tilt) * mixed)
    small[AHEAD] = ((2.0 * p - old_p) + (horizontal + upright)).astype(BF16)
    small[AHEAD + 1] = ((2.0 * q - old_q) + (ratio * horizontal + upright)).astype(BF16)
    both = ratio * horiz
    ends = jnp.where(row == 0, horiz[:1], jnp.where(row == 1, horiz[rows - 1 :], 0.0))
    ends = jnp.where(row == 2, both[:1], jnp.where(row == 3, both[rows - 1 :], ends))
    small[AHEAD + 2] = ends.astype(BF16)


def pack_x(fields):
    shape = fields[0].shape[1:]
    return pl.pallas_call(
        pack_x_kernel,
        out_shape=pltpu.VMEM((LAYERS,) + shape, BF16),
        in_specs=[HBM] * 8,
        out_specs=VMEM,
        scratch_shapes=[
            pltpu.VMEM((sum(DEPTHS),) + shape, F32),
            pltpu.SemaphoreType.DMA((8,)),
        ],
        compiler_params=params(16),
        name="pack_x",
    )(*pin(fields))


def pack_rest_kernel(*refs):
    fields, own, other = refs[:8], *refs[8:10]
    s_ys, s_same, s_cross, edges = refs[10:14]
    stage, snaps, stage_c, snaps_c, mixed, sems = refs[14:]
    core = lax.axis_index("mem")
    width, rows, _ = fields[0].shape
    near, far = width - DEEP, width - HMAX
    to_low = core == 1
    x_near, x_far = jnp.where(to_low, 0, near), jnp.where(to_low, 0, far)

    def y_at(low, size):
        return pl.multiple_of(jnp.where(low, 0, rows - size), size)

    pairs = []
    for i, f in enumerate(fields):
        pairs.append((f.at[:, pl.ds(y_at(to_low, 8), 8)], stage.at[i]))
        pairs.append((f.at[pl.ds(x_near, DEEP), pl.ds(y_at(~to_low, 8), 8)], stage_c.at[i]))
    for ref, half in ((own, core), (other, 1 - core)):
        pairs.append((ref.at[:, :, pl.ds(y_at(to_low, 16), 16)], snaps.at[half]))
        rim = ref.at[:, pl.ds(x_far, HMAX), pl.ds(y_at(~to_low, 16), 16)]
        pairs.append((rim, snaps_c.at[half]))
        pairs.append((ref.at[:, pl.ds(x_far, HMAX)], edges.at[pl.ds(2 * half, 2)]))
    copies = copy_all(pairs, sems)
    wait_all(copies[:16])
    skip, skip_c = jnp.where(to_low, 0, 4), jnp.where(to_low, 4, 0)
    for slab in range(2):
        for i in range(4):
            at = pl.ds(4 * i, 4)
            mixed[:width, at, :] = stage[4 * slab + i, :, pl.ds(skip, 4), :]
            mixed[width : width + DEEP, at, :] = stage_c[4 * slab + i, :, pl.ds(skip_c, 4), :]
        s_ys[slab] = mixed[:width].astype(BF16)
        d, begin = CORNER[slab], slab * CORNER[0]
        part = mixed[pl.ds(width + (DEEP - d) * (1 - core), d)]
        s_cross[begin : begin + d] = part.astype(BF16)
    wait_all(copies[16:])
    for pair in range(2):
        for i in range(2):
            at = slice(8 * i, 8 * i + 8)
            both = snaps[pair, i].astype(F32)
            mixed[:width, at, :] = jnp.where(to_low, both[:, :8], both[:, 8:])
            both = snaps_c[pair, i].astype(F32)
            mixed[width : width + HMAX, at, :] = jnp.where(to_low, both[:, 8:], both[:, :8])
        s_ys[2 + pair] = mixed[:width].astype(BF16)
        begin = sum(CORNER) + pair * HMAX
        s_cross[begin : begin + HMAX] = mixed[width : width + HMAX].astype(BF16)
    for slab in range(2):
        d, begin = CORNER[slab], slab * CORNER[0]
        s_same[begin : begin + d] = s_ys[slab, pl.ds(jnp.where(to_low, 0, width - d), d)]
        begin = sum(CORNER) + slab * HMAX
        s_same[begin : begin + HMAX] = s_ys[2 + slab, pl.ds(x_far, HMAX)]


def pack_rest(fields, own, other):
    width, rows, depth = fields[0].shape
    corner = (sum(CORNER) + 2 * HMAX, 16, depth)
    return pl.pallas_call(
        pack_rest_kernel,
        out_shape=(
            pltpu.VMEM((4, width, 16, depth), BF16),
            pltpu.VMEM(corner, BF16),
            pltpu.VMEM(corner, BF16),
            pltpu.VMEM((NT, HMAX, rows, depth), BF16),
        ),
        in_specs=[HBM] * 9 + [pl.BlockSpec(memory_space=pl.ANY)],
        out_specs=(VMEM,) * 4,
        scratch_shapes=[
            pltpu.VMEM((8, width, 8, depth), F32),
            pltpu.VMEM((2, 2, width, 16, depth), BF16),
            pltpu.VMEM((8, DEEP, 8, depth), F32),
            pltpu.VMEM((2, 2, HMAX, 16, depth), BF16),
            pltpu.VMEM((width + HMAX, 16, depth), F32),
            pltpu.SemaphoreType.DMA((22,)),
        ],
        compiler_params=params(16),
        name="pack_rest",
    )(*pin((*fields, own)), other)


def load_kernel(target, *refs):
    fields, bufs, (ints, listed, s_target, sems, sem_target, sem_ints) = refs[:8], refs[-14:-6], refs[-6:]
    core = lax.axis_index("mem")
    n = target.shape[0] - 4
    fetch = pltpu.make_async_copy(target, s_target, sem_target)
    fetch.start()
    width, rows, _ = fields[0].shape
    inner = width // 2 + DEEP
    pairs = []
    for f, b in zip(fields, bufs):
        to = b.at[pl.ds(DEEP * (1 - core), inner), pl.ds(ROW0, rows)]
        pairs.append((f.at[pl.ds((width - inner) * core, inner)], to))
    copies = copy_all(pairs, sems)
    fetch.wait()

    def one(r, at):
        place = s_target[r]
        listed[at] = r
        listed[at + n + GROUP] = place
        return at + jnp.where(place >= 0, 1, 0)

    end = lax.fori_loop(0, n, one, jnp.int32(HEAD), unroll=16)
    for i in range(GROUP):
        listed[end + i] = 0
        listed[end + i + n + GROUP] = 0
    listed[0] = (end - HEAD + GROUP - 1) // GROUP
    for i in range(4):
        listed[1 + i] = s_target[n + i]
    save = pltpu.make_async_copy(listed, ints, sem_ints)
    save.start()
    wait_all(copies + [save])


def load(fields, target):
    width, rows, depth = fields[0].shape
    any_space = pl.BlockSpec(memory_space=pl.ANY)
    n = target.shape[0] - 4
    listed = (HEAD + 2 * (n + GROUP),)
    shape = (width // 2 + 2 * DEEP, rows + 2 * ROW0, depth)
    return pl.pallas_call(
        load_kernel,
        out_shape=(pltpu.VMEM(shape, F32),) * 8 + (jax.ShapeDtypeStruct(listed, jnp.int32),),
        in_specs=[any_space] + [HBM] * 8,
        out_specs=(VMEM,) * 8 + (any_space,),
        scratch_shapes=[
            pltpu.SMEM(listed, jnp.int32),
            pltpu.SMEM((n + 4,), jnp.int32),
            pltpu.SemaphoreType.DMA((8,)),
            pltpu.SemaphoreType.DMA,
            pltpu.SemaphoreType.DMA,
        ],
        compiler_params=params(8),
        name="load",
    )(target, *pin(fields))


def wave_kernel(ints, amounts, *refs):
    xw, y_own, y_other, same, cross, own, other = refs[:7]
    p_out, q_out, *totals, p_rims = refs[16:21]
    bufs = refs[21:29]
    listed, data, stage, snaps, wide, outer, sem_in = refs[29:]
    core = lax.axis_index("mem")
    half, rows, depth = p_out.shape
    lists = copy_all([(ints, listed), (amounts, data)], sem_in)
    near = pl.ds(core * HMAX, half + HMAX)
    mains = copy_all(
        [
            (own.at[:, near], snaps.at[pl.ds(2 * core, 2)]),
            (other.at[:, near], snaps.at[pl.ds(2 - 2 * core, 2)]),
        ],
        sem_in.at[pl.ds(2, 2)],
    )
    inner = half + DEEP
    for f in range(8):
        d = SENT[f]
        to = jnp.where(core == 0, DEEP - d, half + DEEP)
        part = xw[SENT_AT[f] : SENT_AT[f] + d]
        bufs[f][pl.ds(to, d), ROW0 : ROW0 + rows, :] = part.astype(F32)
    for ys, corner, side in ((y_own, same, core), (y_other, cross, 1 - core)):
        to = jnp.where(side == 0, ROW0 - DEEP, ROW0 + rows)
        for slab in range(2):
            part = ys[slab, pl.ds(core * (half - DEEP), inner)]
            stage[pl.ds(DEEP * (1 - core), inner)] = part.astype(F32)
            d, begin = CORNER[slab], slab * CORNER[0]
            to_x = jnp.where(core == 0, DEEP - d, half + DEEP)
            stage[pl.ds(to_x, d)] = corner[begin : begin + d].astype(F32)
            for i in range(4):
                bufs[4 * slab + i][:, pl.ds(to, DEEP), :] = stage[:, 4 * i : 4 * i + 4, :]

    wait_all(lists)
    horiz, vert, ratio, tilt = bufs[4:]
    thin = lax.broadcasted_iota(jnp.int32, (1, depth), 1)

    def step(k, p, q, old_p, old_q):
        low, high = 1 + k, half + 2 * DEEP - 1 - k
        begin, end = (ROW0 - 8, ROW0 + rows + 8) if k < NT - 1 else (ROW0, ROW0 + rows)
        size = 48 if (end - begin) % 48 == 0 else 64 if (end - begin) % 64 == 0 else 8

        def strip(i, _):
            r = pl.multiple_of(begin + i * size, 8)
            at = pl.ds(r, size)
            p_m, p_c, q_c = p[low - 1, at, :], p[low, at, :], q[low, at, :]
            _, d_m = slopes(q[low - 1, at, :])
            s_c, d_c = slopes(q_c)
            for x in range(low, high):
                p_n, q_n = p[x + 1, at, :], q[x + 1, at, :]
                s_n, d_n = slopes(q_n)
                beside = p[x, pl.ds(r - 1, size), :] + p[x, pl.ds(r + 1, size), :]
                lateral = ((p_m + p_n) + beside) - 4.0 * p_c
                q_2 = 2.0 * q_c
                horizontal = horiz[x, at, :] * lateral
                mixed = (0.25 * tilt[x, at, :]) * (d_n - d_m)
                upright = vert[x, at, :] * ((s_c - q_2) + mixed)
                p_new = (2.0 * p_c - old_p[x, at, :]) + (horizontal + upright)
                q_new = (q_2 - old_q[x, at, :]) + (ratio[x, at, :] * horizontal + upright)
                if k < NT - 1:
                    old_p[x, at, :] = p_new
                    old_q[x, at, :] = q_new
                else:
                    out_at = pl.ds(pl.multiple_of(r - ROW0, 8), size)
                    p_out[x - DEEP, out_at, :] = p_new
                    q_out[x - DEEP, out_at, :] = q_new
                p_m, p_c, q_c, s_c, d_m, d_c = p_c, p_n, q_n, s_n, d_c, d_n
            return 0

        lax.fori_loop(0, (end - begin) // size, strip, 0)

    def inject(k, old_p, old_q):
        def group(g, _):
            for i in range(GROUP):
                j = HEAD + g * GROUP + i
                place = listed[j + (listed.shape[0] - HEAD) // 2]
                amount = data[NT - 1 - k, listed[j]]
                x, y, z = place >> 16, (place >> 8) & 255, place & 255
                add = jnp.where(thin == z, amount, 0.0)
                old_p[x, pl.ds(y, 1), :] = old_p[x, pl.ds(y, 1), :] - add
                old_q[x, pl.ds(y, 1), :] = old_q[x, pl.ds(y, 1), :] - add
            return 0

        lax.fori_loop(0, listed[0], group, 0)

    def add_image(k, p, lag):
        off_x, off_y = listed[1 + 2 * lag], listed[2 + 2 * lag]
        t = NT - 1 - k
        pair, part = t // 2, t % 2
        from_own = core == jnp.where(off_y > 0, 0, 1)

        def layer(i, _):
            at = jnp.clip(core * HMAX + i - off_x, 0, half + HMAX - 1)
            slot = i % 8
            mine, others = y_own[2 + pair, core * HMAX + at], y_other[2 + pair, core * HMAX + at]
            rim = jnp.where(from_own, mine.astype(F32), others.astype(F32))
            rim = rim[8 * part : 8 * part + 8]
            wide[slot, HMAX : HMAX + rows, :] = snaps[t, at].astype(F32)
            wide[slot, 0:HMAX, :] = rim
            wide[slot, HMAX + rows :, :] = rim
            term = wide[slot, pl.ds(HMAX - off_y, rows), :] * p[i + DEEP, ROW0 : ROW0 + rows, :]
            totals[lag][i] = term if k == 0 else totals[lag][i] + term
            return 0

        lax.fori_loop(0, half, layer, 0, unroll=8)

    p_now, q_now, p_old, q_old = bufs[:4]
    main = slice(ROW0, ROW0 + rows)
    far = jnp.where(core == 0, DEEP - 3, half + DEEP + 2)
    for buf in (p_old, q_old):
        buf[far, main, :] = jnp.zeros((rows, depth), F32)
    for k in range(NT):
        inject(k, p_old, q_old)
        if k == 0:
            row = lax.broadcasted_iota(jnp.int32, (rows, depth), 0)
            ends = xw[AHEAD + 2].astype(F32)
            before, behind = p_now[far, pl.ds(ROW0 - 1, 1), :], p_now[far, pl.ds(ROW0 + rows, 1), :]
            for i, buf in enumerate((p_old, q_old)):
                value = xw[AHEAD + i].astype(F32) - buf[far, main, :]
                value += jnp.where(row == 0, ends[2 * i : 2 * i + 1] * before, 0.0)
                value += jnp.where(row == rows - 1, ends[2 * i + 1 : 2 * i + 2] * behind, 0.0)
                outer[i] = value
        p_rims[k] = p_now[pl.ds(DEEP + core * HMAX, HMAX), ROW0 : ROW0 + rows, :]
        step(k, p_now, q_now, p_old, q_old)
        if k == 0:
            for i, buf in enumerate((p_old, q_old)):
                buf[far, main, :] = outer[i]
            wait_all(mains)
        for lag in range(2):
            add_image(k, p_now, lag)
        p_now, p_old, q_now, q_old = p_old, p_now, q_old, q_now


def wave(ints, data, halos, own, other, earlier, bufs):
    width, rows, depth = own.shape[1:]
    half = width // 2
    any_space = pl.BlockSpec(memory_space=pl.ANY)
    return pl.pallas_call(
        wave_kernel,
        out_shape=(
            *(pltpu.VMEM((half, rows, depth), F32),) * 4,
            pltpu.VMEM((NT, HMAX, rows, depth), F32),
        )
        + tuple(pltpu.VMEM(b.shape, F32) for b in bufs),
        in_specs=[any_space] * 2 + [VMEM] * 5 + [HBM] + [any_space] * 2 + [VMEM] * 8,
        out_specs=(VMEM,) * 13,
        input_output_aliases={10 + i: 5 + i for i in range(8)},
        scratch_shapes=[
            pltpu.SMEM(ints.shape, jnp.int32),
            pltpu.SMEM(data.shape, F32),
            pltpu.VMEM((half + 2 * DEEP, 16, depth), F32),
            pltpu.VMEM((NT, half + HMAX, rows, depth), BF16),
            pltpu.VMEM((8, rows + 2 * HMAX, depth), F32),
            pltpu.VMEM((2, rows, depth), F32),
            pltpu.SemaphoreType.DMA((4,)),
        ],
        compiler_params=params(8),
        name="wave",
    )(ints, data, *pin(halos, pltpu.VMEM), *pin((own,)), other, earlier, *pin(bufs, pltpu.VMEM))[:5]


def merge_kernel(p_own, p_other, q_own, q_other, total, _, p, q, image, sems):
    core = lax.axis_index("mem")
    half = total.shape[0]
    here, there = pl.ds(half * core, half), pl.ds(half - half * core, half)
    pairs = [(p_own, p.at[here]), (p_other, p.at[there]), (q_own, q.at[here]), (q_other, q.at[there])]
    wait_all(copy_all(pairs + [(total, image.at[here])], sems))


def merge(halves, earlier):
    half, rows, depth = halves[0].shape
    return pl.pallas_call(
        merge_kernel,
        out_shape=(jax.ShapeDtypeStruct((2 * half, rows, depth), F32),) * 3,
        in_specs=[VMEM] * 5 + [pl.BlockSpec(memory_space=pl.ANY)],
        out_specs=(HBM,) * 3,
        scratch_shapes=[pltpu.SemaphoreType.DMA((5,))],
        compiler_params=params(8),
        name="merge",
    )(*pin(halves, pltpu.VMEM), earlier)


def rim_kernel(offs, offs_other, xs, same, cross, p_rims, _, total, given, wide):
    core = lax.axis_index("mem")
    half, rows, _ = total.shape
    for lag, off in enumerate((offs, offs_other)):
        off_x, off_y = off[0, 0], off[0, 1]
        layers = jnp.maximum(jnp.where(core == 0, off_x, -off_x), 0)
        from_same = core == jnp.where(off_y > 0, 0, 1)

        def layer(i, lag=lag, off_y=off_y, layers=layers, from_same=from_same):
            at = jnp.where(core == 0, HMAX - layers + i, i)
            mine = jnp.where(core == 0, i, HMAX - layers + i)
            result = None
            for pair in range(2):
                place = sum(CORNER) + pair * HMAX + at
                strip = jnp.where(from_same, same[place].astype(F32), cross[place].astype(F32))
                for part in range(2):
                    t = 2 * pair + part
                    rim = strip[8 * part : 8 * part + 8]
                    wide[t, HMAX : HMAX + rows, :] = xs[t, at].astype(F32)
                    wide[t, 0:HMAX, :] = rim
                    wide[t, HMAX + rows :, :] = rim
                    term = wide[t, pl.ds(HMAX - off_y, rows), :] * p_rims[NT - 1 - t, mine]
                    result = term if result is None else result + term
            if lag == 1:
                given[i] = result
            else:
                total[jnp.where(core == 0, i, half - layers + i)] = result

        for i in range(HMAX):
            pl.when(i < layers)(lambda i=i, layer=layer: layer(i))


def rim_image(offs, offs_other, halos, p_rims, total):
    half, rows, depth = total.shape
    return pl.pallas_call(
        rim_kernel,
        out_shape=(
            pltpu.VMEM(total.shape, F32),
            pltpu.VMEM((HMAX, rows, depth), F32),
        ),
        in_specs=[SMEM] * 2 + [VMEM] * 5,
        out_specs=(VMEM, VMEM),
        input_output_aliases={6: 0},
        scratch_shapes=[pltpu.VMEM((NT, rows + 2 * HMAX, depth), F32)],
        compiler_params=params(8),
        name="rim_image",
    )(offs, offs_other, *pin((*halos, p_rims, total), pltpu.VMEM))


def place_kernel(offs, _, given, __, image, others, sems):
    core = lax.axis_index("mem")
    half = others.shape[0]
    there = half - half * core
    rim, inner = (half - HMAX) * (1 - core), HMAX * core
    rest = pltpu.make_async_copy(
        others.at[pl.ds(inner, half - HMAX)], image.at[pl.ds(there + inner, half - HMAX)], sems.at[0]
    )
    rest.start()
    layers = jnp.maximum(jnp.where(core == 0, -offs[0, 0], offs[0, 0]), 0)

    def put(i):
        others[jnp.where(core == 0, half - layers + i, i)] = given[i]

    for i in range(HMAX):
        pl.when(i < layers)(lambda i=i: put(i))
    last = pltpu.make_async_copy(
        others.at[pl.ds(rim, HMAX)], image.at[pl.ds(there + rim, HMAX)], sems.at[1]
    )
    last.start()
    wait_all([rest, last])


def place_image(offs, others, given, image):
    return pl.pallas_call(
        place_kernel,
        out_shape=(jax.ShapeDtypeStruct(image.shape, F32), pltpu.VMEM(others.shape, F32)),
        in_specs=[SMEM] + [VMEM] * 2 + [HBM],
        out_specs=(HBM, VMEM),
        input_output_aliases={1: 1, 3: 0},
        scratch_shapes=[pltpu.SemaphoreType.DMA((2,))],
        compiler_params=params(8),
        name="place_image",
    )(offs, *pin((others, given), pltpu.VMEM), *pin((image,)))[0]


def body(
    src_hist, rec_p, rec_q, prev_p, prev_q, horiz, vert, ratio, tilt, rec_pos, rec_data, lag_offs
):
    width, rows, depth = rec_p.shape
    fields = (rec_p, rec_q, prev_p, prev_q, horiz, vert, ratio, tilt)

    def swap(v):
        return lax.ppermute(v, "mem", [(0, 1), (1, 0)])

    def after(v, earlier):
        return lax.optimization_barrier((v, earlier))[0]

    def outward(v, step_x, step_y):
        count_x, count_y = lax.axis_size("gx"), lax.axis_size("gy")
        pairs = []
        for x in range(count_x):
            for y in range(count_y):
                for core, sign in ((0, 1), (1, -1)):
                    to_x, to_y = x + sign * step_x, y + sign * step_y
                    if 0 <= to_x < count_x and 0 <= to_y < count_y:
                        pairs.append(((x * count_y + y) * 2 + core, (to_x * count_y + to_y) * 2 + core))
        return lax.ppermute(v, ("gx", "gy", "mem"), pairs)

    plane = rows * lax.axis_size("gy") * depth
    half = width // 2
    x = rec_pos // plane - lax.axis_index("gx") * width - lax.axis_index("mem") * half + DEEP
    rest = rec_pos % plane
    y = rest // depth - lax.axis_index("gy") * rows + ROW0
    z = rest % depth
    inside = (x >= 0) & (x < half + 2 * DEEP)
    inside &= (y >= ROW0 - DEEP) & (y < ROW0 + rows + DEEP)
    target = jnp.where(inside, (x << 16) + (y << 8) + z, -1)
    offs_other = swap(lag_offs)
    target = jnp.concatenate([target, lag_offs[0], offs_other[0]])

    other = swap(src_hist)
    packed = pack_x(fields)
    xw = outward(packed, 1, 0)
    ys, same, cross, xs = pack_rest(fields, src_hist, after(other, packed))
    ys, same, cross = outward(ys, 0, 1), outward(same, 1, 1), outward(cross, 1, -1)
    *bufs, ints = load(fields, after(target, packed))
    xs = outward(after(xs, (same, cross)), 1, 0)
    halos = (xw, ys, swap(ys), same, cross)
    token = swap(xw[0, :16])
    p, q, total, total_other, p_rims = wave(ints, rec_data, halos, src_hist, other, token, bufs)
    parts = (swap(p), swap(q), swap(total_other))
    total, given = rim_image(lag_offs, offs_other, (after(xs, p), same, cross), p_rims, total)
    p, q, image = merge((p, parts[0], q, parts[1], total), given)
    image = place_image(lag_offs, parts[2], swap(given), image)
    return image[None], p, q


def solution(mesh):
    block = P("gx", "gy", None)
    return jax.shard_map(
        body,
        mesh=mesh,
        in_specs=(P("mem", "gx", "gy", None),) + (block,) * 8 + (P(), P(), P("mem", None)),
        out_specs=(P("mem", "gx", "gy", None), block, block),
        check_vma=False,
    )
```

```python
import functools

import jax
import jax.numpy as jnp
from jax import lax
from jax.experimental import pallas as pl
from jax.experimental.pallas import tpu as pltpu
from jax.sharding import PartitionSpec as P

NT = 4
HMAX = 8
DEEP = NT
ROW0 = 16
GROUP = 8
CORNER = (DEEP - 1, DEEP - 2)
HEAD = 8
F32 = jnp.float32
BF16 = jnp.bfloat16
HBM = pl.BlockSpec(memory_space=pltpu.HBM)
SMEM = pl.BlockSpec(memory_space=pltpu.SMEM)
VMEM = pl.BlockSpec(memory_space=pltpu.VMEM)
DEPTHS = (DEEP, DEEP) + (DEEP - 1,) * 6
STARTS = tuple(sum(DEPTHS[:i]) for i in range(8))
SENT = tuple(d - 1 for d in DEPTHS)
SENT_AT = tuple(sum(SENT[:i]) for i in range(8))
AHEAD = sum(SENT)
LAYERS = AHEAD + 3


def pin(arrays, space=pltpu.HBM):
    return [pltpu.with_memory_space_constraint(a, space) for a in arrays]


def params(mib=63):
    return pltpu.CompilerParams(vmem_limit_bytes=mib * 2**20)


def copy_all(pairs, sems):
    copies = [pltpu.make_async_copy(a, b, sems.at[i]) for i, (a, b) in enumerate(pairs)]
    for c in copies:
        c.start()
    return copies


def wait_all(copies):
    for c in copies:
        c.wait()


def slopes(v):
    depth = v.shape[-1]
    lane = lax.broadcasted_iota(jnp.int32, v.shape, 1)
    up = jnp.where(lane == depth - 1, 0.0, pltpu.roll(v, depth - 1, 1))
    down = jnp.where(lane == 0, 0.0, pltpu.roll(v, 1, 1))
    return up + down, up - down


def pack_x_kernel(*refs):
    fields, small, stage, sems = refs[:8], *refs[8:]
    core = lax.axis_index("mem")
    width, rows, _ = fields[0].shape
    pairs = []
    for f, s, d in zip(fields, STARTS, DEPTHS):
        begin = jnp.where(core == 0, width - d, 0)
        pairs.append((f.at[pl.ds(begin, d)], stage.at[pl.ds(s, d)]))
    copies = copy_all(pairs, sems)
    for i in range(8):
        copies[i].wait()
        small[SENT_AT[i] : SENT_AT[i] + SENT[i]] = stage[pl.ds(STARTS[i] + 1 - core, SENT[i])].astype(BF16)
    at = [s + (1 + core if i < 2 else 2 * core) for i, s in enumerate(STARTS)]
    p, q, old_p, old_q, horiz, vert, ratio, tilt = [stage[j] for j in at]
    row = lax.broadcasted_iota(jnp.int32, p.shape, 0)
    beside = jnp.where(row == 0, 0.0, pltpu.roll(p, 1, 0))
    beside += jnp.where(row == rows - 1, 0.0, pltpu.roll(p, rows - 1, 0))
    lateral = stage[at[0] - 1] + stage[at[0] + 1] + beside - 4.0 * p
    mixed = slopes(stage[at[1] + 1])[1] - slopes(stage[at[1] - 1])[1]
    horizontal = horiz * lateral
    upright = vert * ((slopes(q)[0] - 2.0 * q) + (0.25 * tilt) * mixed)
    small[AHEAD] = ((2.0 * p - old_p) + (horizontal + upright)).astype(BF16)
    small[AHEAD + 1] = ((2.0 * q - old_q) + (ratio * horizontal + upright)).astype(BF16)
    both = ratio * horiz
    ends = jnp.where(row == 0, horiz[:1], jnp.where(row == 1, horiz[rows - 1 :], 0.0))
    ends = jnp.where(row == 2, both[:1], jnp.where(row == 3, both[rows - 1 :], ends))
    small[AHEAD + 2] = ends.astype(BF16)


def pack_x(fields):
    shape = fields[0].shape[1:]
    return pl.pallas_call(
        pack_x_kernel,
        out_shape=pltpu.VMEM((LAYERS,) + shape, BF16),
        in_specs=[HBM] * 8,
        out_specs=VMEM,
        scratch_shapes=[
            pltpu.VMEM((sum(DEPTHS),) + shape, F32),
            pltpu.SemaphoreType.DMA((8,)),
        ],
        compiler_params=params(16),
        name="pack_x",
    )(*pin(fields))


def pack_rest_kernel(*refs):
    fields, own, other = refs[:8], *refs[8:10]
    s_ys, s_same, s_cross, edges = refs[10:14]
    stage, snaps, stage_c, snaps_c, mixed, sems = refs[14:]
    core = lax.axis_index("mem")
    width, rows, _ = fields[0].shape
    near, far = width - DEEP, width - HMAX
    to_low = core == 1
    x_near, x_far = jnp.where(to_low, 0, near), jnp.where(to_low, 0, far)

    def y_at(low, size):
        return pl.multiple_of(jnp.where(low, 0, rows - size), size)

    pairs = []
    for i, f in enumerate(fields):
        pairs.append((f.at[:, pl.ds(y_at(to_low, 8), 8)], stage.at[i]))
        pairs.append((f.at[pl.ds(x_near, DEEP), pl.ds(y_at(~to_low, 8), 8)], stage_c.at[i]))
    for ref, half in ((own, core), (other, 1 - core)):
        pairs.append((ref.at[:, :, pl.ds(y_at(to_low, 16), 16)], snaps.at[half]))
        rim = ref.at[:, pl.ds(x_far, HMAX), pl.ds(y_at(~to_low, 16), 16)]
        pairs.append((rim, snaps_c.at[half]))
        pairs.append((ref.at[:, pl.ds(x_far, HMAX)], edges.at[pl.ds(2 * half, 2)]))
    copies = copy_all(pairs, sems)
    wait_all(copies[:16])
    skip, skip_c = jnp.where(to_low, 0, 4), jnp.where(to_low, 4, 0)
    for slab in range(2):
        for i in range(4):
            at = pl.ds(4 * i, 4)
            mixed[:width, at, :] = stage[4 * slab + i, :, pl.ds(skip, 4), :]
            mixed[width : width + DEEP, at, :] = stage_c[4 * slab + i, :, pl.ds(skip_c, 4), :]
        s_ys[slab] = mixed[:width].astype(BF16)
        d, begin = CORNER[slab], slab * CORNER[0]
        part = mixed[pl.ds(width + (DEEP - d) * (1 - core), d)]
        s_cross[begin : begin + d] = part.astype(BF16)
    wait_all(copies[16:])
    for pair in range(2):
        for i in range(2):
            at = slice(8 * i, 8 * i + 8)
            both = snaps[pair, i].astype(F32)
            mixed[:width, at, :] = jnp.where(to_low, both[:, :8], both[:, 8:])
            both = snaps_c[pair, i].astype(F32)
            mixed[width : width + HMAX, at, :] = jnp.where(to_low, both[:, 8:], both[:, :8])
        s_ys[2 + pair] = mixed[:width].astype(BF16)
        begin = sum(CORNER) + pair * HMAX
        s_cross[begin : begin + HMAX] = mixed[width : width + HMAX].astype(BF16)
    for slab in range(2):
        d, begin = CORNER[slab], slab * CORNER[0]
        s_same[begin : begin + d] = s_ys[slab, pl.ds(jnp.where(to_low, 0, width - d), d)]
        begin = sum(CORNER) + slab * HMAX
        s_same[begin : begin + HMAX] = s_ys[2 + slab, pl.ds(x_far, HMAX)]


def pack_rest(fields, own, other):
    width, rows, depth = fields[0].shape
    corner = (sum(CORNER) + 2 * HMAX, 16, depth)
    return pl.pallas_call(
        pack_rest_kernel,
        out_shape=(
            pltpu.VMEM((4, width, 16, depth), BF16),
            pltpu.VMEM(corner, BF16),
            pltpu.VMEM(corner, BF16),
            pltpu.VMEM((NT, HMAX, rows, depth), BF16),
        ),
        in_specs=[HBM] * 9 + [pl.BlockSpec(memory_space=pl.ANY)],
        out_specs=(VMEM,) * 4,
        scratch_shapes=[
            pltpu.VMEM((8, width, 8, depth), F32),
            pltpu.VMEM((2, 2, width, 16, depth), BF16),
            pltpu.VMEM((8, DEEP, 8, depth), F32),
            pltpu.VMEM((2, 2, HMAX, 16, depth), BF16),
            pltpu.VMEM((width + HMAX, 16, depth), F32),
            pltpu.SemaphoreType.DMA((22,)),
        ],
        compiler_params=params(16),
        name="pack_rest",
    )(*pin((*fields, own)), other)


def load_kernel(target, *refs):
    fields, bufs, (ints, listed, s_target, sems, sem_target, sem_ints) = refs[:8], refs[-14:-6], refs[-6:]
    core = lax.axis_index("mem")
    n = target.shape[0] - 4
    fetch = pltpu.make_async_copy(target, s_target, sem_target)
    fetch.start()
    width, rows, _ = fields[0].shape
    inner = width // 2 + DEEP
    pairs = []
    for f, b in zip(fields, bufs):
        to = b.at[pl.ds(DEEP * (1 - core), inner), pl.ds(ROW0, rows)]
        pairs.append((f.at[pl.ds((width - inner) * core, inner)], to))
    copies = copy_all(pairs, sems)
    fetch.wait()

    def one(r, at):
        place = s_target[r]
        listed[at] = r
        listed[at + n + GROUP] = place
        return at + jnp.where(place >= 0, 1, 0)

    end = lax.fori_loop(0, n, one, jnp.int32(HEAD), unroll=32)
    for i in range(GROUP):
        listed[end + i] = 0
        listed[end + i + n + GROUP] = 0
    listed[0] = (end - HEAD + GROUP - 1) // GROUP
    for i in range(4):
        listed[1 + i] = s_target[n + i]
    save = pltpu.make_async_copy(listed, ints, sem_ints)
    save.start()
    wait_all(copies + [save])


def load(fields, target):
    width, rows, depth = fields[0].shape
    any_space = pl.BlockSpec(memory_space=pl.ANY)
    n = target.shape[0] - 4
    listed = (HEAD + 2 * (n + GROUP),)
    shape = (width // 2 + 2 * DEEP, rows + 2 * ROW0, depth)
    return pl.pallas_call(
        load_kernel,
        out_shape=(pltpu.VMEM(shape, F32),) * 8 + (jax.ShapeDtypeStruct(listed, jnp.int32),),
        in_specs=[any_space] + [HBM] * 8,
        out_specs=(VMEM,) * 8 + (any_space,),
        scratch_shapes=[
            pltpu.SMEM(listed, jnp.int32),
            pltpu.SMEM((n + 4,), jnp.int32),
            pltpu.SemaphoreType.DMA((8,)),
            pltpu.SemaphoreType.DMA,
            pltpu.SemaphoreType.DMA,
        ],
        compiler_params=params(8),
        name="load",
    )(target, *pin(fields))


def wave_kernel(ints, amounts, *refs):
    xw, y_own, y_other, same, cross, own, other = refs[:7]
    p_out, q_out, *totals, p_rims = refs[16:21]
    bufs = refs[21:29]
    listed, data, stage, snaps, wide, outer, sem_in = refs[29:]
    core = lax.axis_index("mem")
    half, rows, depth = p_out.shape
    lists = copy_all([(ints, listed), (amounts, data)], sem_in)
    near = pl.ds(core * HMAX, half + HMAX)
    mains = copy_all(
        [
            (own.at[:, near], snaps.at[pl.ds(2 * core, 2)]),
            (other.at[:, near], snaps.at[pl.ds(2 - 2 * core, 2)]),
        ],
        sem_in.at[pl.ds(2, 2)],
    )
    inner = half + DEEP
    for f in range(8):
        d = SENT[f]
        to = jnp.where(core == 0, DEEP - d, half + DEEP)
        part = xw[SENT_AT[f] : SENT_AT[f] + d]
        bufs[f][pl.ds(to, d), ROW0 : ROW0 + rows, :] = part.astype(F32)
    for ys, corner, side in ((y_own, same, core), (y_other, cross, 1 - core)):
        to = jnp.where(side == 0, ROW0 - DEEP, ROW0 + rows)
        for slab in range(2):
            part = ys[slab, pl.ds(core * (half - DEEP), inner)]
            stage[pl.ds(DEEP * (1 - core), inner)] = part.astype(F32)
            d, begin = CORNER[slab], slab * CORNER[0]
            to_x = jnp.where(core == 0, DEEP - d, half + DEEP)
            stage[pl.ds(to_x, d)] = corner[begin : begin + d].astype(F32)
            for i in range(4):
                bufs[4 * slab + i][:, pl.ds(to, DEEP), :] = stage[:, 4 * i : 4 * i + 4, :]

    wait_all(lists)
    horiz, vert, ratio, tilt = bufs[4:]
    thin = lax.broadcasted_iota(jnp.int32, (1, depth), 1)

    def step(k, p, q, old_p, old_q):
        low, high = 1 + k, half + 2 * DEEP - 1 - k
        begin, end = (ROW0 - 8, ROW0 + rows + 8) if k < NT - 1 else (ROW0, ROW0 + rows)
        size = 48 if (end - begin) % 48 == 0 else 64 if (end - begin) % 64 == 0 else 8

        def strip(i, _):
            r = pl.multiple_of(begin + i * size, 8)
            at = pl.ds(r, size)
            p_m, p_c, q_c = p[low - 1, at, :], p[low, at, :], q[low, at, :]
            _, d_m = slopes(q[low - 1, at, :])
            s_c, d_c = slopes(q_c)
            for x in range(low, high):
                p_n, q_n = p[x + 1, at, :], q[x + 1, at, :]
                s_n, d_n = slopes(q_n)
                beside = p[x, pl.ds(r - 1, size), :] + p[x, pl.ds(r + 1, size), :]
                lateral = ((p_m + p_n) + beside) - 4.0 * p_c
                q_2 = 2.0 * q_c
                horizontal = horiz[x, at, :] * lateral
                mixed = (0.25 * tilt[x, at, :]) * (d_n - d_m)
                upright = vert[x, at, :] * ((s_c - q_2) + mixed)
                p_new = (2.0 * p_c - old_p[x, at, :]) + (horizontal + upright)
                q_new = (q_2 - old_q[x, at, :]) + (ratio[x, at, :] * horizontal + upright)
                if k < NT - 1:
                    old_p[x, at, :] = p_new
                    old_q[x, at, :] = q_new
                else:
                    out_at = pl.ds(pl.multiple_of(r - ROW0, 8), size)
                    p_out[x - DEEP, out_at, :] = p_new
                    q_out[x - DEEP, out_at, :] = q_new
                p_m, p_c, q_c, s_c, d_m, d_c = p_c, p_n, q_n, s_n, d_c, d_n
            return 0

        lax.fori_loop(0, (end - begin) // size, strip, 0)

    def inject(k, old_p, old_q):
        def group(g, _):
            for i in range(GROUP):
                j = HEAD + g * GROUP + i
                place = listed[j + (listed.shape[0] - HEAD) // 2]
                amount = data[NT - 1 - k, listed[j]]
                x, y, z = place >> 16, (place >> 8) & 255, place & 255
                add = jnp.where(thin == z, amount, 0.0)
                old_p[x, pl.ds(y, 1), :] = old_p[x, pl.ds(y, 1), :] - add
                old_q[x, pl.ds(y, 1), :] = old_q[x, pl.ds(y, 1), :] - add
            return 0

        lax.fori_loop(0, listed[0], group, 0)

    def add_image(k, p, lag):
        off_x, off_y = listed[1 + 2 * lag], listed[2 + 2 * lag]
        t = NT - 1 - k
        pair, part = t // 2, t % 2
        from_own = core == jnp.where(off_y > 0, 0, 1)

        def layer(i, _):
            at = jnp.clip(core * HMAX + i - off_x, 0, half + HMAX - 1)
            slot = i % 8
            mine, others = y_own[2 + pair, core * HMAX + at], y_other[2 + pair, core * HMAX + at]
            rim = jnp.where(from_own, mine.astype(F32), others.astype(F32))
            rim = rim[8 * part : 8 * part + 8]
            wide[slot, HMAX : HMAX + rows, :] = snaps[t, at].astype(F32)
            wide[slot, 0:HMAX, :] = rim
            wide[slot, HMAX + rows :, :] = rim
            term = wide[slot, pl.ds(HMAX - off_y, rows), :] * p[i + DEEP, ROW0 : ROW0 + rows, :]
            totals[lag][i] = term if k == 0 else totals[lag][i] + term
            return 0

        lax.fori_loop(0, half, layer, 0, unroll=8)

    p_now, q_now, p_old, q_old = bufs[:4]
    main = slice(ROW0, ROW0 + rows)
    far = jnp.where(core == 0, DEEP - 3, half + DEEP + 2)
    for buf in (p_old, q_old):
        buf[far, main, :] = jnp.zeros((rows, depth), F32)
    for k in range(NT):
        inject(k, p_old, q_old)
        if k == 0:
            row = lax.broadcasted_iota(jnp.int32, (rows, depth), 0)
            ends = xw[AHEAD + 2].astype(F32)
            before, behind = p_now[far, pl.ds(ROW0 - 1, 1), :], p_now[far, pl.ds(ROW0 + rows, 1), :]
            for i, buf in enumerate((p_old, q_old)):
                value = xw[AHEAD + i].astype(F32) - buf[far, main, :]
                value += jnp.where(row == 0, ends[2 * i : 2 * i + 1] * before, 0.0)
                value += jnp.where(row == rows - 1, ends[2 * i + 1 : 2 * i + 2] * behind, 0.0)
                outer[i] = value
        p_rims[k] = p_now[pl.ds(DEEP + core * HMAX, HMAX), ROW0 : ROW0 + rows, :]
        step(k, p_now, q_now, p_old, q_old)
        if k == 0:
            for i, buf in enumerate((p_old, q_old)):
                buf[far, main, :] = outer[i]
            wait_all(mains)
        for lag in range(2):
            add_image(k, p_now, lag)
        p_now, p_old, q_now, q_old = p_old, p_now, q_old, q_now


def wave(ints, data, halos, own, other, earlier, bufs):
    width, rows, depth = own.shape[1:]
    half = width // 2
    any_space = pl.BlockSpec(memory_space=pl.ANY)
    return pl.pallas_call(
        wave_kernel,
        out_shape=(
            *(pltpu.VMEM((half, rows, depth), F32),) * 4,
            pltpu.VMEM((NT, HMAX, rows, depth), F32),
        )
        + tuple(pltpu.VMEM(b.shape, F32) for b in bufs),
        in_specs=[any_space] * 2 + [VMEM] * 5 + [HBM] + [any_space] * 2 + [VMEM] * 8,
        out_specs=(VMEM,) * 13,
        input_output_aliases={10 + i: 5 + i for i in range(8)},
        scratch_shapes=[
            pltpu.SMEM(ints.shape, jnp.int32),
            pltpu.SMEM(data.shape, F32),
            pltpu.VMEM((half + 2 * DEEP, 16, depth), F32),
            pltpu.VMEM((NT, half + HMAX, rows, depth), BF16),
            pltpu.VMEM((8, rows + 2 * HMAX, depth), F32),
            pltpu.VMEM((2, rows, depth), F32),
            pltpu.SemaphoreType.DMA((4,)),
        ],
        compiler_params=params(8),
        name="wave",
    )(ints, data, *pin(halos, pltpu.VMEM), *pin((own,)), other, earlier, *pin(bufs, pltpu.VMEM))[:5]


def merge_kernel(p_own, p_other, q_own, q_other, total, _, p, q, image, sems):
    core = lax.axis_index("mem")
    half = total.shape[0]
    here, there = pl.ds(half * core, half), pl.ds(half - half * core, half)
    pairs = [(p_own, p.at[here]), (p_other, p.at[there]), (q_own, q.at[here]), (q_other, q.at[there])]
    wait_all(copy_all(pairs + [(total, image.at[here])], sems))


def merge(halves, earlier):
    half, rows, depth = halves[0].shape
    return pl.pallas_call(
        merge_kernel,
        out_shape=(jax.ShapeDtypeStruct((2 * half, rows, depth), F32),) * 3,
        in_specs=[VMEM] * 5 + [pl.BlockSpec(memory_space=pl.ANY)],
        out_specs=(HBM,) * 3,
        scratch_shapes=[pltpu.SemaphoreType.DMA((5,))],
        compiler_params=params(8),
        name="merge",
    )(*pin(halves, pltpu.VMEM), earlier)


def rim_kernel(offs, offs_other, xs, same, cross, p_rims, _, total, given, wide):
    core = lax.axis_index("mem")
    half, rows, _ = total.shape
    for lag, off in enumerate((offs, offs_other)):
        off_x, off_y = off[0, 0], off[0, 1]
        layers = jnp.maximum(jnp.where(core == 0, off_x, -off_x), 0)
        from_same = core == jnp.where(off_y > 0, 0, 1)

        def layer(i, lag=lag, off_y=off_y, layers=layers, from_same=from_same):
            at = jnp.where(core == 0, HMAX - layers + i, i)
            mine = jnp.where(core == 0, i, HMAX - layers + i)
            result = None
            for pair in range(2):
                place = sum(CORNER) + pair * HMAX + at
                strip = jnp.where(from_same, same[place].astype(F32), cross[place].astype(F32))
                for part in range(2):
                    t = 2 * pair + part
                    rim = strip[8 * part : 8 * part + 8]
                    wide[t, HMAX : HMAX + rows, :] = xs[t, at].astype(F32)
                    wide[t, 0:HMAX, :] = rim
                    wide[t, HMAX + rows :, :] = rim
                    term = wide[t, pl.ds(HMAX - off_y, rows), :] * p_rims[NT - 1 - t, mine]
                    result = term if result is None else result + term
            if lag == 1:
                given[i] = result
            else:
                total[jnp.where(core == 0, i, half - layers + i)] = result

        for i in range(HMAX):
            pl.when(i < layers)(lambda i=i, layer=layer: layer(i))


def rim_image(offs, offs_other, halos, p_rims, total):
    half, rows, depth = total.shape
    return pl.pallas_call(
        rim_kernel,
        out_shape=(
            pltpu.VMEM(total.shape, F32),
            pltpu.VMEM((HMAX, rows, depth), F32),
        ),
        in_specs=[SMEM] * 2 + [VMEM] * 5,
        out_specs=(VMEM, VMEM),
        input_output_aliases={6: 0},
        scratch_shapes=[pltpu.VMEM((NT, rows + 2 * HMAX, depth), F32)],
        compiler_params=params(8),
        name="rim_image",
    )(offs, offs_other, *pin((*halos, p_rims, total), pltpu.VMEM))


def place_kernel(offs, _, given, __, image, others, sems):
    core = lax.axis_index("mem")
    half = others.shape[0]
    there = half - half * core
    rim, inner = (half - HMAX) * (1 - core), HMAX * core
    rest = pltpu.make_async_copy(
        others.at[pl.ds(inner, half - HMAX)], image.at[pl.ds(there + inner, half - HMAX)], sems.at[0]
    )
    rest.start()
    layers = jnp.maximum(jnp.where(core == 0, -offs[0, 0], offs[0, 0]), 0)

    def put(i):
        others[jnp.where(core == 0, half - layers + i, i)] = given[i]

    for i in range(HMAX):
        pl.when(i < layers)(lambda i=i: put(i))
    last = pltpu.make_async_copy(
        others.at[pl.ds(rim, HMAX)], image.at[pl.ds(there + rim, HMAX)], sems.at[1]
    )
    last.start()
    wait_all([rest, last])


def place_image(offs, others, given, image):
    return pl.pallas_call(
        place_kernel,
        out_shape=(jax.ShapeDtypeStruct(image.shape, F32), pltpu.VMEM(others.shape, F32)),
        in_specs=[SMEM] + [VMEM] * 2 + [HBM],
        out_specs=(HBM, VMEM),
        input_output_aliases={1: 1, 3: 0},
        scratch_shapes=[pltpu.SemaphoreType.DMA((2,))],
        compiler_params=params(8),
        name="place_image",
    )(offs, *pin((others, given), pltpu.VMEM), *pin((image,)))[0]


def body(
    src_hist, rec_p, rec_q, prev_p, prev_q, horiz, vert, ratio, tilt, rec_pos, rec_data, lag_offs
):
    width, rows, depth = rec_p.shape
    fields = (rec_p, rec_q, prev_p, prev_q, horiz, vert, ratio, tilt)

    def swap(v):
        return lax.ppermute(v, "mem", [(0, 1), (1, 0)])

    def after(v, earlier):
        return lax.optimization_barrier((v, earlier))[0]

    def outward(v, step_x, step_y):
        count_x, count_y = lax.axis_size("gx"), lax.axis_size("gy")
        pairs = []
        for x in range(count_x):
            for y in range(count_y):
                for core, sign in ((0, 1), (1, -1)):
                    to_x, to_y = x + sign * step_x, y + sign * step_y
                    if 0 <= to_x < count_x and 0 <= to_y < count_y:
                        pairs.append(((x * count_y + y) * 2 + core, (to_x * count_y + to_y) * 2 + core))
        return lax.ppermute(v, ("gx", "gy", "mem"), pairs)

    plane = rows * lax.axis_size("gy") * depth
    half = width // 2
    x = rec_pos // plane - lax.axis_index("gx") * width - lax.axis_index("mem") * half + DEEP
    rest = rec_pos % plane
    y = rest // depth - lax.axis_index("gy") * rows + ROW0
    z = rest % depth
    inside = (x >= 0) & (x < half + 2 * DEEP)
    inside &= (y >= ROW0 - DEEP) & (y < ROW0 + rows + DEEP)
    target = jnp.where(inside, (x << 16) + (y << 8) + z, -1)
    offs_other = swap(lag_offs)
    target = jnp.concatenate([target, lag_offs[0], offs_other[0]])

    other = swap(src_hist)
    packed = pack_x(fields)
    xw = outward(packed, 1, 0)
    ys, same, cross, xs = pack_rest(fields, src_hist, after(other, packed))
    ys, same, cross = outward(ys, 0, 1), outward(same, 1, 1), outward(cross, 1, -1)
    *bufs, ints = load(fields, after(target, packed))
    xs = outward(after(xs, (same, cross)), 1, 0)
    halos = (xw, ys, swap(ys), same, cross)
    token = swap(xw[0, :16])
    p, q, total, total_other, p_rims = wave(ints, rec_data, halos, src_hist, other, token, bufs)
    parts = (swap(p), swap(q), swap(total_other))
    total, given = rim_image(lag_offs, offs_other, (after(xs, p), same, cross), p_rims, total)
    p, q, image = merge((p, parts[0], q, parts[1], total), given)
    image = place_image(lag_offs, parts[2], swap(given), image)
    return image[None], p, q


def solution(mesh):
    block = P("gx", "gy", None)
    return jax.shard_map(
        body,
        mesh=mesh,
        in_specs=(P("mem", "gx", "gy", None),) + (block,) * 8 + (P(), P(), P("mem", None)),
        out_specs=(P("mem", "gx", "gy", None), block, block),
        check_vma=False,
    )
```
